128 devices in a mesh: seq: 8 (over y, core), rows: 16 (over z, x).
Axes of the slice: x: 4, y: 4, z: 4, core: 2. Of those that a mesh axis runs over, the one named last changes fastest.
Arguments:
- inputs: bfloat16 [64, 1024, 576], P('rows', 'seq'), may hold values from -6 to 6
- doc_lengths: int32 [64, 3], P('rows'), may hold values from 1 to 1022, as said below
- gain_attn: float32 [576], replicated, may hold values from 0.1 to 1.9
- w_query: bfloat16 [576, 576], replicated, may hold values from -0.25 to 0.25
- w_key: bfloat16 [576, 192], replicated, may hold values from -0.25 to 0.25
- w_value: bfloat16 [576, 192], replicated, may hold values from -0.25 to 0.25
- w_output: bfloat16 [576, 576], replicated, may hold values from -3 to 3
- gain_mlp: float32 [576], replicated, may hold values from 0.1 to 1.9
- w_gate: bfloat16 [576, 1536], replicated, may hold values from -0.25 to 0.25
- w_up: bfloat16 [576, 1536], replicated, may hold values from -0.25 to 0.25
- w_down: bfloat16 [1536, 576], replicated, may hold values from -0.15625 to 0.15625
- cotangent: bfloat16 [64, 1024, 576], P('rows', 'seq'), may hold values from -6 to 6
Outputs:
- output: bfloat16 [64, 1024, 576], P('rows', 'seq')
- input_grad: bfloat16 [64, 1024, 576], P('rows', 'seq')
- grad_gain_attn: float32 [576], replicated
- grad_w_query: float32 [576, 576], replicated
- grad_w_key: float32 [576, 192], replicated
- grad_w_value: float32 [576, 192], replicated
- grad_w_output: float32 [576, 576], replicated
- grad_gain_mlp: float32 [576], replicated
- grad_w_gate: float32 [576, 1536], replicated
- grad_w_up: float32 [576, 1536], replicated
- grad_w_down: float32 [1536, 576], replicated
The draws below stay inside these ranges and needn't reach their ends.
Inputs may be any that keep to these rules, and one draw needn't show every extreme that they name: `doc_lengths`: each row's 3 lengths sum to 1024; the first and the last document of every row are shorter than 128 tokens.
All inputs are finite; a program needn't handle non-finite values.
Results may differ from the reference program's by a relative error of at most 0.023.
Values may be sent and summed in bfloat16 or wider, within the bound.
A program may use at most 192 MiB of HBM per device.

```python
import math
import jax
import jax.numpy as jnp
from jax import lax

D = 576
HEADS = 9
KV_HEADS = 3
HEAD = 64
FF = 1536
ROW_LEN = 1024
LOCAL = 128
NROW = 64


def draw_doc_lengths(key, part):
    key = jax.random.fold_in(key, 11)
    lead_key, tail_key, pick_key = jax.random.split(key, 3)
    leading = jax.random.randint(lead_key, (NROW, 1), 1, LOCAL)
    trailing = jax.random.randint(tail_key, (NROW, 1), 1, LOCAL)
    chosen = jax.random.randint(pick_key, (), 0, NROW)
    marked = (jnp.arange(NROW, dtype=jnp.int32) == chosen)[:, None]
    leading = jnp.where(marked, 1, leading)
    trailing = jnp.where(marked, 1, trailing)
    return jnp.concatenate([leading, ROW_LEN - leading - trailing, trailing], axis=1).astype(jnp.int32)


def level_of(stream_key, dims, shards, smallest, high):
    def one(axis_at, blocks):
        draws = jax.random.uniform(jax.random.fold_in(jax.random.fold_in(stream_key, 6), axis_at), (blocks,), jnp.float32, smallest / len(shards), high / len(shards))
        return jnp.repeat(jnp.exp(draws), dims[axis_at] // blocks).reshape((-1,) + (1,) * (len(dims) - axis_at - 1))

    loudness = one(*shards[0])
    for cut in shards[1:]:
        loudness = loudness * one(*cut)
    return loudness


def noise(key, extent, spread, limit, cuts=(), kind=jnp.bfloat16):
    factor_of = level_of(key, extent, cuts, -0.22, 0.18) if cuts else 1.0
    drawn = jax.random.normal(key, extent, jnp.float32) * spread * factor_of
    return jnp.minimum(jnp.maximum(drawn, -limit), limit).astype(kind)


def setup_inputs(seed: int = 0) -> dict:
    key_list = jax.random.split(jax.random.key(seed), 13)
    inputs = noise(key_list[0], (NROW, ROW_LEN, D), 1.0, 6.0, ((0, 16), (1, 8)))
    doc_lengths = draw_doc_lengths(jax.random.fold_in(key_list[12], 71), 0)
    gain_attn = jnp.clip(1.0 + 0.18 * jax.random.normal(key_list[2], (D,), jnp.float32), 0.1, 1.9)
    w_query = noise(key_list[3], (D, D), D ** -0.5, 0.25)
    w_key = noise(key_list[4], (D, KV_HEADS * HEAD), D ** -0.5, 0.25)
    w_value = noise(key_list[5], (D, KV_HEADS * HEAD), D ** -0.5, 0.25)
    w_output = noise(key_list[6], (D, D), (max(1, D * 8 // ROW_LEN)) ** -0.5, 3.0)
    gain_mlp = jnp.clip(1.0 + 0.18 * jax.random.normal(key_list[7], (D,), jnp.float32), 0.1, 1.9)
    w_gate = noise(key_list[8], (D, FF), D ** -0.5, 0.25)
    w_up = noise(key_list[9], (D, FF), D ** -0.5, 0.25)
    w_down = noise(key_list[10], (FF, D), FF ** -0.5, 0.15625)
    cotangent = noise(key_list[11], (NROW, ROW_LEN, D), 1.0, 6.0, ((0, 16), (1, 8)))
    return dict(inputs=inputs, doc_lengths=doc_lengths, gain_attn=gain_attn, w_query=w_query, w_key=w_key, w_value=w_value, w_output=w_output, gain_mlp=gain_mlp, w_gate=w_gate, w_up=w_up, w_down=w_down, cotangent=cotangent)


EPS = 1e-05
THETA = 10000.0
NEG = -1e+30

@jax.custom_vjp
def low(v):
    return lax.optimization_barrier(v.astype(jnp.bfloat16)).astype(jnp.float32)

@jax.custom_vjp
def low_back(v):
    return v

def low_keep(v):
    return (low(v), None)

def low_pass(kept, grad):
    return (grad,)

def back_keep(v):
    return (v, None)

def back_low(kept, grad):
    return (low(grad),)
low.defvjp(low_keep, low_pass)
low_back.defvjp(back_keep, back_low)

def doc_layout(lengths, tokens):
    doc_ends = jnp.cumsum(lengths, axis=1)
    doc_starts = doc_ends - lengths
    segment = lax.optimization_barrier(jnp.sum((tokens[None, :, None] >= doc_ends[:, None, :]).astype(jnp.int32), axis=2))
    in_doc = segment[:, :, None] == jnp.arange(lengths.shape[1], dtype=jnp.int32)[None, None, :]
    doc_first = lax.optimization_barrier(jnp.sum(jnp.where(in_doc, doc_starts[:, None, :], 0), axis=2))
    return (segment, tokens[None, :] - doc_first)

def rope_tables(position):
    half_size = HEAD // 2
    inverse = THETA ** (-2.0 * jnp.arange(half_size, dtype=jnp.float32) / HEAD)
    angles = position.astype(jnp.float32)[..., None] * inverse
    return (jnp.cos(angles), jnp.sin(angles))

def rotate(flat_heads, cosine_table, sine_table, head_count):
    shaped = flat_heads.reshape(flat_heads.shape[:-1] + (head_count, HEAD))
    half_size = HEAD // 2
    former = shaped[..., :half_size]
    latter = shaped[..., half_size:]
    cos_part = cosine_table[..., None, :]
    sin_part = sine_table[..., None, :]
    turned = jnp.concatenate([former * cos_part - latter * sin_part, latter * cos_part + former * sin_part], axis=-1)
    return turned.reshape(flat_heads.shape)

def rms_scale(values, norm_gain):
    return values * lax.rsqrt(lax.optimization_barrier(jnp.mean(values * values, axis=-1, keepdims=True)) + EPS) * norm_gain

def matmul(left_side, right_side):
    return jnp.dot(left_side, right_side, precision=lax.Precision.HIGHEST)

def attention(queries, key_rot, values, segment):
    length = queries.shape[0]
    qblock = min(length, 512)
    group_size = HEADS // KV_HEADS
    factor = 1.0 / math.sqrt(HEAD)
    key_heads = key_rot.reshape(length, KV_HEADS, HEAD)
    value_heads = values.reshape(length, KV_HEADS, HEAD)
    places = jnp.arange(length, dtype=jnp.int32)

    def one_block(blocks):
        query_block, place_block, segment_block = blocks
        head_split = query_block.reshape(qblock, KV_HEADS, group_size, HEAD)
        scores = jnp.einsum('qkgd,skd->kgqs', head_split, key_heads, precision=lax.Precision.HIGHEST)
        scores = low_back(scores * factor)
        visible = (segment[None, :] == segment_block[:, None]) & (places[None, :] <= place_block[:, None])
        scores = jnp.where(visible[None, None], scores, NEG)
        weights = low(jax.nn.softmax(scores, axis=-1))
        blended = jnp.einsum('kgqs,skd->qkgd', weights, value_heads, precision=lax.Precision.HIGHEST)
        return blended.reshape(qblock, HEADS * HEAD)
    pieces = lax.map(jax.checkpoint(one_block), (queries.reshape(length // qblock, qblock, HEADS * HEAD), places.reshape(length // qblock, qblock), segment.reshape(length // qblock, qblock)))
    return pieces.reshape(length, HEADS * HEAD)

def row_forward(block_in, weights_all, segment, cosine_table, sine_table):
    gain_attn, w_query, w_key, w_value, w_output, gain_mlp, w_gate, w_up, w_down = weights_all
    normed = low(rms_scale(block_in, gain_attn))
    q_raw = low_back(matmul(normed, w_query))
    k_raw = low_back(matmul(normed, w_key))
    values = low_back(low(matmul(normed, w_value)))
    queries = low(rotate(q_raw, cosine_table, sine_table, HEADS))
    key_rot = low(rotate(k_raw, cosine_table, sine_table, KV_HEADS))
    attended = attention(queries, key_rot, values, segment)
    mixed_heads = low_back(low(attended))
    after_attn = block_in + low_back(matmul(mixed_heads, w_output))
    normed_m = low(rms_scale(after_attn, gain_mlp))
    gate_pre = low_back(matmul(normed_m, w_gate))
    up_pre = low_back(matmul(normed_m, w_up))
    hidden = low_back(low(jax.nn.silu(gate_pre) * up_pre))
    return after_attn + low_back(matmul(hidden, w_down))

def reference(inputs, doc_lengths, gain_attn, w_query, w_key, w_value, w_output, gain_mlp, w_gate, w_up, w_down, cotangent):
    weights_all = tuple((member.astype(jnp.float32) for member in (gain_attn, w_query, w_key, w_value, w_output, gain_mlp, w_gate, w_up, w_down)))
    length = inputs.shape[1]
    tokens = jnp.arange(length, dtype=jnp.int32)

    def row_step(totals, row_data):
        block_in, lengths, grad_top = row_data
        segment, position = doc_layout(lengths[None, :], tokens)
        segment = segment[0]
        cosine_table, sine_table = rope_tables(position[0])

        def repeated(start_state, weight_set):
            middle = row_forward(start_state, weight_set, segment, cosine_table, sine_table)
            return row_forward(middle, weight_set, segment, cosine_table, sine_table)
        result, pullback = jax.vjp(repeated, block_in.astype(jnp.float32), weights_all)
        grad_in, grad_weights = pullback(grad_top.astype(jnp.float32))
        totals = tuple((term_one + term_two for term_one, term_two in zip(totals, grad_weights)))
        return (totals, (result.astype(jnp.bfloat16), grad_in.astype(jnp.bfloat16)))
    zero_grads = tuple((jnp.zeros(member.shape, jnp.float32) for member in weights_all))
    totals, outputs = lax.scan(row_step, zero_grads, (inputs, doc_lengths, cotangent))
    return (outputs[0], outputs[1], totals[0], totals[1], totals[2], totals[3], totals[4], totals[5], totals[6], totals[7], totals[8])
```

```python
import functools

import jax
import jax.numpy as jnp
from jax import lax
from jax.experimental import pallas as pl
from jax.experimental.pallas import tpu as pltpu
from jax.sharding import PartitionSpec as P

D = 576
HEADS = 9
KV = 3
HEAD = 64
FF = 1536
ROW = 1024
LOC = 128
TOK = 512
CH = 256
EPS = 1e-05
THETA = 10000.0
NEG = -1e30
BF = jnp.bfloat16
F32 = jnp.float32
MESH = pl.DeviceIdType.MESH

NN = ((1,), (0,))
NT = ((1,), (1,))
TN = ((0,), (0,))

B_WD = 0
B_WG = B_WD + 5 * FF
B_WU = B_WG + 12 * D
B_WO = B_WU + 12 * D
EARLY = 24576
B_WQ = EARLY
B_KV = B_WQ + 5 * D
LATE = 6144
TOTAL = EARLY + LATE


def dot(a, b, dims=NN):
    return lax.dot_general(a, b, (dims, ((), ())), preferred_element_type=F32)


def position():
    s = lax.axis_index("seq")
    r = lax.axis_index("rows")
    return s // 2, s % 2, r // 4, r % 4


def device(y, c, z, x):
    return (y * 2 + c, z * 4 + x)


def mul(offset, size):
    return pl.multiple_of(offset, size)


class Reduction:
    def __init__(self, base, part, grads, result, landings, sems):
        self.base, self.part, self.grads, self.result = base, part, grads, result
        self.landings = landings
        self.send, self.recv, self.pair_s, self.pair_r, self.own = sems
        self.y, self.c, self.z, self.x = position()
        y, z, x = self.y, self.z, self.x
        orders = (("x", "y", "z"), ("y", "z", "x"), ("z", "x", "y"))
        where = {"x": x, "y": y, "z": z}
        self.orders = orders
        self.index = [[where[a] for a in order] for order in orders]
        self.sizes = (part, part // 4, part // 16, part // 64)

    def peer(self, axis, index):
        at = {"x": self.x, "y": self.y, "z": self.z}
        at[axis] = index
        return device(at["y"], self.c, at["z"], at["x"])

    def start_of(self, slot, level, core=None):
        core = self.c if core is None else core
        at = self.base + (2 * slot + core) * self.part
        for k in range(level):
            at = at + self.index[slot][k] * self.sizes[k + 1]
        return at

    def rows(self, ref, start, size):
        return ref.at[pl.ds(mul(start, 16), size)]

    def pair_copy(self, slot):
        rows = self.rows(self.grads, self.start_of(slot, 0, 1 - self.c), self.part)
        return pltpu.make_async_remote_copy(
            src_ref=rows,
            dst_ref=self.landings[0].at[slot],
            send_sem=self.pair_s.at[slot],
            recv_sem=self.pair_r.at[slot],
            device_id=device(self.y, 1 - self.c, self.z, self.x),
            device_id_type=MESH,
        )

    def pair_start(self, slots=(0, 1, 2)):
        for slot in slots:
            self.pair_copy(slot).start()

    def pair_finish(self, slots=(0, 1, 2)):
        step = min(256, self.part)
        for slot in slots:
            self.pair_copy(slot).wait()
            at = self.start_of(slot, 0)
            land = self.landings[0]

            def add(k, carry, slot=slot, at=at):
                here = pl.ds(mul(at + k * step, 16), step)
                there = land[slot, pl.ds(mul(k * step, 16), step), :]
                self.grads[here, :] = (self.grads[here, :].astype(F32) + there.astype(F32)).astype(BF)
                return carry

            lax.fori_loop(0, self.part // step, add, 0)

    def scatter_copy(self, slot, level, d):
        axis = self.orders[slot][level]
        index = (self.index[slot][level] + d) % 4
        size = self.sizes[level + 1]
        return pltpu.make_async_remote_copy(
            src_ref=self.rows(self.grads, self.start_of(slot, level) + index * size, size),
            dst_ref=self.landings[level + 1].at[slot, d - 1],
            send_sem=self.send.at[level, slot, d - 1],
            recv_sem=self.recv.at[level, slot, d - 1],
            device_id=self.peer(axis, index),
            device_id_type=MESH,
        )

    def scatter_start(self, level, slots=(0, 1, 2)):
        for slot in slots:
            for d in (2, 1, 3):
                self.scatter_copy(slot, level, d).start()

    def scatter_finish(self, level, slots=(0, 1, 2)):
        size = self.sizes[level + 1]
        step = min(128, size)
        land = self.landings[level + 1]
        for slot in slots:
            for d in (1, 3, 2):
                self.scatter_copy(slot, level, d).wait()
            at = self.start_of(slot, level + 1)

            def add(k, carry, slot=slot, at=at):
                here = pl.ds(mul(at + k * step, 16), step)
                there = pl.ds(mul(k * step, 16), step)
                total = self.grads[here, :].astype(F32)
                for d in range(3):
                    total = total + land[slot, d, there, :].astype(F32)
                self.grads[here, :] = total.astype(BF)
                return carry

            lax.fori_loop(0, size // step, add, 0)

    def own_copy(self, slot):
        at = self.start_of(slot, 3)
        return pltpu.make_async_copy(
            self.rows(self.grads, at, self.sizes[3]),
            self.rows(self.result, at, self.sizes[3]),
            self.own.at[slot],
        )

    def gather_copy(self, slot, level, d):
        axis = self.orders[slot][level]
        index = (self.index[slot][level] + d) % 4
        at = self.start_of(slot, level + 1)
        size = self.sizes[level + 1]
        source = self.grads if level == 2 else self.result
        return pltpu.make_async_remote_copy(
            src_ref=self.rows(source, at, size),
            dst_ref=self.rows(self.result, at, size),
            send_sem=self.send.at[3 + level, slot, d - 1],
            recv_sem=self.recv.at[3 + level, slot, d - 1],
            device_id=self.peer(axis, index),
            device_id_type=MESH,
        )

    def gather_start(self, level, slots=(0, 1, 2)):
        for slot in slots:
            if level == 2:
                self.own_copy(slot).start()
            for d in (2, 1, 3):
                self.gather_copy(slot, level, d).start()

    def arrival(self, slot, level, d):
        index = (self.index[slot][level] - d) % 4
        size = self.sizes[level + 1]
        at = self.start_of(slot, level) + index * size
        copy = pltpu.make_async_remote_copy(
            src_ref=self.rows(self.result, at, size),
            dst_ref=self.rows(self.result, at, size),
            send_sem=self.send.at[3 + level, slot, d - 1],
            recv_sem=self.recv.at[3 + level, slot, d - 1],
            device_id=self.peer(self.orders[slot][level], index),
            device_id_type=MESH,
        )
        return copy, at

    def gather_finish(self, level, slots=(0, 1, 2)):
        for slot in slots:
            if level == 2:
                self.own_copy(slot).wait()
            for d in (1, 3, 2):
                self.gather_copy(slot, level, d).wait_send()
                self.arrival(slot, level, d)[0].wait_recv()

    def share_copy(self, slot, at, k, core=None):
        size = self.sizes[1]
        return pltpu.make_async_remote_copy(
            src_ref=self.rows(self.result, at, size),
            dst_ref=self.rows(self.result, at, size),
            send_sem=self.pair_s.at[3 + slot * 4 + k],
            recv_sem=self.pair_r.at[3 + slot * 4 + k],
            device_id=device(self.y, 1 - self.c, self.z, self.x),
            device_id_type=MESH,
        )

    def share(self, slots=(0, 1, 2)):
        for slot in slots:
            self.share_copy(slot, self.start_of(slot, 1), 0).start()
        for d in (1, 3, 2):
            for slot in slots:
                self.gather_copy(slot, 0, d).wait_send()
                copy, at = self.arrival(slot, 0, d)
                copy.wait_recv()
                self.share_copy(slot, at, d).start()

    def share_finish(self, slots=(0, 1, 2)):
        size = self.sizes[1]
        for slot in slots:
            for k in range(4):
                mine = self.start_of(slot, 0) + ((self.index[slot][0] - k) % 4) * size
                theirs = mine + (1 - 2 * self.c) * self.part
                self.share_copy(slot, mine, k).wait_send()
                self.share_copy(slot, theirs, k).wait_recv()


def step_kernel(
    x_in, cot_in, docs, gain_a, gain_m, wq_h, wk_h, wv_h, wo_h, wg_h, wu_h, wd_h,
    out, in_grad, total,
    wq, wk, wv, wo, wg, wu, wd,
    x_land, c_land, gain_at, gain_mt, cos_t, sin_t, bias_f, bias_d, big,
    state, after, n_a, n_m, mix, qz, kvt, kvn, lse, root_a, root_m, gate, up,
    grad, d_oz, delta, dkv, dqkv, dkv_out, dkv_in, gg_a, gg_m,
    grads, e0, e1, e2, e3, l0, l1, l2, l3,
    w_sem, x_send, x_recv, c_send, c_recv, o_send, o_recv, i_send, i_recv, kv_send, kv_recv, dkv_send, dkv_recv,
    es, er, eps, epr, eo, ls, lr, lps, lpr, lo_s,
):
    y, c, z, x = position()
    me = y * 2 + c
    my_slot = (me + 2) % 4
    to_core = ((me + 2) % 8) // 4
    chunk_a = 3 - 2 * c
    chunk_b = 2 * c

    barrier = pltpu.get_barrier_semaphore()
    for k in range(1, 8):
        pl.semaphore_signal(barrier, inc=1, device_id=((me + k) % 8, z * 4 + x), device_id_type=MESH)
    for k in range(1, 4):
        pl.semaphore_signal(barrier, inc=1, device_id=device(y, c, (z + k) % 4, x), device_id_type=MESH)
        pl.semaphore_signal(barrier, inc=1, device_id=device(y, c, z, (x + k) % 4), device_id_type=MESH)
    weight_pairs = [(wk_h, wk), (wv_h, wv), (wq_h, wq), (wo_h, wo), (wg_h, wg), (wu_h, wu), (wd_h, wd)]
    loads = [pltpu.make_async_copy(a, b, w_sem.at[k]) for k, (a, b) in enumerate(weight_pairs)]
    pl.semaphore_wait(barrier, 13)

    def spread(source, land, send, recv, k):
        r = (y + k) % 4
        target = r * 2 + to_core
        remote = pltpu.make_async_remote_copy(
            src_ref=source.at[r], dst_ref=land.at[my_slot], send_sem=send.at[k], recv_sem=recv.at[my_slot],
            device_id=(target, z * 4 + x), device_id_type=MESH,
        )
        local = pltpu.make_async_copy(source.at[r], land.at[my_slot], send.at[k])
        return target == me, remote, local

    def spread_start(source, land, send, recv):
        for k in (2, 1, 3, 0):
            own, remote, local = spread(source, land, send, recv, k)
            pl.when(own)(local.start)
            pl.when(jnp.logical_not(own))(remote.start)

    def spread_send_wait(source, land, send, recv):
        for k in range(4):
            own, remote, local = spread(source, land, send, recv, k)
            pl.when(own)(local.wait)
            pl.when(jnp.logical_not(own))(remote.wait_send)

    def spread_recv_wait(source, land, send, recv):
        for slot in range(4):
            home = (slot + 6 + 4 * c) % 8
            landed = pltpu.make_async_remote_copy(
                src_ref=source.at[0], dst_ref=land.at[slot], send_sem=send.at[0], recv_sem=recv.at[slot],
                device_id=(home, z * 4 + x), device_id_type=MESH,
            )
            pl.when(home != me)(landed.wait_recv)

    def home_copy(source, result, send, recv, slot):
        home = (slot + 6 + 4 * c) % 8
        remote = pltpu.make_async_remote_copy(
            src_ref=source.at[slot], dst_ref=result.at[y], send_sem=send.at[slot], recv_sem=recv.at[y],
            device_id=(home, z * 4 + x), device_id_type=MESH,
        )
        local = pltpu.make_async_copy(source.at[slot], result.at[y], send.at[slot])
        return home == me, remote, local

    def home_start(source, result, send, recv, slot):
        own, remote, local = home_copy(source, result, send, recv, slot)
        pl.when(own)(local.start)
        pl.when(jnp.logical_not(own))(remote.start)

    def home_wait(source, result, send, recv):
        for slot in range(4):
            own, remote, local = home_copy(source, result, send, recv, slot)
            pl.when(own)(local.wait)
            pl.when(jnp.logical_not(own))(remote.wait_send)
        for r in range(4):
            origin = r * 2 + to_core
            landed = pltpu.make_async_remote_copy(
                src_ref=source.at[0], dst_ref=result.at[r], send_sem=send.at[0], recv_sem=recv.at[r],
                device_id=(origin, z * 4 + x), device_id_type=MESH,
            )
            pl.when(origin != me)(landed.wait_recv)

    spread_start(x_in, x_land, x_send, x_recv)
    for load in loads:
        load.start()

    end0 = docs[y, 0]
    end1 = end0 + docs[y, 1]
    column = lax.broadcasted_iota(jnp.int32, (1, TOK), 1)
    token = jnp.where(column < CH, column + chunk_a * CH, column - CH + chunk_b * CH)
    first = jnp.where(token < end0, 0, jnp.where(token < end1, end0, end1))
    place = (token - first).astype(F32)
    half = lax.broadcasted_iota(jnp.int32, (HEAD // 2, TOK), 0).astype(F32)
    angles = place * jnp.exp(half * (-2.0 / HEAD * 9.210340371976184))
    cos_t[...] = jnp.cos(angles)
    sin_t[...] = jnp.sin(angles)
    for n, chunk in enumerate((chunk_a, chunk_b)):
        cols = slice(n * CH, n * CH + CH)
        fi, tk = first[:, cols], token[:, cols]
        key = lax.broadcasted_iota(jnp.int32, (LOC, CH), 0)
        bias_f[n] = jnp.where(key >= fi, 0.0, NEG).astype(F32)
        key = lax.broadcasted_iota(jnp.int32, (CH, CH), 0) + chunk * CH
        bias_d[n] = jnp.where((key >= fi) & (key <= tk), 0.0, NEG).astype(F32)
        big[n] = jnp.broadcast_to(jnp.where(fi > LOC, -NEG, 0.0).astype(F32), (8, CH))
    gain_at[...] = jnp.broadcast_to(gain_a[...], (128, D)).T
    gain_mt[...] = jnp.broadcast_to(gain_m[...], (128, D)).T
    gg_a[...] = jnp.zeros(gg_a.shape, F32)
    gg_m[...] = jnp.zeros(gg_m.shape, F32)
    for app in range(2):
        qz[app, :, HEAD:, :] = jnp.zeros((KV, HEAD, 6 * CH), BF)
        kvt[app, :, 2 * HEAD :, :] = jnp.ones((KV, 16, ROW), BF)
    d_oz[:, :HEAD, :] = jnp.zeros((KV, HEAD, 6 * CH), BF)
    grads[pl.ds(B_WD + 4 * FF, FF), :] = jnp.zeros((FF, 128), BF)
    grads[pl.ds(B_WO + 4 * D, D), :] = jnp.zeros((D, 128), BF)
    grads[pl.ds(B_WO + 5 * D, EARLY - B_WO - 5 * D), :] = jnp.zeros((EARLY - B_WO - 5 * D, 128), BF)
    grads[pl.ds(B_KV + 3 * D, TOTAL - B_KV - 3 * D), :] = jnp.zeros((TOTAL - B_KV - 3 * D, 128), BF)

    def wide(gain):
        return jnp.concatenate([gain[...]] * 4, axis=1)

    def norm(values, gain, roots, app):
        root = lax.rsqrt(jnp.mean(values * values, axis=0, keepdims=True) + EPS)
        roots[app] = jnp.broadcast_to(root, (8, TOK))
        return (values * root * wide(gain)).astype(BF)

    def turn(a, b, sign):
        cs, sn = cos_t[...], sin_t[...]
        if sign > 0:
            return a * cs - b * sn, b * cs + a * sn
        return a * cs + b * sn, b * cs - a * sn

    def kv_copy(app, n):
        chunk = chunk_a if n == 0 else chunk_b
        span = kvt.at[app, :, pl.ds(0, 2 * HEAD), pl.ds(mul(chunk * CH, CH), CH)]
        return pltpu.make_async_remote_copy(
            src_ref=span, dst_ref=span, send_sem=kv_send.at[app, n], recv_sem=kv_recv.at[app, n],
            device_id=device(y, 1 - c, z, x), device_id_type=MESH,
        )

    def kv_arrival(app, n):
        chunk = 3 - 2 * (1 - c) if n == 0 else 2 * (1 - c)
        span = kvt.at[app, :, pl.ds(0, 2 * HEAD), pl.ds(mul(chunk * CH, CH), CH)]
        return pltpu.make_async_remote_copy(
            src_ref=span, dst_ref=span, send_sem=kv_send.at[app, n], recv_sem=kv_recv.at[app, n],
            device_id=device(y, 1 - c, z, x), device_id_type=MESH,
        )

    plans = (((0, 3), (1, 0)), ((0, 1), (1, 2)))

    def softmax(s, n, chunk):
        nk = (chunk + 1) * CH
        tail = s[nk - CH :] + bias_d[n]
        top = jnp.max(tail, axis=0, keepdims=True)
        if chunk == 0:
            return top, jnp.exp(tail - top).astype(BF)
        lead = s[:LOC] + bias_f[n]
        shut = big[n][0:1]
        middle = s[LOC : nk - CH]
        top = jnp.maximum(top, jnp.max(lead, axis=0, keepdims=True))
        top = jnp.maximum(top, jnp.max(middle, axis=0, keepdims=True) - shut)
        low = [jnp.exp(lead - top), jnp.exp(middle - (top + shut)), jnp.exp(tail - top)]
        return top, jnp.concatenate([v.astype(BF) for v in low], axis=0)

    def attend(app, plan):
        def group(g, carry):
            scores = []
            for n, chunk in plan:
                nk = (chunk + 1) * CH
                scores.append(dot(kvn[app, g, :nk, :], qz[app, g, :, n * 768 : n * 768 + 768]))
            for (n, chunk), s in zip(plan, scores):
                nk = (chunk + 1) * CH
                for j in range(3):
                    top, low = softmax(s[:, j * CH : j * CH + CH], n, chunk)
                    mixed = dot(kvt[app, g, HEAD:, :nk], low)
                    total_w = mixed[HEAD : HEAD + 1]
                    rows = pl.ds(mul(g * 192 + j * HEAD, HEAD), HEAD)
                    mix[app, rows, n * CH : n * CH + CH] = (mixed[:HEAD] * (1.0 / total_w)).astype(BF)
                    at = n * 768 + j * CH
                    lse[app, g, :, at : at + CH] = jnp.broadcast_to(top + jnp.log(total_w), (8, CH))
            return carry

        lax.fori_loop(0, KV, group, 0)

    def forward(app):
        values = state[app]
        low = norm(values, gain_at, root_a, app)
        n_a[app] = low
        if app == 0:
            loads[0].wait()
            loads[1].wait()
        key_raw = dot(wk[...], low, TN)
        value_raw = dot(wv[...], low, TN)
        for g in range(KV):
            a, b = turn(key_raw[g * 64 : g * 64 + 32], key_raw[g * 64 + 32 : g * 64 + 64], 1)
            packed = jnp.concatenate([a, b, value_raw[g * 64 : g * 64 + 64]], axis=0).astype(BF)
            for n, chunk in enumerate((chunk_a, chunk_b)):
                part = packed[:, n * CH : n * CH + CH]
                kvt[app, g, : 2 * HEAD, pl.ds(mul(chunk * CH, CH), CH)] = part
                kvn[app, g, pl.ds(mul(chunk * CH, CH), CH), :] = part.T
        kv_copy(app, 0).start()
        kv_copy(app, 1).start()
        if app == 0:
            loads[2].wait()
        query_raw = dot(wq[...], low, TN)
        for h in range(HEADS):
            g, j = h // 3, h % 3
            a, b = turn(query_raw[h * 64 : h * 64 + 32], query_raw[h * 64 + 32 : h * 64 + 64], 1)
            both = (jnp.concatenate([a, b], axis=0) * 0.125).astype(BF)
            for n in range(2):
                at = n * 768 + j * CH
                qz[app, g, :HEAD, at : at + CH] = both[:, n * CH : n * CH + CH]
        for n in range(2):
            kv_copy(app, n).wait_send()
            kv_arrival(app, n).wait_recv()
            chunk = 3 - 2 * (1 - c) if n == 0 else 2 * (1 - c)
            for g in range(KV):
                part = kvt[app, g, : 2 * HEAD, pl.ds(mul(chunk * CH, CH), CH)]
                kvn[app, g, pl.ds(mul(chunk * CH, CH), CH), :] = part.T
        pl.when(c == 0)(lambda: attend(app, plans[0]))
        pl.when(c == 1)(lambda: attend(app, plans[1]))
        if app == 0:
            loads[3].wait()
        att = state[app] + dot(wo[...], mix[app], TN)
        after[app] = att
        low = norm(att, gain_mt, root_m, app)
        n_m[app] = low
        if app == 0:
            loads[4].wait()
            loads[5].wait()
            loads[6].wait()
        result = att
        for k in range(3):
            span = slice(k * 512, k * 512 + 512)
            pre = dot(wg[:, span], low, TN)
            pre_up = dot(wu[:, span], low, TN)
            gate[app, span, :] = pre.astype(BF)
            up[app, span, :] = pre_up.astype(BF)
            hidden = (pre * (1.0 / (1.0 + jnp.exp(-pre))) * pre_up).astype(BF)
            result = result + dot(wd[span, :], hidden, TN)
        return result

    def put(base, height, row, value, app):
        width = value.shape[1]
        rows = value.shape[0]
        for j in range((width + 127) // 128):
            lanes = min(128, width - j * 128)
            here = pl.ds(base + j * height + row, rows)
            part = value[:, j * 128 : j * 128 + lanes]
            if app == 0:
                part = part + grads[here, :lanes].astype(F32)
            grads[here, :lanes] = part.astype(BF)

    def fold(value):
        return value[:, :128] + value[:, 128:256] + value[:, 256:384] + value[:, 384:]

    def norm_back(d_normed, values, root, gain, sums):
        scaled = d_normed * wide(gain)
        sums[...] += fold(d_normed * (values * root))
        mean = jnp.mean(scaled * values, axis=0, keepdims=True)
        return root * scaled - values * (root * root * root * mean)

    early = Reduction(0, EARLY // 6, grads, total, (e0, e1, e2, e3), (es, er, eps, epr, eo))
    late = Reduction(EARLY, LATE // 6, grads, total, (l0, l1, l2, l3), (ls, lr, lps, lpr, lo_s))

    def mlp_back(app):
        g_low = grad[...].astype(BF)
        d_normed = None
        for k in range(3):
            span = slice(k * 512, k * 512 + 512)
            d_hidden = dot(wd[span, :], g_low).astype(BF).astype(F32)
            pre = gate[app, span, :].astype(F32)
            pre_up = up[app, span, :].astype(F32)
            s = 1.0 / (1.0 + jnp.exp(-pre))
            act = pre * s
            hidden = (act * pre_up).astype(BF)
            put(B_WD, FF, k * 512, dot(hidden, g_low, NT), app)
            d_gate = (d_hidden * pre_up * (s + act * (1.0 - s))).astype(BF)
            d_up = (d_hidden * act).astype(BF)
            put(B_WG + k * 4 * D, D, 0, dot(n_m[app], d_gate, NT), app)
            put(B_WU + k * 4 * D, D, 0, dot(n_m[app], d_up, NT), app)
            term = dot(wg[:, span], d_gate) + dot(wu[:, span], d_up)
            d_normed = term if d_normed is None else d_normed + term
        grad[...] += norm_back(d_normed, after[app], root_m[app][0:1], gain_mt, gg_m)

    def attend_back(app, plan, between):
        dkv[...] = jnp.zeros(dkv.shape, F32)

        def group(g, carry):
            for n, chunk in plan:
                nk = (chunk + 1) * CH
                cols = slice(n * 768, n * 768 + 768)
                s = dot(kvn[app, g, :nk, :], qz[app, g, :, cols])
                d_probs = dot(kvn[app, g, :nk, :], d_oz[g, :, cols])
                lows, d_scores = [], []
                for j in range(3):
                    at = slice(n * 768 + j * CH, n * 768 + j * CH + CH)
                    sj = s[:, j * CH : j * CH + CH]
                    norm_j = lse[app, g, 0:1, at]
                    pieces = [jnp.exp(sj[nk - CH :] + bias_d[n] - norm_j)]
                    if chunk > 0:
                        pieces = [
                            jnp.exp(sj[:LOC] + bias_f[n] - norm_j),
                            jnp.exp(sj[LOC : nk - CH] - (norm_j + big[n][0:1])),
                        ] + pieces
                    probs = jnp.concatenate(pieces, axis=0)
                    diff = d_probs[:, j * CH : j * CH + CH] - delta[g, 0:1, at]
                    lows.append(probs.astype(BF))
                    d_scores.append((probs * diff).astype(BF))
                low = jnp.concatenate(lows, axis=1)
                d_score = jnp.concatenate(d_scores, axis=1)
                d_query = dot(kvt[app, g, :HEAD, :nk], d_score) * 0.125
                for j in range(3):
                    rows = pl.ds(mul(g * 192 + j * HEAD, HEAD), HEAD)
                    at = slice(n * CH, n * CH + CH)
                    a, b = d_query[:32, j * CH : j * CH + CH], d_query[32:, j * CH : j * CH + CH]
                    cs, sn = cos_t[:, at], sin_t[:, at]
                    both = jnp.concatenate([a * cs + b * sn, b * cs - a * sn], axis=0)
                    dqkv[rows, at] = both.astype(BF)
                dkv[g, :nk, :] += dot(d_score, qz[app, g, :, cols], NT) + dot(low, d_oz[g, :, cols], NT)
            between(g)
            return carry

        lax.fori_loop(0, KV, group, 0)

    def dkv_copy(app):
        return pltpu.make_async_remote_copy(
            src_ref=dkv_out, dst_ref=dkv_in.at[app], send_sem=dkv_send.at[app], recv_sem=dkv_recv.at[app],
            device_id=device(y, 1 - c, z, x), device_id_type=MESH,
        )

    def attn_back(app, before, between, after_query):
        g_low = grad[...].astype(BF)
        put(B_WO, D, 0, dot(mix[app], g_low, NT), app)
        before()
        d_mixed = dot(wo[...], g_low)
        for h in range(HEADS):
            g, j = h // 3, h % 3
            dm = d_mixed[h * 64 : h * 64 + 64].astype(BF)
            dl = jnp.sum(dm.astype(F32) * mix[app, h * 64 : h * 64 + 64, :].astype(F32), axis=0, keepdims=True)
            for n in range(2):
                at = n * 768 + j * CH
                d_oz[g, HEAD:, at : at + CH] = dm[:, n * CH : n * CH + CH]
                delta[g, :, at : at + CH] = jnp.broadcast_to(dl[:, n * CH : n * CH + CH], (8, CH))
        pl.when(c == 0)(lambda: attend_back(app, plans[0], between))
        pl.when(c == 1)(lambda: attend_back(app, plans[1], between))
        if app == 0:
            dkv_copy(1).wait_send()
        for n in range(2):
            chunk = 3 - 2 * (1 - c) if n == 0 else 2 * (1 - c)
            dkv_out[:, n * CH : n * CH + CH, :] = dkv[:, pl.ds(mul(chunk * CH, CH), CH), :].astype(BF)
        dkv_copy(app).start()
        dq = dqkv[:D, :]
        low = n_a[app]
        put(B_WQ, D, 0, dot(low, dq, NT), app)
        d_normed = dot(wq[...], dq)
        after_query()
        dkv_copy(app).wait_recv()
        for g in range(KV):
            parts = []
            for n, chunk in enumerate((chunk_a, chunk_b)):
                own = dkv[g, pl.ds(mul(chunk * CH, CH), CH), :]
                other = dkv_in[app, g, n * CH : n * CH + CH, :].astype(F32)
                parts.append((own + other).T)
            both = jnp.concatenate(parts, axis=1)
            a, b = turn(both[:32], both[32:64], -1)
            dqkv[D + g * 64 : D + g * 64 + 64, :] = jnp.concatenate([a, b], axis=0).astype(BF)
            dqkv[D + 192 + g * 64 : D + 192 + g * 64 + 64, :] = both[64:].astype(BF)
        dk = dqkv[D : D + 192, :]
        dv = dqkv[D + 192 :, :]
        put(B_KV, D, 0, dot(low, dqkv[D:, :], NT), app)
        d_normed = d_normed + dot(wk[...], dk) + dot(wv[...], dv)
        grad[...] += norm_back(d_normed, state[app], root_a[app][0:1], gain_at, gg_a)

    def nothing(*unused):
        return None

    spread_send_wait(x_in, x_land, x_send, x_recv)
    spread_recv_wait(x_in, x_land, x_send, x_recv)
    spread_start(cot_in, c_land, c_send, c_recv)
    for slot in range(4):
        state[0, :, slot * LOC : slot * LOC + LOC] = x_land[slot].astype(F32).T
    state[1] = forward(0)
    final = forward(1)
    for slot in range(4):
        x_land[slot] = final[:, slot * LOC : slot * LOC + LOC].T.astype(BF)
    for slot in range(4):
        home_start(x_land, out, o_send, o_recv, slot)
    spread_send_wait(cot_in, c_land, c_send, c_recv)
    spread_recv_wait(cot_in, c_land, c_send, c_recv)
    for slot in range(4):
        grad[:, slot * LOC : slot * LOC + LOC] = c_land[slot].astype(F32).T

    mlp_back(1)
    attn_back(1, nothing, nothing, nothing)
    mlp_back(0)

    def between(g):
        @pl.when(g == 0)
        def _():
            early.pair_finish()
            early.scatter_start(0)

    def after_query():
        early.scatter_finish(0)
        early.scatter_start(1)

    attn_back(0, early.pair_start, between, after_query)
    lane = lax.broadcasted_iota(jnp.int32, (D, 64), 1)
    sum_a = jnp.sum(gg_a[...], axis=1, keepdims=True)
    sum_m = jnp.sum(gg_m[...], axis=1, keepdims=True)
    columns = jnp.where(lane == 0, sum_a, jnp.where(lane == 1, sum_m, 0.0))
    grads[pl.ds(B_WQ + 4 * D, D), 64:] = columns.astype(BF)
    late.pair_start()
    early.scatter_finish(1)
    early.scatter_start(2)
    for slot in range(4):
        c_land[slot] = grad[:, slot * LOC : slot * LOC + LOC].T.astype(BF)
    late.pair_finish()
    late.scatter_start(0)
    early.scatter_finish(2)
    early.gather_start(2)
    late.scatter_finish(0)
    late.scatter_start(1)
    early.gather_finish(2)
    early.gather_start(1)
    late.scatter_finish(1)
    late.scatter_start(2)
    early.gather_finish(1)
    early.gather_start(0)
    for slot in range(4):
        home_start(c_land, in_grad, i_send, i_recv, slot)
    late.scatter_finish(2)
    late.gather_start(2)
    late.gather_finish(2)
    late.gather_start(1)
    late.gather_finish(1)
    late.gather_start(0)
    early.share()
    late.share()
    early.share_finish()
    late.share_finish()
    dkv_copy(0).wait_send()
    home_wait(x_land, out, o_send, o_recv)
    home_wait(c_land, in_grad, i_send, i_recv)


def train_step(inputs, docs, gain_a, wq, wk, wv, wo, gain_m, wg, wu, wd, cot):
    hbm = pl.BlockSpec(memory_space=pl.ANY)
    vmem = pl.BlockSpec(memory_space=pltpu.VMEM)
    smem = pl.BlockSpec(memory_space=pltpu.SMEM)
    dma = pltpu.SemaphoreType.DMA
    v = pltpu.VMEM
    scratch = [
        v((D, D), BF), v((D, 192), BF), v((D, 192), BF), v((D, D), BF), v((D, FF), BF), v((D, FF), BF), v((FF, D), BF),
        v((4, LOC, D), BF), v((4, LOC, D), BF), v((D, 128), F32), v((D, 128), F32),
        v((32, TOK), F32), v((32, TOK), F32), v((2, LOC, CH), F32), v((2, CH, CH), F32), v((2, 8, CH), F32),
        v((2, D, TOK), F32), v((2, D, TOK), F32), v((2, D, TOK), BF), v((2, D, TOK), BF), v((2, D, TOK), BF),
        v((2, KV, 128, 6 * CH), BF), v((2, KV, 144, ROW), BF), v((2, KV, ROW, 128), BF), v((2, KV, 8, 6 * CH), F32),
        v((2, 8, TOK), F32), v((2, 8, TOK), F32), v((2, FF, TOK), BF), v((2, FF, TOK), BF),
        v((D, TOK), F32), v((KV, 128, 6 * CH), BF), v((KV, 8, 6 * CH), F32), v((KV, ROW, 128), F32),
        v((960, TOK), BF), v((KV, TOK, 128), BF), v((2, KV, TOK, 128), BF), v((D, 128), F32), v((D, 128), F32),
        v((TOTAL, 128), BF),
    ]
    for span in (EARLY, LATE):
        part = span // 6
        scratch += [v((3, part, 128), BF)]
        scratch += [v((3, 3, part // 4**k, 128), BF) for k in (1, 2, 3)]
    scratch += [dma((7,))] + [dma((4,))] * 8 + [dma((2, 2))] * 2 + [dma((2,))] * 2
    scratch += [dma((6, 3, 3)), dma((6, 3, 3)), dma((15,)), dma((15,)), dma((3,))] * 2
    out, in_grad, total = pl.pallas_call(
        step_kernel,
        out_shape=(
            jax.ShapeDtypeStruct((4, LOC, D), BF),
            jax.ShapeDtypeStruct((4, LOC, D), BF),
            jax.ShapeDtypeStruct((TOTAL, 128), BF),
        ),
        in_specs=[hbm, hbm, smem, vmem, vmem] + [hbm] * 7,
        out_specs=(hbm, hbm, hbm),
        scratch_shapes=scratch,
        compiler_params=pltpu.CompilerParams(
            collective_id=0, has_side_effects=True, vmem_limit_bytes=63 * 2**20
        ),
        name="train_step",
    )(inputs, cot, docs, gain_a.reshape(1, D), gain_m.reshape(1, D), wq, wk, wv, wo, wg, wu, wd)
    return out, in_grad, total


def unpack_kernel(total, ga, gq, gk, gv, go, gm, gg, gu, gd, land, sq, sk, sv, so, sg, su, sd, in_sem, out_sem):
    spans = ((B_WD, 5 * FF), (B_WG, 12 * D), (B_WU, 12 * D), (B_WO, 5 * D), (B_WQ, 5 * D), (B_KV, 3 * D))
    loads = []
    for k, (base, rows) in enumerate(spans):
        loads.append(pltpu.make_async_copy(total.at[pl.ds(base, rows)], land.at[pl.ds(base, rows)], in_sem.at[k]))
        loads[-1].start()
    stores = []

    def store(source, target):
        stores.append(pltpu.make_async_copy(source, target, out_sem.at[len(stores)]))
        stores[-1].start()

    def panels(base, height, width, target):
        for j in range((width + 127) // 128):
            lanes = min(128, width - j * 128)
            target[:, j * 128 : j * 128 + lanes] = land[pl.ds(base + j * height, height), :lanes].astype(F32)

    for k, (base, height, width, source, target) in enumerate(
        ((B_WD, FF, D, sd, gd), (B_WG, D, FF, sg, gg), (B_WU, D, FF, su, gu), (B_WO, D, D, so, go), (B_WQ, D, D, sq, gq))
    ):
        loads[k].wait()
        panels(base, height, width, source)
        store(source, target)
    loads[5].wait()
    for j in range(2):
        lanes = 128 if j == 0 else 64
        sk[:, j * 128 : j * 128 + lanes] = land[pl.ds(B_KV + j * D, D), :lanes].astype(F32)
    sv[:, :64] = land[pl.ds(B_KV + D, D), 64:].astype(F32)
    sv[:, 64:] = land[pl.ds(B_KV + 2 * D, D), :].astype(F32)
    store(sk, gk)
    store(sv, gv)
    gains = land[pl.ds(B_WQ + 4 * D, D), :].astype(F32).T
    ga[...] = gains[64:65]
    gm[...] = gains[65:66]
    for copy in stores:
        copy.wait()


def unpack(total):
    hbm = pl.BlockSpec(memory_space=pl.ANY)
    vmem = pl.BlockSpec(memory_space=pltpu.VMEM)
    shape = jax.ShapeDtypeStruct
    v = pltpu.VMEM
    result = pl.pallas_call(
        unpack_kernel,
        out_shape=(
            shape((1, D), F32), shape((D, D), F32), shape((D, 192), F32), shape((D, 192), F32), shape((D, D), F32),
            shape((1, D), F32), shape((D, FF), F32), shape((D, FF), F32), shape((FF, D), F32),
        ),
        in_specs=[hbm],
        out_specs=(vmem, hbm, hbm, hbm, hbm, vmem, hbm, hbm, hbm),
        scratch_shapes=[
            v((TOTAL, 128), BF), v((D, D), F32), v((D, 192), F32), v((D, 192), F32), v((D, D), F32),
            v((D, FF), F32), v((D, FF), F32), v((FF, D), F32),
            pltpu.SemaphoreType.DMA((6,)), pltpu.SemaphoreType.DMA((7,)),
        ],
        compiler_params=pltpu.CompilerParams(vmem_limit_bytes=40 * 2**20),
        name="unpack",
    )(total)
    return result


def on_device(inputs, docs, gain_a, wq, wk, wv, wo, gain_m, wg, wu, wd, cot):
    out, in_grad, total = train_step(inputs, docs, gain_a, wq, wk, wv, wo, gain_m, wg, wu, wd, cot)
    ga, gq, gk, gv, go, gm, gg, gu, gd = unpack(total)
    return out, in_grad, ga.reshape(D), gq, gk, gv, go, gm.reshape(D), gg, gu, gd


def solution(mesh):
    token = P("rows", "seq", None)
    in_specs = (token, P("rows", None)) + (P(),) * 9 + (token,)
    out_specs = (token, token) + (P(),) * 9
    return jax.shard_map(on_device, mesh=mesh, in_specs=in_specs, out_specs=out_specs, check_vma=False)
```

```python
import functools

import jax
import jax.numpy as jnp
from jax import lax
from jax.experimental import pallas as pl
from jax.experimental.pallas import tpu as pltpu
from jax.sharding import PartitionSpec as P

D = 576
HEADS = 9
KV = 3
HEAD = 64
FF = 1536
ROW = 1024
LOC = 128
TOK = 512
CH = 256
EPS = 1e-05
THETA = 10000.0
NEG = -1e30
BF = jnp.bfloat16
F32 = jnp.float32
MESH = pl.DeviceIdType.MESH

NN = ((1,), (0,))
NT = ((1,), (1,))
TN = ((0,), (0,))

TILE = 12 * D
B_WD, B_WG, B_WU = 0, 4 * D, 8 * D
B_WO = 3 * TILE
EARLY = 24576
B_WQ = EARLY
B_KV = B_WQ + 5 * D
KV_ROWS = 2 * KV * HEAD
LATE = 5120
TOTAL = EARLY + LATE
ORDERS = (("x", "y", "z"), ("y", "z", "x"), ("z", "x", "y"))
LATE_ORDERS = (("x", "y", "z"), ("z", "y", "x"))


def dot(a, b, dims=NN):
    return lax.dot_general(a, b, (dims, ((), ())), preferred_element_type=F32)


def position():
    s = lax.axis_index("seq")
    r = lax.axis_index("rows")
    return s // 2, s % 2, r // 4, r % 4


def device(y, c, z, x):
    return (y * 2 + c, z * 4 + x)


def mul(offset, size):
    return pl.multiple_of(offset, size)


class Reduction:
    def __init__(self, base, part, orders, grads, result, landings, sems):
        self.base, self.part, self.grads, self.result = base, part, grads, result
        self.slots = range(len(orders))
        self.landings = landings
        self.send, self.recv, self.pair_s, self.pair_r, self.own = sems
        self.y, self.c, self.z, self.x = position()
        y, z, x = self.y, self.z, self.x
        where = {"x": x, "y": y, "z": z}
        self.orders = orders
        self.index = [[where[a] for a in order] for order in orders]
        self.sizes = (part, part // 4, part // 16)

    def peer(self, axis, index):
        at = {"x": self.x, "y": self.y, "z": self.z}
        at[axis] = index
        return device(at["y"], self.c, at["z"], at["x"])

    def start_of(self, slot, level, core=None):
        core = self.c if core is None else core
        at = self.base + (2 * slot + core) * self.part
        for k in range(level):
            at = at + self.index[slot][k] * self.sizes[k + 1]
        return at

    def rows(self, ref, start, size):
        return ref.at[pl.ds(mul(start, 16), size)]

    def remote(self, source, target, send, recv, slot, axis, index):
        if axis == "core":
            where = device(self.y, 1 - self.c, self.z, self.x)
        else:
            where = self.peer(axis, index)
        return pltpu.make_async_remote_copy(
            src_ref=source, dst_ref=target, send_sem=send, recv_sem=recv, device_id=where, device_id_type=MESH
        )

    def pair_copy(self, slot):
        rows = self.rows(self.grads, self.start_of(slot, 0, 1 - self.c), self.part)
        return self.remote(rows, self.landings[0].at[slot], self.pair_s.at[slot], self.pair_r.at[slot], slot, "core", 0)

    def pair_start(self):
        for slot in self.slots:
            self.pair_copy(slot).start()

    def pair_finish(self):
        step = min(256, self.part)
        land = self.landings[0]
        for slot in self.slots:
            self.pair_copy(slot).wait()
            at = self.start_of(slot, 0)

            def add(k, carry, slot=slot, at=at):
                here = pl.ds(mul(at + k * step, 16), step)
                there = land[slot, pl.ds(mul(k * step, 16), step), :]
                self.grads[here, :] = (self.grads[here, :].astype(F32) + there.astype(F32)).astype(BF)
                return carry

            lax.fori_loop(0, self.part // step, add, 0)

    def scatter_copy(self, slot, level, d):
        index = (self.index[slot][level] + d) % 4
        size = self.sizes[level + 1]
        return self.remote(
            self.rows(self.grads, self.start_of(slot, level) + index * size, size),
            self.landings[level + 1].at[slot, d - 1],
            self.send.at[level, slot, d - 1],
            self.recv.at[level, slot, d - 1],
            slot, self.orders[slot][level], index,
        )

    def scatter_start(self, level):
        for d in (2, 1, 3):
            for slot in self.slots:
                self.scatter_copy(slot, level, d).start()

    def scatter_finish(self, level):
        size = self.sizes[level + 1]
        step = next(k for k in (128, 160, size) if size % k == 0)
        land = self.landings[level + 1]
        for slot in self.slots:
            for d in (1, 3, 2):
                self.scatter_copy(slot, level, d).wait()
            at = self.start_of(slot, level + 1)

            def add(k, carry, slot=slot, at=at):
                here = pl.ds(mul(at + k * step, 16), step)
                there = pl.ds(mul(k * step, 16), step)
                total = self.grads[here, :].astype(F32)
                for d in range(3):
                    total = total + land[slot, d, there, :].astype(F32)
                self.grads[here, :] = total.astype(BF)
                return carry

            lax.fori_loop(0, size // step, add, 0)

    def swap_copy(self, slot, d, arriving=False):
        mine = self.index[slot][2]
        index = (mine + d) % 4
        land = self.landings[3]
        at = land.at[slot, (mine - d) % 4 if arriving else mine]
        return self.remote(
            self.rows(self.grads, self.start_of(slot, 2), self.sizes[2]),
            at, self.send.at[2, slot, d - 1], self.recv.at[2, slot, d - 1], slot, self.orders[slot][2], index,
        )

    def swap_start(self):
        for d in (2, 1, 3):
            for slot in self.slots:
                self.swap_copy(slot, d).start()
        for slot in self.slots:
            at = pl.ds(mul(self.start_of(slot, 2), 16), self.sizes[2])
            self.landings[3][slot, self.index[slot][2]] = self.grads[at, :]

    def swap_finish(self):
        land = self.landings[3]
        for slot in self.slots:
            for d in (1, 3, 2):
                self.swap_copy(slot, d).wait_send()
                self.swap_copy(slot, d, True).wait_recv()
            total = land[slot, 0].astype(F32)
            for k in range(1, 4):
                total = total + land[slot, k].astype(F32)
            self.grads[pl.ds(mul(self.start_of(slot, 2), 16), self.sizes[2]), :] = total.astype(BF)

    def own_copy(self, slot):
        at = self.start_of(slot, 2)
        return pltpu.make_async_copy(
            self.rows(self.grads, at, self.sizes[2]), self.rows(self.result, at, self.sizes[2]), self.own.at[slot]
        )

    def gather_copy(self, slot, level, d, arriving=False):
        mine = self.index[slot][level]
        index = (mine + d) % 4
        size = self.sizes[level + 1]
        at = self.start_of(slot, level) + ((mine - d) % 4 if arriving else mine) * size
        source = self.grads if level == 1 and not arriving else self.result
        return self.remote(
            self.rows(source, at, size), self.rows(self.result, at, size),
            self.send.at[3 + level, slot, d - 1], self.recv.at[3 + level, slot, d - 1],
            slot, self.orders[slot][level], index,
        )

    def gather_start(self, level):
        for d in (2, 1, 3):
            for slot in self.slots:
                self.gather_copy(slot, level, d).start()
        if level == 1:
            for slot in self.slots:
                self.own_copy(slot).start()

    def gather_finish(self, level):
        for slot in self.slots:
            if level == 1:
                self.own_copy(slot).wait()
            self.gather_wait(slot, level)

    def gather_wait(self, slot, level):
        for d in (1, 3, 2):
            self.gather_copy(slot, level, d).wait_send()
            self.gather_copy(slot, level, d, True).wait_recv()

    def share_copy(self, slot, core):
        rows = self.rows(self.result, self.start_of(slot, 0, core), self.part)
        return self.remote(rows, rows, self.pair_s.at[len(self.slots) + slot], self.pair_r.at[len(self.slots) + slot], slot, "core", 0)

    def share(self):
        for slot in self.slots:
            self.gather_wait(slot, 0)
            self.share_copy(slot, self.c).start()

    def share_finish(self):
        for slot in self.slots:
            self.share_copy(slot, self.c).wait_send()
            self.share_copy(slot, 1 - self.c).wait_recv()


def step_kernel(
    x_in, cot_in, docs, gain_a, gain_m, wq_h, wk_h, wv_h, wo_h, wg_h, wu_h, wd_h,
    out, in_grad, total,
    wq, wk, wv, wo, wg, wu, wd,
    x_land, c_land, gain_at, gain_mt, cos_t, sin_t, bias_f, bias_d, big,
    state, after, n_a, n_m, mix, qz, kvt, kvn, lse, root_a, root_m, gate, up,
    grad, d_oz, delta, dkv, dqkv, dkv_out, dkv_in, gg_a, gg_m, hid_keep, g_keep, d_keep,
    grads, a0, a1, a2, a3, b0, b1, b2, b3, l0, l1, l2, l3,
    w_sem, x_send, x_recv, c_send, c_recv, o_send, o_recv, i_send, i_recv, kv_send, kv_recv, dkv_send, dkv_recv,
    a_s, a_r, a_ps, a_pr, a_o, b_s, b_r, b_ps, b_pr, b_o, l_s, l_r, l_ps, l_pr, l_o,
):
    y, c, z, x = position()
    me = y * 2 + c
    my_slot = (me + 2) % 4
    to_core = ((me + 2) % 8) // 4
    chunk_a = 3 - 2 * c
    chunk_b = 2 * c

    barrier = pltpu.get_barrier_semaphore()
    for k in range(1, 8):
        pl.semaphore_signal(barrier, inc=1, device_id=((me + k) % 8, z * 4 + x), device_id_type=MESH)
    for k in range(1, 4):
        pl.semaphore_signal(barrier, inc=1, device_id=device(y, c, (z + k) % 4, x), device_id_type=MESH)
        pl.semaphore_signal(barrier, inc=1, device_id=device(y, c, z, (x + k) % 4), device_id_type=MESH)
    weight_pairs = [(wk_h, wk), (wv_h, wv), (wq_h, wq), (wo_h, wo), (wg_h, wg), (wu_h, wu), (wd_h, wd)]
    loads = [pltpu.make_async_copy(a, b, w_sem.at[k]) for k, (a, b) in enumerate(weight_pairs)]
    pl.semaphore_wait(barrier, 13)

    def spread(source, land, send, recv, k):
        r = (y + k) % 4
        target = r * 2 + to_core
        remote = pltpu.make_async_remote_copy(
            src_ref=source.at[r], dst_ref=land.at[my_slot], send_sem=send.at[k], recv_sem=recv.at[my_slot],
            device_id=(target, z * 4 + x), device_id_type=MESH,
        )
        local = pltpu.make_async_copy(source.at[r], land.at[my_slot], send.at[k])
        return target == me, remote, local

    def spread_start(source, land, send, recv):
        for k in (2, 1, 3, 0):
            own, remote, local = spread(source, land, send, recv, k)
            pl.when(own)(local.start)
            pl.when(jnp.logical_not(own))(remote.start)

    def spread_send_wait(source, land, send, recv):
        for k in range(4):
            own, remote, local = spread(source, land, send, recv, k)
            pl.when(own)(local.wait)
            pl.when(jnp.logical_not(own))(remote.wait_send)

    def spread_recv_wait(source, land, send, recv):
        for slot in range(4):
            home = (slot + 6 + 4 * c) % 8
            landed = pltpu.make_async_remote_copy(
                src_ref=source.at[0], dst_ref=land.at[slot], send_sem=send.at[0], recv_sem=recv.at[slot],
                device_id=(home, z * 4 + x), device_id_type=MESH,
            )
            pl.when(home != me)(landed.wait_recv)

    def home_copy(source, result, send, recv, slot):
        home = (slot + 6 + 4 * c) % 8
        remote = pltpu.make_async_remote_copy(
            src_ref=source.at[slot], dst_ref=result.at[y], send_sem=send.at[slot], recv_sem=recv.at[y],
            device_id=(home, z * 4 + x), device_id_type=MESH,
        )
        local = pltpu.make_async_copy(source.at[slot], result.at[y], send.at[slot])
        return home == me, remote, local

    def home_start(source, result, send, recv, slot):
        own, remote, local = home_copy(source, result, send, recv, slot)
        pl.when(own)(local.start)
        pl.when(jnp.logical_not(own))(remote.start)

    def home_wait(source, result, send, recv):
        for slot in range(4):
            own, remote, local = home_copy(source, result, send, recv, slot)
            pl.when(own)(local.wait)
            pl.when(jnp.logical_not(own))(remote.wait_send)
        for r in range(4):
            origin = r * 2 + to_core
            landed = pltpu.make_async_remote_copy(
                src_ref=source.at[0], dst_ref=result.at[r], send_sem=send.at[0], recv_sem=recv.at[r],
                device_id=(origin, z * 4 + x), device_id_type=MESH,
            )
            pl.when(origin != me)(landed.wait_recv)

    spread_start(x_in, x_land, x_send, x_recv)
    for load in loads:
        load.start()

    end0 = docs[y, 0]
    end1 = end0 + docs[y, 1]
    column = lax.broadcasted_iota(jnp.int32, (1, TOK), 1)
    token = jnp.where(column < CH, column + chunk_a * CH, column - CH + chunk_b * CH)
    first = jnp.where(token < end0, 0, jnp.where(token < end1, end0, end1))
    place = (token - first).astype(F32)
    half = lax.broadcasted_iota(jnp.int32, (HEAD // 2, TOK), 0).astype(F32)
    angles = place * jnp.exp(half * (-2.0 / HEAD * 9.210340371976184))
    cos_t[...] = jnp.cos(angles)
    sin_t[...] = jnp.sin(angles)
    for n, chunk in enumerate((chunk_a, chunk_b)):
        cols = slice(n * CH, n * CH + CH)
        fi, tk = first[:, cols], token[:, cols]
        key = lax.broadcasted_iota(jnp.int32, (LOC, CH), 0)
        bias_f[n] = jnp.where(key >= fi, 0.0, NEG).astype(F32)
        key = lax.broadcasted_iota(jnp.int32, (CH, CH), 0) + chunk * CH
        bias_d[n] = jnp.where((key >= fi) & (key <= tk), 0.0, NEG).astype(F32)
        big[n] = jnp.broadcast_to(jnp.where(fi > LOC, -NEG, 0.0).astype(F32), (8, CH))
    gain_at[...] = jnp.broadcast_to(gain_a[...].reshape(1, D), (128, D)).T
    gain_mt[...] = jnp.broadcast_to(gain_m[...].reshape(1, D), (128, D)).T
    gg_a[...] = jnp.zeros(gg_a.shape, F32)
    gg_m[...] = jnp.zeros(gg_m.shape, F32)
    for app in range(2):
        qz[app, :, HEAD:, :] = jnp.zeros((KV, HEAD, 6 * CH), BF)
        kvt[app, :, 2 * HEAD :, :] = jnp.ones((KV, 16, ROW), BF)
    d_oz[:, :HEAD, :] = jnp.zeros((KV, HEAD, 6 * CH), BF)
    grads[pl.ds(B_WO + 4 * D, D), :] = jnp.zeros((D, 128), BF)
    grads[pl.ds(B_WO + 5 * D, EARLY - B_WO - 5 * D), :] = jnp.zeros((EARLY - B_WO - 5 * D, 128), BF)
    grads[pl.ds(B_KV + 4 * KV_ROWS, TOTAL - B_KV - 4 * KV_ROWS), :] = jnp.zeros((TOTAL - B_KV - 4 * KV_ROWS, 128), BF)

    def wide(gain):
        return jnp.concatenate([gain[...]] * 4, axis=1)

    def norm(values, gain, roots, app):
        root = lax.rsqrt(jnp.mean(values * values, axis=0, keepdims=True) + EPS)
        roots[app] = jnp.broadcast_to(root, (8, TOK))
        return (values * root * wide(gain)).astype(BF)

    def turn(a, b, sign):
        cs, sn = cos_t[...], sin_t[...]
        if sign > 0:
            return a * cs - b * sn, b * cs + a * sn
        return a * cs + b * sn, b * cs - a * sn

    def kv_copy(app, n):
        chunk = chunk_a if n == 0 else chunk_b
        span = kvt.at[app, :, pl.ds(0, 2 * HEAD), pl.ds(mul(chunk * CH, CH), CH)]
        return pltpu.make_async_remote_copy(
            src_ref=span, dst_ref=span, send_sem=kv_send.at[app, n], recv_sem=kv_recv.at[app, n],
            device_id=device(y, 1 - c, z, x), device_id_type=MESH,
        )

    def kv_arrival(app, n):
        chunk = 3 - 2 * (1 - c) if n == 0 else 2 * (1 - c)
        span = kvt.at[app, :, pl.ds(0, 2 * HEAD), pl.ds(mul(chunk * CH, CH), CH)]
        return pltpu.make_async_remote_copy(
            src_ref=span, dst_ref=span, send_sem=kv_send.at[app, n], recv_sem=kv_recv.at[app, n],
            device_id=device(y, 1 - c, z, x), device_id_type=MESH,
        )

    plans = (((0, 3), (1, 0)), ((0, 1), (1, 2)))

    def softmax(s, n, chunk):
        nk = (chunk + 1) * CH
        tail = s[nk - CH :] + bias_d[n]
        top = jnp.max(tail, axis=0, keepdims=True)
        if chunk == 0:
            return top, jnp.exp(tail - top).astype(BF)
        lead = s[:LOC] + bias_f[n]
        shut = big[n][0:1]
        middle = s[LOC : nk - CH]
        top = jnp.maximum(top, jnp.max(lead, axis=0, keepdims=True))
        top = jnp.maximum(top, jnp.max(middle, axis=0, keepdims=True) - shut)
        low = [jnp.exp(lead - top), jnp.exp(middle - (top + shut)), jnp.exp(tail - top)]
        return top, jnp.concatenate([v.astype(BF) for v in low], axis=0)

    def attend(app, plan):
        def group(g, carry):
            scores = []
            for n, chunk in plan:
                nk = (chunk + 1) * CH
                scores.append(dot(kvn[app, g, :nk, :], qz[app, g, :, n * 768 : n * 768 + 768]))
            for (n, chunk), s in zip(plan, scores):
                nk = (chunk + 1) * CH
                for j in range(3):
                    top, low = softmax(s[:, j * CH : j * CH + CH], n, chunk)
                    mixed = dot(kvt[app, g, HEAD:, :nk], low)
                    total_w = mixed[HEAD : HEAD + 1]
                    rows = pl.ds(mul(g * 192 + j * HEAD, HEAD), HEAD)
                    mix[app, rows, n * CH : n * CH + CH] = (mixed[:HEAD] * (1.0 / total_w)).astype(BF)
                    at = n * 768 + j * CH
                    lse[app, g, :, at : at + CH] = jnp.broadcast_to(top + jnp.log(total_w), (8, CH))
            return carry

        lax.fori_loop(0, KV, group, 0)

    def forward(app):
        values = state[app]
        low = norm(values, gain_at, root_a, app)
        n_a[app] = low
        if app == 0:
            loads[0].wait()
            loads[1].wait()
        key_raw = dot(wk[...], low)
        value_raw = dot(wv[...], low)
        for g in range(KV):
            a, b = turn(key_raw[g * 64 : g * 64 + 32], key_raw[g * 64 + 32 : g * 64 + 64], 1)
            packed = jnp.concatenate([a, b, value_raw[g * 64 : g * 64 + 64]], axis=0).astype(BF)
            for n, chunk in enumerate((chunk_a, chunk_b)):
                kvt[app, g, : 2 * HEAD, pl.ds(mul(chunk * CH, CH), CH)] = packed[:, n * CH : n * CH + CH]
        kv_copy(app, 0).start()
        kv_copy(app, 1).start()
        for n, chunk in enumerate((chunk_a, chunk_b)):
            for g in range(KV):
                part = kvt[app, g, : 2 * HEAD, pl.ds(mul(chunk * CH, CH), CH)]
                kvn[app, g, pl.ds(mul(chunk * CH, CH), CH), :] = part.T
        if app == 0:
            loads[2].wait()
        query_raw = dot(wq[...], low, TN)
        for h in range(HEADS):
            g, j = h // 3, h % 3
            a, b = turn(query_raw[h * 64 : h * 64 + 32], query_raw[h * 64 + 32 : h * 64 + 64], 1)
            both = (jnp.concatenate([a, b], axis=0) * 0.125).astype(BF)
            for n in range(2):
                at = n * 768 + j * CH
                qz[app, g, :HEAD, at : at + CH] = both[:, n * CH : n * CH + CH]
        for n in range(2):
            kv_copy(app, n).wait_send()
            kv_arrival(app, n).wait_recv()
            chunk = 3 - 2 * (1 - c) if n == 0 else 2 * (1 - c)
            for g in range(KV):
                part = kvt[app, g, : 2 * HEAD, pl.ds(mul(chunk * CH, CH), CH)]
                kvn[app, g, pl.ds(mul(chunk * CH, CH), CH), :] = part.T
        pl.when(c == 0)(lambda: attend(app, plans[0]))
        pl.when(c == 1)(lambda: attend(app, plans[1]))
        if app == 0:
            loads[3].wait()
        att = state[app] + dot(wo[...], mix[app], TN)
        after[app] = att
        low = norm(att, gain_mt, root_m, app)
        n_m[app] = low
        if app == 0:
            loads[4].wait()
            loads[5].wait()
            loads[6].wait()
        result = att
        for k in range(3):
            span = slice(k * 512, k * 512 + 512)
            pre = dot(wg[:, span], low, TN)
            pre_up = dot(wu[:, span], low, TN)
            gate[app, span, :] = pre.astype(BF)
            up[app, span, :] = pre_up.astype(BF)
            hidden = (pre * (1.0 / (1.0 + jnp.exp(-pre))) * pre_up).astype(BF)
            result = result + dot(wd[:, span], hidden)
        return result

    def put(base, height, value, add=False):
        width = value.shape[1]
        for j in range((width + 127) // 128):
            lanes = min(128, width - j * 128)
            here = pl.ds(base + j * height, height)
            part = value[:, j * 128 : j * 128 + lanes]
            if add:
                part = part + grads[here, :lanes].astype(F32)
            grads[here, :lanes] = part.astype(BF)

    def fold(value):
        return value[:, :128] + value[:, 128:256] + value[:, 256:384] + value[:, 384:]

    def norm_back(d_normed, values, root, gain, sums):
        scaled = d_normed * wide(gain)
        sums[...] += fold(d_normed * (values * root))
        mean = jnp.mean(scaled * values, axis=0, keepdims=True)
        return root * scaled - values * (root * root * root * mean)

    one = Reduction(0, EARLY // 12, ORDERS, grads, total, (a0, a1, a2, a3), (a_s, a_r, a_ps, a_pr, a_o))
    two = Reduction(EARLY // 2, EARLY // 12, ORDERS, grads, total, (b0, b1, b2, b3), (b_s, b_r, b_ps, b_pr, b_o))
    late = Reduction(EARLY, LATE // 4, LATE_ORDERS, grads, total, (l0, l1, l2, l3), (l_s, l_r, l_ps, l_pr, l_o))

    def mlp_back(app, after_tile):
        g_low = grad[...].astype(BF)
        if app == 1:
            g_keep[...] = g_low
        d_normed = None
        for k in range(3):
            span = slice(k * 512, k * 512 + 512)
            d_hidden = dot(wd[:, span], g_low, TN).astype(BF).astype(F32)
            pre = gate[app, span, :].astype(F32)
            pre_up = up[app, span, :].astype(F32)
            s = 1.0 / (1.0 + jnp.exp(-pre))
            act = pre * s
            hidden = (act * pre_up).astype(BF)
            d_gate = (d_hidden * pre_up * (s + act * (1.0 - s))).astype(BF)
            d_up = (d_hidden * act).astype(BF)
            if app == 1:
                hid_keep[span, :] = hidden
                gate[1, span, :] = d_gate
                up[1, span, :] = d_up
            else:
                put(k * TILE + B_WD, D, dot(g_low, hidden, NT) + dot(g_keep[...], hid_keep[span, :], NT))
                put(k * TILE + B_WG, D, dot(n_m[0], d_gate, NT) + dot(n_m[1], gate[1, span, :], NT))
                put(k * TILE + B_WU, D, dot(n_m[0], d_up, NT) + dot(n_m[1], up[1, span, :], NT))
            term = dot(wg[:, span], d_gate) + dot(wu[:, span], d_up)
            d_normed = term if d_normed is None else d_normed + term
            after_tile(k)
        grad[...] += norm_back(d_normed, after[app], root_m[app][0:1], gain_mt, gg_m)

    def attend_back(app, plan, between):
        dkv[...] = jnp.zeros(dkv.shape, F32)

        def products(g, n, k):
            cols = slice(n * 768, n * 768 + 768)
            rows = slice(k * CH, k * CH + CH)
            return dot(kvn[app, g, rows, :], qz[app, g, :, cols]), dot(kvn[app, g, rows, :], d_oz[g, :, cols])

        def three(v):
            return jnp.concatenate([v] * 3, axis=1)

        def group(g, carry):
            tiles = [(n, chunk, k) for n, chunk in plan for k in range(chunk + 1)]
            coming = products(g, tiles[0][0], tiles[0][2])
            d_query = None
            for i, (n, chunk, k) in enumerate(tiles):
                s, d_probs = coming
                if i + 1 < len(tiles):
                    coming = products(g, tiles[i + 1][0], tiles[i + 1][2])
                cols = slice(n * 768, n * 768 + 768)
                rows = slice(k * CH, k * CH + CH)
                log_sum = lse[app, g, 0:1, cols]
                if k == chunk:
                    s = s + three(bias_d[n])
                elif k == 0:
                    s = jnp.concatenate([s[:LOC] + three(bias_f[n]), s[LOC:] - three(big[n][0:1])], axis=0)
                else:
                    log_sum = log_sum + three(big[n][0:1])
                probs = jnp.exp(s - log_sum)
                d_score = (probs * (d_probs - delta[g, 0:1, cols])).astype(BF)
                low = probs.astype(BF)
                term = dot(kvt[app, g, :HEAD, rows], d_score)
                d_query = term if k == 0 else d_query + term
                dkv[g, rows, :] += dot(d_score, qz[app, g, :, cols], NT) + dot(low, d_oz[g, :, cols], NT)
                if k < chunk:
                    continue
                d_query = d_query * 0.125
                at = slice(n * CH, n * CH + CH)
                cs, sn = cos_t[:, at], sin_t[:, at]
                for j in range(3):
                    head = pl.ds(mul(g * 192 + j * HEAD, HEAD), HEAD)
                    a, b = d_query[:32, j * CH : j * CH + CH], d_query[32:, j * CH : j * CH + CH]
                    both = jnp.concatenate([a * cs + b * sn, b * cs - a * sn], axis=0)
                    dqkv[app, head, at] = both.astype(BF)
            between(g)
            return carry

        lax.fori_loop(0, KV, group, 0)

    def dkv_copy(app):
        return pltpu.make_async_remote_copy(
            src_ref=dkv_out, dst_ref=dkv_in.at[app], send_sem=dkv_send.at[app], recv_sem=dkv_recv.at[app],
            device_id=device(y, 1 - c, z, x), device_id_type=MESH,
        )

    def attn_back(app, before, before_groups, between, after_query):
        g_low = grad[...].astype(BF)
        if app == 1:
            d_keep[...] = g_low
        else:
            put(B_WO, D, dot(mix[0], g_low, NT) + dot(mix[1], d_keep[...], NT))
        before()
        d_mixed = dot(wo[...], g_low)
        for h in range(HEADS):
            g, j = h // 3, h % 3
            dm = d_mixed[h * 64 : h * 64 + 64].astype(BF)
            dl = jnp.sum(dm.astype(F32) * mix[app, h * 64 : h * 64 + 64, :].astype(F32), axis=0, keepdims=True)
            for n in range(2):
                at = n * 768 + j * CH
                d_oz[g, HEAD:, at : at + CH] = dm[:, n * CH : n * CH + CH]
                delta[g, :, at : at + CH] = jnp.broadcast_to(dl[:, n * CH : n * CH + CH], (8, CH))
        before_groups()
        if app == 0:
            put(B_WQ, D, dot(n_a[1], dqkv[1, :D, :], NT))
            put(B_KV, KV_ROWS, dot(dqkv[1, D:, :], n_a[1], NT))
        pl.when(c == 0)(lambda: attend_back(app, plans[0], between))
        pl.when(c == 1)(lambda: attend_back(app, plans[1], between))
        if app == 0:
            dkv_copy(1).wait_send()
        for n in range(2):
            chunk = 3 - 2 * (1 - c) if n == 0 else 2 * (1 - c)
            dkv_out[:, n * CH : n * CH + CH, :] = dkv[:, pl.ds(mul(chunk * CH, CH), CH), :].astype(BF)
        dkv_copy(app).start()
        dq = dqkv[app, :D, :]
        low = n_a[app]
        if app == 0:
            put(B_WQ, D, dot(low, dq, NT), True)
        d_normed = dot(wq[...], dq)
        after_query()
        dkv_copy(app).wait_recv()
        for g in range(KV):
            parts = []
            for n, chunk in enumerate((chunk_a, chunk_b)):
                own = dkv[g, pl.ds(mul(chunk * CH, CH), CH), :]
                other = dkv_in[app, g, n * CH : n * CH + CH, :].astype(F32)
                parts.append((own + other).T)
            both = jnp.concatenate(parts, axis=1)
            a, b = turn(both[:32], both[32:64], -1)
            dqkv[app, D + g * 64 : D + g * 64 + 64, :] = jnp.concatenate([a, b], axis=0).astype(BF)
            dqkv[app, D + 192 + g * 64 : D + 192 + g * 64 + 64, :] = both[64:].astype(BF)
        dk = dqkv[app, D : D + 192, :]
        dv = dqkv[app, D + 192 :, :]
        if app == 0:
            put(B_KV, KV_ROWS, dot(dqkv[0, D:, :], low, NT), True)
        d_normed = d_normed + dot(wk[...], dk, TN) + dot(wv[...], dv, TN)
        grad[...] += norm_back(d_normed, state[app], root_a[app][0:1], gain_at, gg_a)

    def nothing(*unused):
        return None

    spread_send_wait(x_in, x_land, x_send, x_recv)
    spread_recv_wait(x_in, x_land, x_send, x_recv)
    spread_start(cot_in, c_land, c_send, c_recv)
    for slot in range(4):
        state[0, :, slot * LOC : slot * LOC + LOC] = x_land[slot].astype(F32)
    state[1] = forward(0)
    final = forward(1)
    for slot in range(4):
        x_land[slot] = final[:, slot * LOC : slot * LOC + LOC].astype(BF)
    for slot in range(4):
        home_start(x_land, out, o_send, o_recv, slot)
    spread_send_wait(cot_in, c_land, c_send, c_recv)
    spread_recv_wait(cot_in, c_land, c_send, c_recv)
    for slot in range(4):
        grad[:, slot * LOC : slot * LOC + LOC] = c_land[slot].astype(F32)

    mlp_back(1, nothing)
    attn_back(1, nothing, nothing, nothing, nothing)
    def after_tile(k):
        if k == 1:
            one.pair_start()

    mlp_back(0, after_tile)

    def after_wo():
        two.pair_start()
        one.pair_finish()
        one.scatter_start(0)

    def before_groups():
        two.pair_finish()
        two.scatter_start(0)

    def between(g):
        @pl.when(g == 1)
        def _():
            one.scatter_finish(0)
            one.scatter_start(1)

        @pl.when(g == 2)
        def _():
            one.scatter_finish(1)
            one.swap_start()
            two.scatter_finish(0)
            two.scatter_start(1)

    def after_query():
        one.swap_finish()
        one.gather_start(1)

    attn_back(0, after_wo, before_groups, between, after_query)
    lane = lax.broadcasted_iota(jnp.int32, (D, 64), 1)
    sum_a = jnp.sum(gg_a[...], axis=1, keepdims=True)
    sum_m = jnp.sum(gg_m[...], axis=1, keepdims=True)
    columns = jnp.where(lane == 0, sum_a, jnp.where(lane == 1, sum_m, 0.0))
    grads[pl.ds(B_WQ + 4 * D, D), 64:] = columns.astype(BF)
    late.pair_start()
    two.scatter_finish(1)
    two.swap_start()
    for slot in range(4):
        c_land[slot] = grad[:, slot * LOC : slot * LOC + LOC].astype(BF)
    late.pair_finish()
    late.scatter_start(0)
    one.gather_finish(1)
    one.gather_start(0)
    two.swap_finish()
    two.gather_start(1)
    late.scatter_finish(0)
    late.scatter_start(1)
    two.gather_finish(1)
    two.gather_start(0)
    late.scatter_finish(1)
    late.swap_start()
    for slot in range(4):
        home_start(c_land, in_grad, i_send, i_recv, slot)
    one.share()
    late.swap_finish()
    late.gather_start(1)
    late.gather_finish(1)
    late.gather_start(0)
    two.share()
    late.share()
    one.share_finish()
    two.share_finish()
    late.share_finish()
    dkv_copy(0).wait_send()
    home_wait(x_land, out, o_send, o_recv)
    home_wait(c_land, in_grad, i_send, i_recv)


def train_step(inputs, docs, gain_a, wq, wk, wv, wo, gain_m, wg, wu, wd, cot):
    hbm = pl.BlockSpec(memory_space=pl.ANY)
    vmem = pl.BlockSpec(memory_space=pltpu.VMEM)
    smem = pl.BlockSpec(memory_space=pltpu.SMEM)
    dma = pltpu.SemaphoreType.DMA
    v = pltpu.VMEM
    scratch = [
        v((D, D), BF), v((192, D), BF), v((192, D), BF), v((D, D), BF), v((D, FF), BF), v((D, FF), BF), v((D, FF), BF),
        v((4, D, LOC), BF), v((4, D, LOC), BF), v((D, 128), F32), v((D, 128), F32),
        v((32, TOK), F32), v((32, TOK), F32), v((2, LOC, CH), F32), v((2, CH, CH), F32), v((2, 8, CH), F32),
        v((2, D, TOK), F32), v((2, D, TOK), F32), v((2, D, TOK), BF), v((2, D, TOK), BF), v((2, D, TOK), BF),
        v((2, KV, 128, 6 * CH), BF), v((2, KV, 144, ROW), BF), v((2, KV, ROW, 128), BF), v((2, KV, 8, 6 * CH), F32),
        v((2, 8, TOK), F32), v((2, 8, TOK), F32), v((2, FF, TOK), BF), v((2, FF, TOK), BF),
        v((D, TOK), F32), v((KV, 128, 6 * CH), BF), v((KV, 8, 6 * CH), F32), v((KV, ROW, 128), F32),
        v((2, 960, TOK), BF), v((KV, TOK, 128), BF), v((2, KV, TOK, 128), BF), v((D, 128), F32), v((D, 128), F32),
        v((FF, TOK), BF), v((D, TOK), BF), v((D, TOK), BF),
        v((TOTAL, 128), BF),
    ]
    for n, part in ((3, EARLY // 12), (3, EARLY // 12), (2, LATE // 4)):
        scratch += [v((n, part, 128), BF), v((n, 3, part // 4, 128), BF), v((n, 3, part // 16, 128), BF)]
        scratch += [v((n, 4, part // 16, 128), BF)]
    scratch += [dma((7,))] + [dma((4,))] * 8 + [dma((2, 2))] * 2 + [dma((2,))] * 2
    for n in (3, 3, 2):
        scratch += [dma((5, n, 3)), dma((5, n, 3)), dma((2 * n,)), dma((2 * n,)), dma((n,))]
    out, in_grad, total = pl.pallas_call(
        step_kernel,
        out_shape=(
            jax.ShapeDtypeStruct((4, D, LOC), BF),
            jax.ShapeDtypeStruct((4, D, LOC), BF),
            jax.ShapeDtypeStruct((TOTAL, 128), BF),
        ),
        in_specs=[hbm, hbm, smem, vmem, vmem] + [hbm] * 7,
        out_specs=(hbm, hbm, hbm),
        scratch_shapes=scratch,
        compiler_params=pltpu.CompilerParams(
            collective_id=0, has_side_effects=True, vmem_limit_bytes=63 * 2**20
        ),
        name="train_step",
    )(inputs, cot, docs, gain_a, gain_m, wq, wk, wv, wo, wg, wu, wd)
    return out, in_grad, total


def unpack_kernel(total, out, in_grad, out_c, in_grad_c, ga, gq, gk, gv, go, gm, gg, gu, gd, land, state, sq, sk, sv, so, sg, su, sd, in_sem, out_sem):
    spans = ((0, TILE), (TILE, TILE), (2 * TILE, TILE), (B_WO, 5 * D), (B_WQ, 5 * D), (B_KV, 5 * KV_ROWS))
    loads = []
    for k, (base, rows) in enumerate(spans):
        loads.append(pltpu.make_async_copy(total.at[pl.ds(base, rows)], land.at[pl.ds(base, rows)], in_sem.at[k]))
        loads[-1].start()
    for k, source in ((6, out), (7, in_grad)):
        loads.append(pltpu.make_async_copy(source, state.at[k - 6], in_sem.at[k]))
        loads[-1].start()
    stores = []

    def store(source, target):
        stores.append(pltpu.make_async_copy(source, target, out_sem.at[len(stores)]))
        stores[-1].start()

    def panels(base, height, width, target):
        for j in range((width + 127) // 128):
            lanes = min(128, width - j * 128)
            target[:, j * 128 : j * 128 + lanes] = land[pl.ds(base + j * height, height), :lanes].astype(F32)

    for k in range(3):
        loads[k].wait()
        for base, source, target in ((B_WD, sd, gd), (B_WG, sg, gg), (B_WU, su, gu)):
            span = slice(k * 512, k * 512 + 512)
            panels(k * TILE + base, D, 512, source.at[:, span])
            store(source.at[:, span], target.at[:, span])
    for k, base, source, target in ((3, B_WO, so, go), (4, B_WQ, sq, gq)):
        loads[k].wait()
        panels(base, D, D, source)
        store(source, target)
    loads[5].wait()
    for j in range(5):
        lanes = min(128, D - j * 128)
        sk[:, j * 128 : j * 128 + lanes] = land[pl.ds(B_KV + j * KV_ROWS, 192), :lanes].astype(F32)
        sv[:, j * 128 : j * 128 + lanes] = land[pl.ds(B_KV + j * KV_ROWS + 192, 192), :lanes].astype(F32)
    store(sk, gk)
    store(sv, gv)
    gains = land[pl.ds(B_WQ + 4 * D, D), :].astype(F32).T
    ga[...] = gains[64]
    gm[...] = gains[65]
    for k, target in ((6, out_c), (7, in_grad_c)):
        loads[k].wait()
        store(state.at[k - 6], target)
    for copy in stores:
        copy.wait()


def unpack(total, out, in_grad):
    hbm = pl.BlockSpec(memory_space=pl.ANY)
    vmem = pl.BlockSpec(memory_space=pltpu.VMEM)
    shape = jax.ShapeDtypeStruct
    v = pltpu.VMEM
    result = pl.pallas_call(
        unpack_kernel,
        out_shape=(
            shape(out.shape, BF), shape(out.shape, BF),
            shape((D,), F32), shape((D, D), F32), shape((192, D), F32), shape((192, D), F32), shape((D, D), F32),
            shape((D,), F32), shape((D, FF), F32), shape((D, FF), F32), shape((D, FF), F32),
        ),
        in_specs=[hbm, hbm, hbm],
        out_specs=(hbm, hbm, vmem, hbm, hbm, hbm, hbm, vmem, hbm, hbm, hbm),
        scratch_shapes=[
            v((TOTAL, 128), BF), v((2,) + out.shape, BF), v((D, D), F32), v((192, D), F32), v((192, D), F32), v((D, D), F32),
            v((D, FF), F32), v((D, FF), F32), v((D, FF), F32),
            pltpu.SemaphoreType.DMA((8,)), pltpu.SemaphoreType.DMA((15,)),
        ],
        compiler_params=pltpu.CompilerParams(vmem_limit_bytes=60 * 2**20),
        name="unpack",
    )(total, out, in_grad)
    return result


def on_device(inputs, docs, gain_a, wq, wk, wv, wo, gain_m, wg, wu, wd, cot):
    out, in_grad, total = train_step(
        inputs.transpose(0, 2, 1), docs, gain_a, wq, wk.T, wv.T, wo, gain_m, wg, wu, wd.T, cot.transpose(0, 2, 1)
    )
    out, in_grad, ga, gq, gk, gv, go, gm, gg, gu, gd = unpack(total, out, in_grad)
    return out.transpose(0, 2, 1), in_grad.transpose(0, 2, 1), ga, gq, gk.T, gv.T, go, gm, gg, gu, gd.T


def solution(mesh):
    token = P("rows", "seq", None)
    in_specs = (token, P("rows", None)) + (P(),) * 9 + (token,)
    out_specs = (token, token) + (P(),) * 9
    return jax.shard_map(on_device, mesh=mesh, in_specs=in_specs, out_specs=out_specs, check_vma=False)
```

```python
import functools

import jax
import jax.numpy as jnp
from jax import lax
from jax.experimental import pallas as pl
from jax.experimental.pallas import tpu as pltpu
from jax.sharding import PartitionSpec as P

D = 576
HEADS = 9
KV = 3
HEAD = 64
FF = 1536
ROW = 1024
LOC = 128
TOK = 512
CH = 256
EPS = 1e-05
THETA = 10000.0
NEG = -1e30
BF = jnp.bfloat16
F32 = jnp.float32
MESH = pl.DeviceIdType.MESH

NN = ((1,), (0,))
NT = ((1,), (1,))
TN = ((0,), (0,))

TILE = 12 * D
B_WD, B_WG, B_WU = 0, 4 * D, 8 * D
B_WO = 3 * TILE
EARLY = 24576
KV_ROWS = 2 * KV * HEAD
LATE1, LATE2 = 3072, 2048
B_Q1 = EARLY
B_K1 = B_Q1 + 3 * D
B_Q2 = EARLY + LATE1
B_K2 = B_Q2 + 2 * D
TOTAL = EARLY + LATE1 + LATE2
ORDERS = (("x", "y", "z"), ("y", "z", "x"), ("z", "x", "y"))
LATE_ORDERS = (("x", "z", "y"), ("z", "x", "y"))


def dot(a, b, dims=NN):
    return lax.dot_general(a, b, (dims, ((), ())), preferred_element_type=F32)


def position():
    s = lax.axis_index("seq")
    r = lax.axis_index("rows")
    return s // 2, s % 2, r // 4, r % 4


def device(y, c, z, x):
    return (y * 2 + c, z * 4 + x)


def mul(offset, size):
    return pl.multiple_of(offset, size)


class Reduction:
    def __init__(self, base, part, orders, grads, landings, sems):
        self.base, self.part, self.grads = base, part, grads
        self.slots = range(len(orders))
        self.landings = landings
        self.send, self.recv, self.pair_s, self.pair_r, self.free = sems
        self.y, self.c, self.z, self.x = position()
        y, z, x = self.y, self.z, self.x
        where = {"x": x, "y": y, "z": z}
        self.orders = orders
        self.index = [[where[a] for a in order] for order in orders]
        self.sizes = (part, part // 4, part // 16)
        self.axes = sorted({order[k] for order in orders for k in range(2)})

    def peer(self, axis, index):
        at = {"x": self.x, "y": self.y, "z": self.z}
        at[axis] = index
        return device(at["y"], self.c, at["z"], at["x"])

    def start_of(self, slot, level, core=None):
        core = self.c if core is None else core
        at = self.base + (2 * slot + core) * self.part
        for k in range(level):
            at = at + self.index[slot][k] * self.sizes[k + 1]
        return at

    def rows(self, ref, start, size):
        return ref.at[pl.ds(mul(start, 16), size)]

    def remote(self, source, target, send, recv, slot, axis, index):
        if axis == "core":
            where = device(self.y, 1 - self.c, self.z, self.x)
        else:
            where = self.peer(axis, index)
        return pltpu.make_async_remote_copy(
            src_ref=source, dst_ref=target, send_sem=send, recv_sem=recv, device_id=where, device_id_type=MESH
        )

    def pair_copy(self, slot):
        rows = self.rows(self.grads, self.start_of(slot, 0, 1 - self.c), self.part)
        return self.remote(rows, self.landings[0].at[slot], self.pair_s.at[slot], self.pair_r.at[slot], slot, "core", 0)

    def pair_start(self):
        for slot in self.slots:
            self.pair_copy(slot).start()

    def pair_finish(self):
        step = min(256, self.part)
        land = self.landings[0]
        for slot in self.slots:
            self.pair_copy(slot).wait()
            at = self.start_of(slot, 0)

            def add(k, carry, slot=slot, at=at):
                here = pl.ds(mul(at + k * step, 16), step)
                there = land[slot, pl.ds(mul(k * step, 16), step), :]
                self.grads[here, :] = (self.grads[here, :].astype(F32) + there.astype(F32)).astype(BF)
                return carry

            lax.fori_loop(0, self.part // step, add, 0)
        where = device(self.y, 1 - self.c, self.z, self.x)
        pl.semaphore_signal(self.free.at[1], inc=1, device_id=where, device_id_type=MESH)

    def counted(self, ref, level, slot):
        axis = self.orders[slot][level % 3]
        index = (self.index[slot][level % 3] + 1) % 4
        return self.remote(ref, ref, self.send.at[level, slot], self.recv.at[level, slot], slot, axis, index)

    def scatter_copy(self, slot, level, d):
        index = (self.index[slot][level] + d) % 4
        size = self.sizes[level + 1]
        return self.remote(
            self.rows(self.grads, self.start_of(slot, level) + index * size, size),
            self.landings[level + 1].at[slot, d - 1],
            self.send.at[level, slot],
            self.recv.at[level, slot],
            slot, self.orders[slot][level], index,
        )

    def scatter_start(self, level):
        for d in (2, 1, 3):
            for slot in self.slots:
                self.scatter_copy(slot, level, d).start()

    def scatter_finish(self, level):
        size = self.sizes[level + 1]
        step = next(k for k in (128, 160, size) if size % k == 0)
        land = self.landings[level + 1]
        for slot in self.slots:
            self.counted(land.at[slot], level, slot).wait()
            at = self.start_of(slot, level + 1)

            def add(k, carry, slot=slot, at=at):
                here = pl.ds(mul(at + k * step, 16), step)
                there = pl.ds(mul(k * step, 16), step)
                total = self.grads[here, :].astype(F32)
                for d in range(3):
                    total = total + land[slot, d, there, :].astype(F32)
                self.grads[here, :] = total.astype(BF)
                return carry

            lax.fori_loop(0, size // step, add, 0)
        if level == 1:
            at = {"x": self.x, "y": self.y, "z": self.z}
            for axis in self.axes:
                for d in (1, 2, 3):
                    where = self.peer(axis, (at[axis] + d) % 4)
                    pl.semaphore_signal(self.free.at[0], inc=1, device_id=where, device_id_type=MESH)

    def swap_copy(self, slot, d):
        mine = self.index[slot][2]
        return self.remote(
            self.rows(self.grads, self.start_of(slot, 2), self.sizes[2]),
            self.landings[3].at[slot, mine], self.send.at[2, slot], self.recv.at[2, slot],
            slot, self.orders[slot][2], (mine + d) % 4,
        )

    def swap_start(self):
        for d in (2, 1, 3):
            for slot in self.slots:
                self.swap_copy(slot, d).start()
        for slot in self.slots:
            at = pl.ds(mul(self.start_of(slot, 2), 16), self.sizes[2])
            self.landings[3][slot, self.index[slot][2]] = self.grads[at, :]

    def swap_finish(self):
        land = self.landings[3]
        for slot in self.slots:
            self.counted(land.at[slot, pl.ds(0, 3)], 2, slot).wait()
            total = land[slot, 0].astype(F32)
            for k in range(1, 4):
                total = total + land[slot, k].astype(F32)
            self.grads[pl.ds(mul(self.start_of(slot, 2), 16), self.sizes[2]), :] = total.astype(BF)

    def gather_copy(self, slot, level, d):
        mine = self.index[slot][level]
        rows = self.rows(self.grads, self.start_of(slot, level + 1), self.sizes[level + 1])
        return self.remote(
            rows, rows, self.send.at[3 + level, slot], self.recv.at[3 + level, slot],
            slot, self.orders[slot][level], (mine + d) % 4,
        )

    def gather_start(self, level):
        if level == 1:
            pl.semaphore_wait(self.free.at[0], 3 * len(self.axes))
        for d in (2, 1, 3):
            for slot in self.slots:
                self.gather_copy(slot, level, d).start()

    def gather_finish(self, level):
        for slot in self.slots:
            self.gather_wait(slot, level)

    def gather_wait(self, slot, level):
        rows = self.rows(self.grads, self.start_of(slot, level), 3 * self.sizes[level + 1])
        self.counted(rows, 3 + level, slot).wait()

    def share_copy(self, slot, core):
        rows = self.rows(self.grads, self.start_of(slot, 0, core), self.part)
        n = len(self.slots)
        return self.remote(rows, rows, self.pair_s.at[n + slot], self.pair_r.at[n + slot], slot, "core", 0)

    def share(self):
        pl.semaphore_wait(self.free.at[1], 1)
        for slot in self.slots:
            self.gather_wait(slot, 0)
            self.share_copy(slot, self.c).start()

    def share_finish(self):
        for slot in self.slots:
            self.share_copy(slot, self.c).wait_send()
            self.share_copy(slot, 1 - self.c).wait_recv()


def step_kernel(
    x_in, cot_in, docs, gain_a, gain_m, wq_h, wk_h, wv_h, wo_h, wg_h, wu_h, wd_h,
    out, in_grad, grads,
    wq, wkv, wo, wg, wu, wd,
    x_land, c_land, gain_at, gain_mt, cos_t, sin_t, bias_f, bias_d, big,
    state, after, n_a, n_m, mix, qz, kvt, kvn, lse, root_a, root_m, gate, up,
    grad, d_oz, delta, dkv, dqkv, dkv_out, dkv_in, gg_a, gg_m, hid_keep, g_keep, d_keep,
    a0, a1, a2, a3, b0, b1, b2, b3, l0, l1, l2, l3, m0, m1, m2, m3,
    w_sem, x_send, x_recv, c_send, c_recv, o_send, o_recv, i_send, i_recv, kv_send, kv_recv, dkv_send, dkv_recv,
    a_s, a_r, a_ps, a_pr, a_f, b_s, b_r, b_ps, b_pr, b_f, l_s, l_r, l_ps, l_pr, l_f, m_s, m_r, m_ps, m_pr, m_f,
):
    y, c, z, x = position()
    me = y * 2 + c
    my_slot = (me + 2) % 4
    to_core = ((me + 2) % 8) // 4
    chunk_a = 3 - 2 * c
    chunk_b = 2 * c

    barrier = pltpu.get_barrier_semaphore()
    for k in range(1, 8):
        pl.semaphore_signal(barrier, inc=1, device_id=((me + k) % 8, z * 4 + x), device_id_type=MESH)
    for k in range(1, 4):
        pl.semaphore_signal(barrier, inc=1, device_id=device(y, c, (z + k) % 4, x), device_id_type=MESH)
        pl.semaphore_signal(barrier, inc=1, device_id=device(y, c, z, (x + k) % 4), device_id_type=MESH)
    weight_pairs = [(wq_h, wq), (wo_h, wo), (wg_h, wg), (wu_h, wu), (wd_h, wd)]
    for g in range(KV):
        for k, source in enumerate((wk_h, wv_h)):
            pair = (source.at[pl.ds(g * HEAD, HEAD)], wkv.at[pl.ds((2 * g + k) * HEAD, HEAD)])
            weight_pairs.append(pair)
    loads = [pltpu.make_async_copy(a, b, w_sem.at[k]) for k, (a, b) in enumerate(weight_pairs)]
    pl.semaphore_wait(barrier, 13)

    def spread(source, land, send, recv, k):
        r = (y + k) % 4
        target = r * 2 + to_core
        remote = pltpu.make_async_remote_copy(
            src_ref=source.at[r], dst_ref=land.at[my_slot], send_sem=send.at[k], recv_sem=recv.at[my_slot],
            device_id=(target, z * 4 + x), device_id_type=MESH,
        )
        local = pltpu.make_async_copy(source.at[r], land.at[my_slot], send.at[k])
        return target == me, remote, local

    def spread_start(source, land, send, recv):
        for k in (2, 1, 3, 0):
            own, remote, local = spread(source, land, send, recv, k)
            pl.when(own)(local.start)
            pl.when(jnp.logical_not(own))(remote.start)

    def spread_send_wait(source, land, send, recv):
        for k in range(4):
            own, remote, local = spread(source, land, send, recv, k)
            pl.when(own)(local.wait)
            pl.when(jnp.logical_not(own))(remote.wait_send)

    def spread_recv_wait(source, land, send, recv):
        for slot in range(4):
            home = (slot + 6 + 4 * c) % 8
            landed = pltpu.make_async_remote_copy(
                src_ref=source.at[0], dst_ref=land.at[slot], send_sem=send.at[0], recv_sem=recv.at[slot],
                device_id=(home, z * 4 + x), device_id_type=MESH,
            )
            pl.when(home != me)(landed.wait_recv)

    def home_copy(source, result, send, recv, slot):
        home = (slot + 6 + 4 * c) % 8
        remote = pltpu.make_async_remote_copy(
            src_ref=source.at[slot], dst_ref=result.at[y], send_sem=send.at[slot], recv_sem=recv.at[y],
            device_id=(home, z * 4 + x), device_id_type=MESH,
        )
        local = pltpu.make_async_copy(source.at[slot], result.at[y], send.at[slot])
        return home == me, remote, local

    def home_start(source, result, send, recv, slot):
        own, remote, local = home_copy(source, result, send, recv, slot)
        pl.when(own)(local.start)
        pl.when(jnp.logical_not(own))(remote.start)

    def home_wait(source, result, send, recv):
        for slot in range(4):
            own, remote, local = home_copy(source, result, send, recv, slot)
            pl.when(own)(local.wait)
            pl.when(jnp.logical_not(own))(remote.wait_send)
        for r in range(4):
            origin = r * 2 + to_core
            landed = pltpu.make_async_remote_copy(
                src_ref=source.at[0], dst_ref=result.at[r], send_sem=send.at[0], recv_sem=recv.at[r],
                device_id=(origin, z * 4 + x), device_id_type=MESH,
            )
            pl.when(origin != me)(landed.wait_recv)

    spread_start(x_in, x_land, x_send, x_recv)
    for load in loads:
        load.start()

    end0 = docs[y, 0]
    end1 = end0 + docs[y, 1]
    column = lax.broadcasted_iota(jnp.int32, (1, TOK), 1)
    token = jnp.where(column < CH, column + chunk_a * CH, column - CH + chunk_b * CH)
    first = jnp.where(token < end0, 0, jnp.where(token < end1, end0, end1))
    place = (token - first).astype(F32)
    half = lax.broadcasted_iota(jnp.int32, (HEAD // 2, TOK), 0).astype(F32)
    angles = place * jnp.exp(half * (-2.0 / HEAD * 9.210340371976184))
    cos_t[...] = jnp.cos(angles)
    sin_t[...] = jnp.sin(angles)
    for n, chunk in enumerate((chunk_a, chunk_b)):
        cols = slice(n * CH, n * CH + CH)
        fi, tk = first[:, cols], token[:, cols]
        key = lax.broadcasted_iota(jnp.int32, (LOC, CH), 0)
        bias_f[n] = jnp.where(key >= fi, 0.0, NEG).astype(F32)
        key = lax.broadcasted_iota(jnp.int32, (CH, CH), 0) + chunk * CH
        bias_d[n] = jnp.where((key >= fi) & (key <= tk), 0.0, NEG).astype(F32)
        big[n] = jnp.broadcast_to(jnp.where(fi > LOC, -NEG, 0.0).astype(F32), (8, CH))
    gain_at[...] = jnp.broadcast_to(gain_a[...].reshape(1, D), (128, D)).T
    gain_mt[...] = jnp.broadcast_to(gain_m[...].reshape(1, D), (128, D)).T
    gg_a[...] = jnp.zeros(gg_a.shape, F32)
    gg_m[...] = jnp.zeros(gg_m.shape, F32)
    for app in range(2):
        qz[app, :, HEAD:, :] = jnp.zeros((KV, HEAD, 6 * CH), BF)
        kvt[app, :, 2 * HEAD :, :] = jnp.ones((KV, 16, ROW), BF)
    d_oz[:, :HEAD, :] = jnp.zeros((KV, HEAD, 6 * CH), BF)
    grads[pl.ds(B_WO + 4 * D, D), :] = jnp.zeros((D, 128), BF)
    grads[pl.ds(B_WO + 5 * D, EARLY - B_WO - 5 * D), :] = jnp.zeros((EARLY - B_WO - 5 * D, 128), BF)
    for start, end in ((B_K1 + 4 * 256, EARLY + LATE1), (B_K2 + 4 * 128, TOTAL)):
        grads[pl.ds(start, end - start), :] = jnp.zeros((end - start, 128), BF)

    def wide(gain):
        return jnp.concatenate([gain[...]] * 4, axis=1)

    def norm(values, gain, roots, app):
        root = lax.rsqrt(jnp.mean(values * values, axis=0, keepdims=True) + EPS)
        roots[app] = jnp.broadcast_to(root, (8, TOK))
        return (values * root * wide(gain)).astype(BF)

    def turn(a, b, sign):
        cs, sn = cos_t[...], sin_t[...]
        if sign > 0:
            return a * cs - b * sn, b * cs + a * sn
        return a * cs + b * sn, b * cs - a * sn

    def kv_copy(app, n):
        chunk = chunk_a if n == 0 else chunk_b
        span = kvt.at[app, :, pl.ds(0, 2 * HEAD), pl.ds(mul(chunk * CH, CH), CH)]
        return pltpu.make_async_remote_copy(
            src_ref=span, dst_ref=span, send_sem=kv_send.at[app, n], recv_sem=kv_recv.at[app, n],
            device_id=device(y, 1 - c, z, x), device_id_type=MESH,
        )

    def kv_arrival(app, n):
        chunk = 3 - 2 * (1 - c) if n == 0 else 2 * (1 - c)
        span = kvt.at[app, :, pl.ds(0, 2 * HEAD), pl.ds(mul(chunk * CH, CH), CH)]
        return pltpu.make_async_remote_copy(
            src_ref=span, dst_ref=span, send_sem=kv_send.at[app, n], recv_sem=kv_recv.at[app, n],
            device_id=device(y, 1 - c, z, x), device_id_type=MESH,
        )

    plans = (((0, 3), (1, 0)), ((0, 1), (1, 2)))

    def softmax(s, n, chunk):
        nk = (chunk + 1) * CH
        tail = s[nk - CH :] + bias_d[n]
        top = jnp.max(tail, axis=0, keepdims=True)
        if chunk == 0:
            return top, jnp.exp(tail - top).astype(BF)
        lead = s[:LOC] + bias_f[n]
        shut = big[n][0:1]
        middle = s[LOC : nk - CH]
        top = jnp.maximum(top, jnp.max(lead, axis=0, keepdims=True))
        top = jnp.maximum(top, jnp.max(middle, axis=0, keepdims=True) - shut)
        low = [jnp.exp(lead - top), jnp.exp(middle - (top + shut)), jnp.exp(tail - top)]
        return top, jnp.concatenate([v.astype(BF) for v in low], axis=0)

    def attend(app, plan):
        def group(g, carry):
            scores = []
            for n, chunk in plan:
                nk = (chunk + 1) * CH
                scores.append(dot(kvn[app, g, :nk, :], qz[app, g, :, n * 768 : n * 768 + 768]))
            for (n, chunk), s in zip(plan, scores):
                nk = (chunk + 1) * CH
                for j in range(3):
                    top, low = softmax(s[:, j * CH : j * CH + CH], n, chunk)
                    mixed = dot(kvt[app, g, HEAD:, :nk], low)
                    total_w = mixed[HEAD : HEAD + 1]
                    rows = pl.ds(mul(g * 192 + j * HEAD, HEAD), HEAD)
                    mix[app, rows, n * CH : n * CH + CH] = (mixed[:HEAD] * (1.0 / total_w)).astype(BF)
                    at = n * 768 + j * CH
                    lse[app, g, :, at : at + CH] = jnp.broadcast_to(top + jnp.log(total_w), (8, CH))
            return carry

        lax.fori_loop(0, KV, group, 0)

    def forward(app):
        values = state[app]
        low = norm(values, gain_at, root_a, app)
        n_a[app] = low
        if app == 0:
            for load in loads[5:]:
                load.wait()
        raw = dot(wkv[...], low)
        for g in range(KV):
            a, b = turn(raw[g * 128 : g * 128 + 32], raw[g * 128 + 32 : g * 128 + 64], 1)
            packed = jnp.concatenate([a, b, raw[g * 128 + 64 : g * 128 + 128]], axis=0).astype(BF)
            for n, chunk in enumerate((chunk_a, chunk_b)):
                kvt[app, g, : 2 * HEAD, pl.ds(mul(chunk * CH, CH), CH)] = packed[:, n * CH : n * CH + CH]
        kv_copy(app, 0).start()
        kv_copy(app, 1).start()
        for n, chunk in enumerate((chunk_a, chunk_b)):
            for g in range(KV):
                part = kvt[app, g, : 2 * HEAD, pl.ds(mul(chunk * CH, CH), CH)]
                kvn[app, g, pl.ds(mul(chunk * CH, CH), CH), :] = part.T
        if app == 0:
            loads[0].wait()
        query_raw = dot(wq[...], low, TN)
        for h in range(HEADS):
            g, j = h // 3, h % 3
            a, b = turn(query_raw[h * 64 : h * 64 + 32], query_raw[h * 64 + 32 : h * 64 + 64], 1)
            both = (jnp.concatenate([a, b], axis=0) * 0.125).astype(BF)
            for n in range(2):
                at = n * 768 + j * CH
                qz[app, g, :HEAD, at : at + CH] = both[:, n * CH : n * CH + CH]
        for n in range(2):
            kv_copy(app, n).wait_send()
            kv_arrival(app, n).wait_recv()
            chunk = 3 - 2 * (1 - c) if n == 0 else 2 * (1 - c)
            for g in range(KV):
                part = kvt[app, g, : 2 * HEAD, pl.ds(mul(chunk * CH, CH), CH)]
                kvn[app, g, pl.ds(mul(chunk * CH, CH), CH), :] = part.T
        pl.when(c == 0)(lambda: attend(app, plans[0]))
        pl.when(c == 1)(lambda: attend(app, plans[1]))
        if app == 0:
            loads[1].wait()
        att = state[app] + dot(wo[...], mix[app], TN)
        after[app] = att
        low = norm(att, gain_mt, root_m, app)
        n_m[app] = low
        if app == 0:
            for load in loads[2:5]:
                load.wait()
        result = att
        for k in range(3):
            span = slice(k * 512, k * 512 + 512)
            pre = dot(wg[:, span], low, TN)
            pre_up = dot(wu[:, span], low, TN)
            gate[app, span, :] = pre.astype(BF)
            up[app, span, :] = pre_up.astype(BF)
            hidden = (pre * (1.0 / (1.0 + jnp.exp(-pre))) * pre_up).astype(BF)
            result = result + dot(wd[:, span], hidden)
        return result

    def put(base, height, value, add=False):
        width = value.shape[1]
        for j in range((width + 127) // 128):
            lanes = min(128, width - j * 128)
            here = pl.ds(base + j * height, height)
            part = value[:, j * 128 : j * 128 + lanes]
            if add:
                part = part + grads[here, :lanes].astype(F32)
            grads[here, :lanes] = part.astype(BF)

    def fold(value):
        return value[:, :128] + value[:, 128:256] + value[:, 256:384] + value[:, 384:]

    def norm_back(d_normed, values, root, gain, sums):
        scaled = d_normed * wide(gain)
        sums[...] += fold(d_normed * (values * root))
        mean = jnp.mean(scaled * values, axis=0, keepdims=True)
        return root * scaled - values * (root * root * root * mean)

    one = Reduction(0, EARLY // 12, ORDERS, grads, (a0, a1, a2, a3), (a_s, a_r, a_ps, a_pr, a_f))
    two = Reduction(EARLY // 2, EARLY // 12, ORDERS, grads, (b0, b1, b2, b3), (b_s, b_r, b_ps, b_pr, b_f))
    third = Reduction(EARLY, LATE1 // 4, LATE_ORDERS, grads, (l0, l1, l2, l3), (l_s, l_r, l_ps, l_pr, l_f))
    four = Reduction(EARLY + LATE1, LATE2 // 4, LATE_ORDERS, grads, (m0, m1, m2, m3), (m_s, m_r, m_ps, m_pr, m_f))

    def mlp_back(app, after_tile):
        g_low = grad[...].astype(BF)
        if app == 1:
            g_keep[...] = g_low
        d_normed = None
        for k in range(3):
            span = slice(k * 512, k * 512 + 512)
            d_hidden = dot(wd[:, span], g_low, TN).astype(BF).astype(F32)
            pre = gate[app, span, :].astype(F32)
            pre_up = up[app, span, :].astype(F32)
            s = 1.0 / (1.0 + jnp.exp(-pre))
            act = pre * s
            hidden = (act * pre_up).astype(BF)
            d_gate = (d_hidden * pre_up * (s + act * (1.0 - s))).astype(BF)
            d_up = (d_hidden * act).astype(BF)
            if app == 1:
                hid_keep[span, :] = hidden
                gate[1, span, :] = d_gate
                up[1, span, :] = d_up
            else:
                put(k * TILE + B_WD, D, dot(g_low, hidden, NT) + dot(g_keep[...], hid_keep[span, :], NT))
                put(k * TILE + B_WG, D, dot(n_m[0], d_gate, NT) + dot(n_m[1], gate[1, span, :], NT))
                put(k * TILE + B_WU, D, dot(n_m[0], d_up, NT) + dot(n_m[1], up[1, span, :], NT))
            term = dot(wg[:, span], d_gate) + dot(wu[:, span], d_up)
            d_normed = term if d_normed is None else d_normed + term
            after_tile(k)
        grad[...] += norm_back(d_normed, after[app], root_m[app][0:1], gain_mt, gg_m)

    def attend_back(app, plan, between):
        dkv[...] = jnp.zeros(dkv.shape, F32)

        def products(g, n, k):
            cols = slice(n * 768, n * 768 + 768)
            rows = slice(k * CH, k * CH + CH)
            return dot(kvn[app, g, rows, :], qz[app, g, :, cols]), dot(kvn[app, g, rows, :], d_oz[g, :, cols])

        def three(v):
            return jnp.concatenate([v] * 3, axis=1)

        def group(g, carry):
            tiles = [(n, chunk, k) for n, chunk in plan for k in range(chunk + 1)]
            coming = products(g, tiles[0][0], tiles[0][2])
            d_query = None
            for i, (n, chunk, k) in enumerate(tiles):
                s, d_probs = coming
                if i + 1 < len(tiles):
                    coming = products(g, tiles[i + 1][0], tiles[i + 1][2])
                cols = slice(n * 768, n * 768 + 768)
                rows = slice(k * CH, k * CH + CH)
                log_sum = lse[app, g, 0:1, cols]
                if k == chunk:
                    s = s + three(bias_d[n])
                elif k == 0:
                    s = jnp.concatenate([s[:LOC] + three(bias_f[n]), s[LOC:] - three(big[n][0:1])], axis=0)
                else:
                    log_sum = log_sum + three(big[n][0:1])
                probs = jnp.exp(s - log_sum)
                d_score = (probs * (d_probs - delta[g, 0:1, cols])).astype(BF)
                low = probs.astype(BF)
                term = dot(kvt[app, g, :HEAD, rows], d_score)
                d_query = term if k == 0 else d_query + term
                dkv[g, rows, :] += dot(d_score, qz[app, g, :, cols], NT) + dot(low, d_oz[g, :, cols], NT)
                if k < chunk:
                    continue
                d_query = d_query * 0.125
                at = slice(n * CH, n * CH + CH)
                cs, sn = cos_t[:, at], sin_t[:, at]
                for j in range(3):
                    head = pl.ds(mul(g * 192 + j * HEAD, HEAD), HEAD)
                    a, b = d_query[:32, j * CH : j * CH + CH], d_query[32:, j * CH : j * CH + CH]
                    both = jnp.concatenate([a * cs + b * sn, b * cs - a * sn], axis=0)
                    dqkv[app, head, at] = both.astype(BF)
            for n in range(2):
                chunk = 3 - 2 * (1 - c) if n == 0 else 2 * (1 - c)
                dkv_out[g, n * CH : n * CH + CH, :] = dkv[g, pl.ds(mul(chunk * CH, CH), CH), :].astype(BF)
            dkv_copy(app, g).start()
            between(g)
            return carry

        lax.fori_loop(0, KV, group, 0)

    def dkv_copy(app, g):
        return pltpu.make_async_remote_copy(
            src_ref=dkv_out.at[g], dst_ref=dkv_in.at[app, g], send_sem=dkv_send.at[app, g],
            recv_sem=dkv_recv.at[app, g], device_id=device(y, 1 - c, z, x), device_id_type=MESH,
        )

    def attn_back(app, before, before_groups, between, after_query):
        g_low = grad[...].astype(BF)
        if app == 1:
            d_keep[...] = g_low
        else:
            put(B_WO, D, dot(mix[0], g_low, NT) + dot(mix[1], d_keep[...], NT))
        before()
        d_mixed = dot(wo[...], g_low)
        for h in range(HEADS):
            g, j = h // 3, h % 3
            dm = d_mixed[h * 64 : h * 64 + 64].astype(BF)
            dl = jnp.sum(dm.astype(F32) * mix[app, h * 64 : h * 64 + 64, :].astype(F32), axis=0, keepdims=True)
            for n in range(2):
                at = n * 768 + j * CH
                d_oz[g, HEAD:, at : at + CH] = dm[:, n * CH : n * CH + CH]
                delta[g, :, at : at + CH] = jnp.broadcast_to(dl[:, n * CH : n * CH + CH], (8, CH))
        before_groups()
        if app == 0:
            for span in (0, 1):
                put_late(1, span, False)
        pl.when(c == 0)(lambda: attend_back(app, plans[0], between))
        pl.when(c == 1)(lambda: attend_back(app, plans[1], between))
        dq = dqkv[app, :D, :]
        if app == 0:
            put_late_query(0, 1, True)
        d_normed = dot(wq[...], dq)
        after_query()
        if app == 0:
            join_keys(0, (2,))
            put_late_keys(0, 1, True)
        else:
            join_keys(1, range(KV))
        d_normed = d_normed + dot(wkv[...], dqkv[app, D:, :], TN)
        grad[...] += norm_back(d_normed, state[app], root_a[app][0:1], gain_at, gg_a)

    def join_keys(app, groups):
        for g in groups:
            dkv_copy(app, g).wait()
            parts = []
            for n, chunk in enumerate((chunk_a, chunk_b)):
                own = dkv[g, pl.ds(mul(chunk * CH, CH), CH), :]
                other = dkv_in[app, g, n * CH : n * CH + CH, :].astype(F32)
                parts.append((own + other).T)
            both = jnp.concatenate(parts, axis=1)
            a, b = turn(both[:32], both[32:64], -1)
            at = D + g * 2 * HEAD
            dqkv[app, at : at + 2 * HEAD, :] = jnp.concatenate([a, b, both[64:]], axis=0).astype(BF)

    def put_late_query(app, span, add):
        base, start, end = ((B_Q1, 0, 384), (B_Q2, 384, D))[span]
        put(base, D, dot(n_a[app], dqkv[app, start:end, :], NT), add)

    def put_late_keys(app, span, add):
        base, start, end = ((B_K1, D, D + 256), (B_K2, D + 256, D + KV_ROWS))[span]
        put(base, end - start, dot(dqkv[app, start:end, :], n_a[app], NT), add)

    def put_late(app, span, add):
        put_late_query(app, span, add)
        put_late_keys(app, span, add)

    def nothing(*unused):
        return None

    spread_send_wait(x_in, x_land, x_send, x_recv)
    spread_recv_wait(x_in, x_land, x_send, x_recv)
    spread_start(cot_in, c_land, c_send, c_recv)
    for slot in range(4):
        state[0, :, slot * LOC : slot * LOC + LOC] = x_land[slot].astype(F32)
    state[1] = forward(0)
    final = forward(1)
    for slot in range(4):
        x_land[slot] = final[:, slot * LOC : slot * LOC + LOC].astype(BF)
    for slot in range(4):
        home_start(x_land, out, o_send, o_recv, slot)
    spread_send_wait(cot_in, c_land, c_send, c_recv)
    spread_recv_wait(cot_in, c_land, c_send, c_recv)
    for slot in range(4):
        grad[:, slot * LOC : slot * LOC + LOC] = c_land[slot].astype(F32)

    mlp_back(1, nothing)
    attn_back(1, nothing, nothing, nothing, nothing)
    def after_tile(k):
        if k == 1:
            one.pair_start()
        if k == 2:
            one.pair_finish()
            one.scatter_start(0)

    mlp_back(0, after_tile)

    def before_groups():
        two.pair_finish()
        two.scatter_start(0)

    def between(g):
        @pl.when(g == 0)
        def _():
            one.scatter_finish(0)
            one.scatter_start(1)

        @pl.when(g == 1)
        def _():
            one.scatter_finish(1)
            one.swap_start()
            join_keys(0, (0, 1))
            put_late(0, 0, True)
            third.pair_start()

        @pl.when(g == 2)
        def _():
            one.swap_finish()
            one.gather_start(1)
            two.scatter_finish(0)
            two.scatter_start(1)
            third.pair_finish()
            third.scatter_start(0)

    attn_back(0, two.pair_start, before_groups, between, nothing)
    lane = lax.broadcasted_iota(jnp.int32, (D, 64), 1)
    sum_a = jnp.sum(gg_a[...], axis=1, keepdims=True)
    sum_m = jnp.sum(gg_m[...], axis=1, keepdims=True)
    columns = jnp.where(lane == 0, sum_a, jnp.where(lane == 1, sum_m, 0.0))
    grads[pl.ds(B_Q2 + D, D), 64:] = columns.astype(BF)
    four.pair_start()
    for slot in range(4):
        c_land[slot] = grad[:, slot * LOC : slot * LOC + LOC].astype(BF)
    for slot in range(4):
        home_start(c_land, in_grad, i_send, i_recv, slot)
    two.scatter_finish(1)
    two.swap_start()
    four.pair_finish()
    four.scatter_start(0)
    one.gather_finish(1)
    one.gather_start(0)
    third.scatter_finish(0)
    third.scatter_start(1)
    two.swap_finish()
    two.gather_start(1)
    four.scatter_finish(0)
    four.scatter_start(1)
    third.scatter_finish(1)
    third.swap_start()
    two.gather_finish(1)
    two.gather_start(0)
    four.scatter_finish(1)
    four.swap_start()
    third.swap_finish()
    third.gather_start(1)
    one.share()
    four.swap_finish()
    four.gather_start(1)
    third.gather_finish(1)
    third.gather_start(0)
    four.gather_finish(1)
    four.gather_start(0)
    two.share()
    third.share()
    four.share()
    one.share_finish()
    two.share_finish()
    third.share_finish()
    four.share_finish()
    home_wait(x_land, out, o_send, o_recv)
    home_wait(c_land, in_grad, i_send, i_recv)


def train_step(inputs, docs, gain_a, wq, wk, wv, wo, gain_m, wg, wu, wd, cot):
    hbm = pl.BlockSpec(memory_space=pl.ANY)
    vmem = pl.BlockSpec(memory_space=pltpu.VMEM)
    smem = pl.BlockSpec(memory_space=pltpu.SMEM)
    dma = pltpu.SemaphoreType.DMA
    v = pltpu.VMEM
    scratch = [
        v((D, D), BF), v((KV_ROWS, D), BF), v((D, D), BF), v((D, FF), BF), v((D, FF), BF), v((D, FF), BF),
        v((4, D, LOC), BF), v((4, D, LOC), BF), v((D, 128), F32), v((D, 128), F32),
        v((32, TOK), F32), v((32, TOK), F32), v((2, LOC, CH), F32), v((2, CH, CH), F32), v((2, 8, CH), F32),
        v((2, D, TOK), F32), v((2, D, TOK), F32), v((2, D, TOK), BF), v((2, D, TOK), BF), v((2, D, TOK), BF),
        v((2, KV, 128, 6 * CH), BF), v((2, KV, 144, ROW), BF), v((2, KV, ROW, 128), BF), v((2, KV, 8, 6 * CH), F32),
        v((2, 8, TOK), F32), v((2, 8, TOK), F32), v((2, FF, TOK), BF), v((2, FF, TOK), BF),
        v((D, TOK), F32), v((KV, 128, 6 * CH), BF), v((KV, 8, 6 * CH), F32), v((KV, ROW, 128), F32),
        v((2, 960, TOK), BF), v((KV, TOK, 128), BF), v((2, KV, TOK, 128), BF), v((D, 128), F32), v((D, 128), F32),
        v((FF, TOK), BF), v((D, TOK), BF), v((D, TOK), BF),
    ]
    for n, part in ((3, EARLY // 12), (3, EARLY // 12), (2, LATE1 // 4), (2, LATE2 // 4)):
        scratch += [v((n, part, 128), BF), v((n, 3, part // 4, 128), BF), v((n, 3, part // 16, 128), BF)]
        scratch += [v((n, 4, part // 16, 128), BF)]
    scratch += [dma((11,))] + [dma((4,))] * 8 + [dma((2, 2))] * 2 + [dma((2, KV))] * 2
    for n in (3, 3, 2, 2):
        scratch += [dma((5, n)), dma((5, n)), dma((2 * n,)), dma((2 * n,)), pltpu.SemaphoreType.REGULAR((2,))]
    out, in_grad, total = pl.pallas_call(
        step_kernel,
        out_shape=(
            jax.ShapeDtypeStruct((4, D, LOC), BF),
            jax.ShapeDtypeStruct((4, D, LOC), BF),
            pltpu.VMEM((TOTAL, 128), BF),
        ),
        in_specs=[hbm, hbm, smem, vmem, vmem] + [hbm] * 7,
        out_specs=(hbm, hbm, vmem),
        scratch_shapes=scratch,
        compiler_params=pltpu.CompilerParams(
            collective_id=0, has_side_effects=True, vmem_limit_bytes=55 * 2**20
        ),
        name="train_step",
    )(inputs, cot, docs, gain_a, gain_m, wq, wk, wv, wo, wg, wu, wd)
    return out, in_grad, total


def unpack_kernel(total, out, in_grad, out_c, in_grad_c, ga, gq, gk, gv, go, gm, gg, gu, gd, state, sq, sk, sv, so, sg, su, sd, in_sem, out_sem):
    loads = [pltpu.make_async_copy(a, state.at[k], in_sem.at[k]) for k, a in enumerate((out, in_grad))]
    for load in loads:
        load.start()
    stores = []

    def store(source, target):
        stores.append(pltpu.make_async_copy(source, target, out_sem.at[len(stores)]))
        stores[-1].start()

    def panels(base, height, width, target):
        for j in range((width + 127) // 128):
            lanes = min(128, width - j * 128)
            target[:, j * 128 : j * 128 + lanes] = total[pl.ds(base + j * height, height), :lanes].astype(F32)

    for k in range(3):
        for base, source, target in ((B_WD, sd, gd), (B_WG, sg, gg), (B_WU, su, gu)):
            span = slice(k * 512, k * 512 + 512)
            panels(k * TILE + base, D, 512, source.at[:, span])
            store(source.at[:, span], target.at[:, span])
    panels(B_WO, D, D, so)
    store(so, go)
    panels(B_Q1, D, 384, sq.at[:, :384])
    panels(B_Q2, D, 192, sq.at[:, 384:])
    store(sq, gq)
    for g, base, height in ((0, B_K1, 256), (1, B_K1 + 128, 256), (2, B_K2, 128)):
        for k, target in enumerate((sk, sv)):
            for j in range(5):
                lanes = min(128, D - j * 128)
                rows = pl.ds(base + j * height + k * HEAD, HEAD)
                target[g * HEAD : g * HEAD + HEAD, j * 128 : j * 128 + lanes] = total[rows, :lanes].astype(F32)
    store(sk, gk)
    store(sv, gv)
    gains = total[pl.ds(B_Q2 + D, D), :].astype(F32).T
    ga[...] = gains[64]
    gm[...] = gains[65]
    for k, target in enumerate((out_c, in_grad_c)):
        loads[k].wait()
        store(state.at[k], target)
    for copy in stores:
        copy.wait()


def unpack(total, out, in_grad):
    hbm = pl.BlockSpec(memory_space=pl.ANY)
    vmem = pl.BlockSpec(memory_space=pltpu.VMEM)
    shape = jax.ShapeDtypeStruct
    v = pltpu.VMEM
    result = pl.pallas_call(
        unpack_kernel,
        out_shape=(
            shape(out.shape, BF), shape(out.shape, BF),
            shape((D,), F32), shape((D, D), F32), shape((192, D), F32), shape((192, D), F32), shape((D, D), F32),
            shape((D,), F32), shape((D, FF), F32), shape((D, FF), F32), shape((D, FF), F32),
        ),
        in_specs=[vmem, hbm, hbm],
        out_specs=(hbm, hbm, vmem, hbm, hbm, hbm, hbm, vmem, hbm, hbm, hbm),
        scratch_shapes=[
            v((2,) + out.shape, BF), v((D, D), F32), v((192, D), F32), v((192, D), F32), v((D, D), F32),
            v((D, FF), F32), v((D, FF), F32), v((D, FF), F32),
            pltpu.SemaphoreType.DMA((2,)), pltpu.SemaphoreType.DMA((15,)),
        ],
        compiler_params=pltpu.CompilerParams(vmem_limit_bytes=56 * 2**20),
        name="unpack",
    )(pltpu.with_memory_space_constraint(total, pltpu.VMEM), out, in_grad)
    return result


def on_device(inputs, docs, gain_a, wq, wk, wv, wo, gain_m, wg, wu, wd, cot):
    out, in_grad, total = train_step(
        inputs.transpose(0, 2, 1), docs, gain_a, wq, wk.T, wv.T, wo, gain_m, wg, wu, wd.T, cot.transpose(0, 2, 1)
    )
    out, in_grad, ga, gq, gk, gv, go, gm, gg, gu, gd = unpack(total, out, in_grad)
    return out.transpose(0, 2, 1), in_grad.transpose(0, 2, 1), ga, gq, gk.T, gv.T, go, gm, gg, gu, gd.T


def solution(mesh):
    token = P("rows", "seq", None)
    in_specs = (token, P("rows", None)) + (P(),) * 9 + (token,)
    out_specs = (token, token) + (P(),) * 9
    return jax.shard_map(on_device, mesh=mesh, in_specs=in_specs, out_specs=out_specs, check_vma=False)
```

```python
import functools

import jax
import jax.numpy as jnp
from jax import lax
from jax.experimental import pallas as pl
from jax.experimental.pallas import tpu as pltpu
from jax.sharding import PartitionSpec as P

D = 576
HEADS = 9
KV = 3
HEAD = 64
FF = 1536
ROW = 1024
LOC = 128
TOK = 512
CH = 256
EPS = 1e-05
THETA = 10000.0
NEG = -1e30
BF = jnp.bfloat16
F32 = jnp.float32
MESH = pl.DeviceIdType.MESH

NN = ((1,), (0,))
NT = ((1,), (1,))
TN = ((0,), (0,))

TILE = 12 * D
B_WD, B_WG, B_WU = 0, 4 * D, 8 * D
B_WO = 3 * TILE
EARLY = 24576
KV_ROWS = 2 * KV * HEAD
LATE1, LATE2 = 3072, 2048
B_Q1 = EARLY
B_K1 = B_Q1 + 3 * D
B_Q2 = EARLY + LATE1
B_K2 = B_Q2 + 2 * D
TOTAL = EARLY + LATE1 + LATE2
ORDERS = (("x", "y", "z"), ("y", "z", "x"), ("z", "x", "y"))
LATE_ORDERS = (("x", "z", "y"), ("z", "x", "y"))


def dot(a, b, dims=NN):
    return lax.dot_general(a, b, (dims, ((), ())), preferred_element_type=F32)


def position():
    s = lax.axis_index("seq")
    r = lax.axis_index("rows")
    return s // 2, s % 2, r // 4, r % 4


def device(y, c, z, x):
    return (y * 2 + c, z * 4 + x)


def mul(offset, size):
    return pl.multiple_of(offset, size)


class Reduction:
    def __init__(self, base, part, orders, grads, landings, sems):
        self.base, self.part, self.grads = base, part, grads
        self.slots = range(len(orders))
        self.landings = landings
        self.send, self.recv, self.pair_s, self.pair_r, self.free = sems
        self.y, self.c, self.z, self.x = position()
        y, z, x = self.y, self.z, self.x
        where = {"x": x, "y": y, "z": z}
        self.orders = orders
        self.index = [[where[a] for a in order] for order in orders]
        self.sizes = (part, part // 4, part // 16)

    def peer(self, axis, index):
        at = {"x": self.x, "y": self.y, "z": self.z}
        at[axis] = index
        return device(at["y"], self.c, at["z"], at["x"])

    def start_of(self, slot, level, core=None):
        core = self.c if core is None else core
        at = self.base + (2 * slot + core) * self.part
        for k in range(level):
            at = at + self.index[slot][k] * self.sizes[k + 1]
        return at

    def within(self, slot, level):
        return self.start_of(slot, level) - self.start_of(slot, 0)

    def rows(self, ref, start, size):
        return ref.at[pl.ds(mul(start, 16), size)]

    def remote(self, source, target, send, recv, slot, axis, index):
        if axis == "core":
            where = device(self.y, 1 - self.c, self.z, self.x)
        else:
            where = self.peer(axis, index)
        return pltpu.make_async_remote_copy(
            src_ref=source, dst_ref=target, send_sem=send, recv_sem=recv, device_id=where, device_id_type=MESH
        )

    def pair_copy(self, slot):
        rows = self.rows(self.grads, self.start_of(slot, 0, 1 - self.c), self.part)
        return self.remote(rows, self.landings[0].at[slot], self.pair_s.at[slot], self.pair_r.at[slot], slot, "core", 0)

    def pair_start(self):
        for slot in self.slots:
            self.pair_copy(slot).start()

    def pair_finish(self):
        step = min(256, self.part)
        land = self.landings[0]
        for slot in self.slots:
            self.pair_copy(slot).wait()
            at = self.start_of(slot, 0)

            def add(k, carry, slot=slot, at=at):
                here = pl.ds(mul(at + k * step, 16), step)
                there = pl.ds(mul(k * step, 16), step)
                both = self.grads[here, :].astype(F32) + land[slot, there, :].astype(F32)
                land[slot, there, :] = both.astype(BF)
                return carry

            lax.fori_loop(0, self.part // step, add, 0)
        where = device(self.y, 1 - self.c, self.z, self.x)
        pl.semaphore_signal(self.free, inc=1, device_id=where, device_id_type=MESH)

    def counted(self, ref, level, slot):
        axis = self.orders[slot][level % 3]
        index = (self.index[slot][level % 3] + 1) % 4
        return self.remote(ref, ref, self.send.at[level, slot], self.recv.at[level, slot], slot, axis, index)

    def scatter_copy(self, slot, level, d):
        index = (self.index[slot][level] + d) % 4
        size = self.sizes[level + 1]
        return self.remote(
            self.rows(self.landings[0].at[slot], self.within(slot, level) + index * size, size),
            self.landings[level + 1].at[slot, d - 1],
            self.send.at[level, slot],
            self.recv.at[level, slot],
            slot, self.orders[slot][level], index,
        )

    def scatter_start(self, level):
        for d in (2, 1, 3):
            for slot in self.slots:
                self.scatter_copy(slot, level, d).start()

    def scatter_finish(self, level):
        size = self.sizes[level + 1]
        step = next(k for k in (128, 160, size) if size % k == 0)
        land = self.landings[level + 1]
        for slot in self.slots:
            self.counted(land.at[slot], level, slot).wait()
            at = self.within(slot, level + 1)
            work = self.landings[0].at[slot]

            def add(k, carry, slot=slot, at=at, work=work):
                here = pl.ds(mul(at + k * step, 16), step)
                there = pl.ds(mul(k * step, 16), step)
                total = work[here, :].astype(F32)
                for d in range(3):
                    total = total + land[slot, d, there, :].astype(F32)
                work[here, :] = total.astype(BF)
                return carry

            lax.fori_loop(0, size // step, add, 0)

    def swap_copy(self, slot, d):
        mine = self.index[slot][2]
        return self.remote(
            self.rows(self.landings[0].at[slot], self.within(slot, 2), self.sizes[2]),
            self.landings[3].at[slot, mine], self.send.at[2, slot], self.recv.at[2, slot],
            slot, self.orders[slot][2], (mine + d) % 4,
        )

    def swap_start(self):
        for d in (2, 1, 3):
            for slot in self.slots:
                self.swap_copy(slot, d).start()
        for slot in self.slots:
            at = pl.ds(mul(self.within(slot, 2), 16), self.sizes[2])
            self.landings[3][slot, self.index[slot][2]] = self.landings[0][slot, at, :]

    def swap_finish(self):
        land = self.landings[3]
        for slot in self.slots:
            self.counted(land.at[slot, pl.ds(0, 3)], 2, slot).wait()
            total = land[slot, 0].astype(F32)
            for k in range(1, 4):
                total = total + land[slot, k].astype(F32)
            self.grads[pl.ds(mul(self.start_of(slot, 2), 16), self.sizes[2]), :] = total.astype(BF)

    def gather_copy(self, slot, level, d):
        mine = self.index[slot][level]
        rows = self.rows(self.grads, self.start_of(slot, level + 1), self.sizes[level + 1])
        return self.remote(
            rows, rows, self.send.at[3 + level, slot], self.recv.at[3 + level, slot],
            slot, self.orders[slot][level], (mine + d) % 4,
        )

    def gather_piece(self, d):
        for slot in self.slots:
            self.gather_copy(slot, 0, d).start()

    def gather_start(self, level):
        for d in (2, 1, 3):
            for slot in self.slots:
                self.gather_copy(slot, level, d).start()

    def gather_finish(self, level):
        for slot in self.slots:
            self.gather_wait(slot, level)

    def gather_wait(self, slot, level):
        rows = self.rows(self.grads, self.start_of(slot, level), 3 * self.sizes[level + 1])
        self.counted(rows, 3 + level, slot).wait()

    def share_copy(self, slot, core):
        rows = self.rows(self.grads, self.start_of(slot, 0, core), self.part)
        n = len(self.slots)
        return self.remote(rows, rows, self.pair_s.at[n + slot], self.pair_r.at[n + slot], slot, "core", 0)

    def share(self):
        pl.semaphore_wait(self.free, 1)
        for slot in self.slots:
            self.gather_wait(slot, 0)
            self.share_copy(slot, self.c).start()

    def share_finish(self):
        for slot in self.slots:
            self.share_copy(slot, self.c).wait_send()
            self.share_copy(slot, 1 - self.c).wait_recv()


def step_kernel(
    x_in, cot_in, docs, gain_a, gain_m, wq_h, wk_h, wv_h, wo_h, wg_h, wu_h, wd_h,
    out, in_grad, grads,
    wq, wkv, wo, wg, wu, wd,
    x_land, c_land, gain_at, gain_mt, cos_t, sin_t, bias_f, bias_d, big,
    state, after, n_a, n_m, mix, qz, kvt, kvn, lse, root_a, root_m, gate, up,
    grad, d_oz, delta, dkv, dqkv, dkv_out, dkv_in, gg_a, gg_m, hid_keep, g_keep, d_keep,
    a0, a1, a2, a3, b0, b1, b2, b3, l0, l1, l2, l3, m0, m1, m2, m3,
    w_sem, x_send, x_recv, c_send, c_recv, o_send, o_recv, i_send, i_recv, kv_send, kv_recv, dkv_send, dkv_recv,
    a_s, a_r, a_ps, a_pr, a_f, b_s, b_r, b_ps, b_pr, b_f, l_s, l_r, l_ps, l_pr, l_f, m_s, m_r, m_ps, m_pr, m_f,
):
    y, c, z, x = position()
    me = y * 2 + c
    my_slot = (me + 2) % 4
    to_core = ((me + 2) % 8) // 4
    chunk_a = 3 - 2 * c
    chunk_b = 2 * c

    barrier = pltpu.get_barrier_semaphore()
    for k in range(1, 8):
        pl.semaphore_signal(barrier, inc=1, device_id=((me + k) % 8, z * 4 + x), device_id_type=MESH)
    for k in range(1, 4):
        pl.semaphore_signal(barrier, inc=1, device_id=device(y, c, (z + k) % 4, x), device_id_type=MESH)
        pl.semaphore_signal(barrier, inc=1, device_id=device(y, c, z, (x + k) % 4), device_id_type=MESH)
    weight_pairs = [(wq_h, wq), (wo_h, wo), (wg_h, wg), (wu_h, wu), (wd_h, wd)]
    for g in range(KV):
        for k, source in enumerate((wk_h, wv_h)):
            pair = (source.at[pl.ds(g * HEAD, HEAD)], wkv.at[pl.ds((2 * g + k) * HEAD, HEAD)])
            weight_pairs.append(pair)
    loads = [pltpu.make_async_copy(a, b, w_sem.at[k]) for k, (a, b) in enumerate(weight_pairs)]
    pl.semaphore_wait(barrier, 13)

    def spread(source, land, send, recv, k):
        r = (y + k) % 4
        target = r * 2 + to_core
        remote = pltpu.make_async_remote_copy(
            src_ref=source.at[r], dst_ref=land.at[my_slot], send_sem=send.at[k], recv_sem=recv.at[my_slot],
            device_id=(target, z * 4 + x), device_id_type=MESH,
        )
        local = pltpu.make_async_copy(source.at[r], land.at[my_slot], send.at[k])
        return target == me, remote, local

    def spread_start(source, land, send, recv):
        for k in (2, 1, 3, 0):
            own, remote, local = spread(source, land, send, recv, k)
            pl.when(own)(local.start)
            pl.when(jnp.logical_not(own))(remote.start)

    def spread_send_wait(source, land, send, recv):
        for k in range(4):
            own, remote, local = spread(source, land, send, recv, k)
            pl.when(own)(local.wait)
            pl.when(jnp.logical_not(own))(remote.wait_send)

    def spread_recv_wait(source, land, send, recv):
        for slot in range(4):
            home = (slot + 6 + 4 * c) % 8
            landed = pltpu.make_async_remote_copy(
                src_ref=source.at[0], dst_ref=land.at[slot], send_sem=send.at[0], recv_sem=recv.at[slot],
                device_id=(home, z * 4 + x), device_id_type=MESH,
            )
            pl.when(home != me)(landed.wait_recv)

    def home_copy(source, result, send, recv, slot):
        home = (slot + 6 + 4 * c) % 8
        remote = pltpu.make_async_remote_copy(
            src_ref=source.at[slot], dst_ref=result.at[y], send_sem=send.at[slot], recv_sem=recv.at[y],
            device_id=(home, z * 4 + x), device_id_type=MESH,
        )
        local = pltpu.make_async_copy(source.at[slot], result.at[y], send.at[slot])
        return home == me, remote, local

    def home_start(source, result, send, recv, slot):
        own, remote, local = home_copy(source, result, send, recv, slot)
        pl.when(own)(local.start)
        pl.when(jnp.logical_not(own))(remote.start)

    def home_wait(source, result, send, recv):
        for slot in range(4):
            own, remote, local = home_copy(source, result, send, recv, slot)
            pl.when(own)(local.wait)
            pl.when(jnp.logical_not(own))(remote.wait_send)
        for r in range(4):
            origin = r * 2 + to_core
            landed = pltpu.make_async_remote_copy(
                src_ref=source.at[0], dst_ref=result.at[r], send_sem=send.at[0], recv_sem=recv.at[r],
                device_id=(origin, z * 4 + x), device_id_type=MESH,
            )
            pl.when(origin != me)(landed.wait_recv)

    spread_start(x_in, x_land, x_send, x_recv)
    for load in loads:
        load.start()

    end0 = docs[y, 0]
    end1 = end0 + docs[y, 1]
    column = lax.broadcasted_iota(jnp.int32, (1, TOK), 1)
    token = jnp.where(column < CH, column + chunk_a * CH, column - CH + chunk_b * CH)
    first = jnp.where(token < end0, 0, jnp.where(token < end1, end0, end1))
    place = (token - first).astype(F32)
    half = lax.broadcasted_iota(jnp.int32, (HEAD // 2, TOK), 0).astype(F32)
    angles = place * jnp.exp(half * (-2.0 / HEAD * 9.210340371976184))
    cos_t[...] = jnp.cos(angles)
    sin_t[...] = jnp.sin(angles)
    for n, chunk in enumerate((chunk_a, chunk_b)):
        cols = slice(n * CH, n * CH + CH)
        fi, tk = first[:, cols], token[:, cols]
        key = lax.broadcasted_iota(jnp.int32, (LOC, CH), 0)
        bias_f[n] = jnp.where(key >= fi, 0.0, NEG).astype(F32)
        key = lax.broadcasted_iota(jnp.int32, (CH, CH), 0) + chunk * CH
        bias_d[n] = jnp.where((key >= fi) & (key <= tk), 0.0, NEG).astype(F32)
        big[n] = jnp.broadcast_to(jnp.where(fi > LOC, -NEG, 0.0).astype(F32), (8, CH))
    gain_at[...] = jnp.broadcast_to(gain_a[...].reshape(1, D), (128, D)).T
    gain_mt[...] = jnp.broadcast_to(gain_m[...].reshape(1, D), (128, D)).T
    gg_a[...] = jnp.zeros(gg_a.shape, F32)
    gg_m[...] = jnp.zeros(gg_m.shape, F32)
    for app in range(2):
        qz[app, :, HEAD:, :] = jnp.zeros((KV, HEAD, 6 * CH), BF)
        kvt[app, :, 2 * HEAD :, :] = jnp.ones((KV, 16, ROW), BF)
    d_oz[:, :HEAD, :] = jnp.zeros((KV, HEAD, 6 * CH), BF)
    grads[pl.ds(B_WO + 4 * D, D), :] = jnp.zeros((D, 128), BF)
    grads[pl.ds(B_WO + 5 * D, EARLY - B_WO - 5 * D), :] = jnp.zeros((EARLY - B_WO - 5 * D, 128), BF)
    for start, end in ((B_K1 + 4 * 256, EARLY + LATE1), (B_K2 + 4 * 128, TOTAL)):
        grads[pl.ds(start, end - start), :] = jnp.zeros((end - start, 128), BF)

    def wide(gain):
        return jnp.concatenate([gain[...]] * 4, axis=1)

    def norm(values, gain, roots, app):
        root = lax.rsqrt(jnp.mean(values * values, axis=0, keepdims=True) + EPS)
        roots[app] = jnp.broadcast_to(root, (8, TOK))
        return (values * root * wide(gain)).astype(BF)

    def turn(a, b, sign):
        cs, sn = cos_t[...], sin_t[...]
        if sign > 0:
            return a * cs - b * sn, b * cs + a * sn
        return a * cs + b * sn, b * cs - a * sn

    def kv_copy(app, n):
        chunk = chunk_a if n == 0 else chunk_b
        span = kvt.at[app, :, pl.ds(0, 2 * HEAD), pl.ds(mul(chunk * CH, CH), CH)]
        return pltpu.make_async_remote_copy(
            src_ref=span, dst_ref=span, send_sem=kv_send.at[app, n], recv_sem=kv_recv.at[app, n],
            device_id=device(y, 1 - c, z, x), device_id_type=MESH,
        )

    def kv_arrival(app, n):
        chunk = 3 - 2 * (1 - c) if n == 0 else 2 * (1 - c)
        span = kvt.at[app, :, pl.ds(0, 2 * HEAD), pl.ds(mul(chunk * CH, CH), CH)]
        return pltpu.make_async_remote_copy(
            src_ref=span, dst_ref=span, send_sem=kv_send.at[app, n], recv_sem=kv_recv.at[app, n],
            device_id=device(y, 1 - c, z, x), device_id_type=MESH,
        )

    plans = (((0, 3), (1, 0)), ((0, 1), (1, 2)))

    def softmax(s, n, chunk):
        nk = (chunk + 1) * CH
        tail = s[nk - CH :] + bias_d[n]
        top = jnp.max(tail, axis=0, keepdims=True)
        if chunk == 0:
            return top, jnp.exp(tail - top).astype(BF)
        lead = s[:LOC] + bias_f[n]
        shut = big[n][0:1]
        middle = s[LOC : nk - CH]
        top = jnp.maximum(top, jnp.max(lead, axis=0, keepdims=True))
        top = jnp.maximum(top, jnp.max(middle, axis=0, keepdims=True) - shut)
        low = [jnp.exp(lead - top), jnp.exp(middle - (top + shut)), jnp.exp(tail - top)]
        return top, jnp.concatenate([v.astype(BF) for v in low], axis=0)

    def attend(app, plan):
        def group(g, carry):
            scores = []
            for n, chunk in plan:
                nk = (chunk + 1) * CH
                scores.append(dot(kvn[app, g, :nk, :], qz[app, g, :, n * 768 : n * 768 + 768]))
            for (n, chunk), s in zip(plan, scores):
                nk = (chunk + 1) * CH
                for j in range(3):
                    top, low = softmax(s[:, j * CH : j * CH + CH], n, chunk)
                    mixed = dot(kvt[app, g, HEAD:, :nk], low)
                    total_w = mixed[HEAD : HEAD + 1]
                    rows = pl.ds(mul(g * 192 + j * HEAD, HEAD), HEAD)
                    mix[app, rows, n * CH : n * CH + CH] = (mixed[:HEAD] * (1.0 / total_w)).astype(BF)
                    at = n * 768 + j * CH
                    lse[app, g, :, at : at + CH] = jnp.broadcast_to(top + jnp.log(total_w), (8, CH))
            return carry

        lax.fori_loop(0, KV, group, 0)

    def forward(app):
        values = state[app]
        low = norm(values, gain_at, root_a, app)
        n_a[app] = low
        if app == 0:
            for load in loads[5:]:
                load.wait()
        raw = dot(wkv[...], low)
        for g in range(KV):
            a, b = turn(raw[g * 128 : g * 128 + 32], raw[g * 128 + 32 : g * 128 + 64], 1)
            packed = jnp.concatenate([a, b, raw[g * 128 + 64 : g * 128 + 128]], axis=0).astype(BF)
            for n, chunk in enumerate((chunk_a, chunk_b)):
                kvt[app, g, : 2 * HEAD, pl.ds(mul(chunk * CH, CH), CH)] = packed[:, n * CH : n * CH + CH]
        kv_copy(app, 0).start()
        kv_copy(app, 1).start()
        for n, chunk in enumerate((chunk_a, chunk_b)):
            for g in range(KV):
                part = kvt[app, g, : 2 * HEAD, pl.ds(mul(chunk * CH, CH), CH)]
                kvn[app, g, pl.ds(mul(chunk * CH, CH), CH), :] = part.T
        if app == 0:
            loads[0].wait()
        query_raw = dot(wq[...], low, TN)
        for h in range(HEADS):
            g, j = h // 3, h % 3
            a, b = turn(query_raw[h * 64 : h * 64 + 32], query_raw[h * 64 + 32 : h * 64 + 64], 1)
            both = (jnp.concatenate([a, b], axis=0) * 0.125).astype(BF)
            for n in range(2):
                at = n * 768 + j * CH
                qz[app, g, :HEAD, at : at + CH] = both[:, n * CH : n * CH + CH]
        for n in range(2):
            kv_copy(app, n).wait_send()
            kv_arrival(app, n).wait_recv()
            chunk = 3 - 2 * (1 - c) if n == 0 else 2 * (1 - c)
            for g in range(KV):
                part = kvt[app, g, : 2 * HEAD, pl.ds(mul(chunk * CH, CH), CH)]
                kvn[app, g, pl.ds(mul(chunk * CH, CH), CH), :] = part.T
        pl.when(c == 0)(lambda: attend(app, plans[0]))
        pl.when(c == 1)(lambda: attend(app, plans[1]))
        if app == 0:
            loads[1].wait()
        att = state[app] + dot(wo[...], mix[app], TN)
        after[app] = att
        low = norm(att, gain_mt, root_m, app)
        n_m[app] = low
        if app == 0:
            for load in loads[2:5]:
                load.wait()
        result = att
        for k in range(3):
            span = slice(k * 512, k * 512 + 512)
            pre = dot(wg[:, span], low, TN)
            pre_up = dot(wu[:, span], low, TN)
            gate[app, span, :] = pre.astype(BF)
            up[app, span, :] = pre_up.astype(BF)
            hidden = (pre * (1.0 / (1.0 + jnp.exp(-pre))) * pre_up).astype(BF)
            result = result + dot(wd[:, span], hidden)
        return result

    def put(base, height, value, add=False):
        width = value.shape[1]
        for j in range((width + 127) // 128):
            lanes = min(128, width - j * 128)
            here = pl.ds(base + j * height, height)
            part = value[:, j * 128 : j * 128 + lanes]
            if add:
                part = part + grads[here, :lanes].astype(F32)
            grads[here, :lanes] = part.astype(BF)

    def fold(value):
        return value[:, :128] + value[:, 128:256] + value[:, 256:384] + value[:, 384:]

    def norm_back(d_normed, values, root, gain, sums):
        scaled = d_normed * wide(gain)
        sums[...] += fold(d_normed * (values * root))
        mean = jnp.mean(scaled * values, axis=0, keepdims=True)
        return root * scaled - values * (root * root * root * mean)

    one = Reduction(0, EARLY // 12, ORDERS, grads, (a0, a1, a2, a3), (a_s, a_r, a_ps, a_pr, a_f))
    two = Reduction(EARLY // 2, EARLY // 12, ORDERS, grads, (b0, b1, b2, b3), (b_s, b_r, b_ps, b_pr, b_f))
    third = Reduction(EARLY, LATE1 // 4, LATE_ORDERS, grads, (l0, l1, l2, l3), (l_s, l_r, l_ps, l_pr, l_f))
    four = Reduction(EARLY + LATE1, LATE2 // 4, LATE_ORDERS, grads, (m0, m1, m2, m3), (m_s, m_r, m_ps, m_pr, m_f))

    def mlp_back(app, after_tile):
        g_low = grad[...].astype(BF)
        if app == 1:
            g_keep[...] = g_low
        d_normed = None
        for k in range(3):
            span = slice(k * 512, k * 512 + 512)
            d_hidden = dot(wd[:, span], g_low, TN).astype(BF).astype(F32)
            pre = gate[app, span, :].astype(F32)
            pre_up = up[app, span, :].astype(F32)
            s = 1.0 / (1.0 + jnp.exp(-pre))
            act = pre * s
            hidden = (act * pre_up).astype(BF)
            d_gate = (d_hidden * pre_up * (s + act * (1.0 - s))).astype(BF)
            d_up = (d_hidden * act).astype(BF)
            if app == 1:
                hid_keep[span, :] = hidden
                gate[1, span, :] = d_gate
                up[1, span, :] = d_up
            else:
                put(k * TILE + B_WD, D, dot(g_low, hidden, NT) + dot(g_keep[...], hid_keep[span, :], NT))
                put(k * TILE + B_WG, D, dot(n_m[0], d_gate, NT) + dot(n_m[1], gate[1, span, :], NT))
                put(k * TILE + B_WU, D, dot(n_m[0], d_up, NT) + dot(n_m[1], up[1, span, :], NT))
            term = dot(wg[:, span], d_gate) + dot(wu[:, span], d_up)
            d_normed = term if d_normed is None else d_normed + term
            after_tile(k)
        grad[...] += norm_back(d_normed, after[app], root_m[app][0:1], gain_mt, gg_m)

    def attend_back(app, plan, between):
        dkv[...] = jnp.zeros(dkv.shape, F32)

        def products(g, n, k):
            cols = slice(n * 768, n * 768 + 768)
            rows = slice(k * CH, k * CH + CH)
            return dot(kvn[app, g, rows, :], qz[app, g, :, cols]), dot(kvn[app, g, rows, :], d_oz[g, :, cols])

        def three(v):
            return jnp.concatenate([v] * 3, axis=1)

        def group(g, carry):
            tiles = [(n, chunk, k) for n, chunk in plan for k in range(chunk + 1)]
            coming = products(g, tiles[0][0], tiles[0][2])
            d_query = None
            for i, (n, chunk, k) in enumerate(tiles):
                s, d_probs = coming
                if i + 1 < len(tiles):
                    coming = products(g, tiles[i + 1][0], tiles[i + 1][2])
                cols = slice(n * 768, n * 768 + 768)
                rows = slice(k * CH, k * CH + CH)
                log_sum = lse[app, g, 0:1, cols]
                if k == chunk:
                    s = s + three(bias_d[n])
                elif k == 0:
                    s = jnp.concatenate([s[:LOC] + three(bias_f[n]), s[LOC:] - three(big[n][0:1])], axis=0)
                else:
                    log_sum = log_sum + three(big[n][0:1])
                probs = jnp.exp(s - log_sum)
                d_score = (probs * (d_probs - delta[g, 0:1, cols])).astype(BF)
                low = probs.astype(BF)
                term = dot(kvt[app, g, :HEAD, rows], d_score)
                d_query = term if k == 0 else d_query + term
                dkv[g, rows, :] += dot(d_score, qz[app, g, :, cols], NT) + dot(low, d_oz[g, :, cols], NT)
                if k < chunk:
                    continue
                d_query = d_query * 0.125
                at = slice(n * CH, n * CH + CH)
                cs, sn = cos_t[:, at], sin_t[:, at]
                for j in range(3):
                    head = pl.ds(mul(g * 192 + j * HEAD, HEAD), HEAD)
                    a, b = d_query[:32, j * CH : j * CH + CH], d_query[32:, j * CH : j * CH + CH]
                    both = jnp.concatenate([a * cs + b * sn, b * cs - a * sn], axis=0)
                    dqkv[app, head, at] = both.astype(BF)
            for n in range(2):
                chunk = 3 - 2 * (1 - c) if n == 0 else 2 * (1 - c)
                dkv_out[g, n * CH : n * CH + CH, :] = dkv[g, pl.ds(mul(chunk * CH, CH), CH), :].astype(BF)
            dkv_copy(app, g).start()
            between(g)
            return carry

        lax.fori_loop(0, KV, group, 0)

    def dkv_copy(app, g):
        return pltpu.make_async_remote_copy(
            src_ref=dkv_out.at[g], dst_ref=dkv_in.at[app, g], send_sem=dkv_send.at[app, g],
            recv_sem=dkv_recv.at[app, g], device_id=device(y, 1 - c, z, x), device_id_type=MESH,
        )

    def attn_back(app, before, before_groups, between, after_query):
        g_low = grad[...].astype(BF)
        if app == 1:
            d_keep[...] = g_low
        else:
            put(B_WO, D, dot(mix[0], g_low, NT) + dot(mix[1], d_keep[...], NT))
        before()
        d_mixed = dot(wo[...], g_low)
        for h in range(HEADS):
            g, j = h // 3, h % 3
            dm = d_mixed[h * 64 : h * 64 + 64].astype(BF)
            dl = jnp.sum(dm.astype(F32) * mix[app, h * 64 : h * 64 + 64, :].astype(F32), axis=0, keepdims=True)
            for n in range(2):
                at = n * 768 + j * CH
                d_oz[g, HEAD:, at : at + CH] = dm[:, n * CH : n * CH + CH]
                delta[g, :, at : at + CH] = jnp.broadcast_to(dl[:, n * CH : n * CH + CH], (8, CH))
        before_groups()
        if app == 0:
            for span in (0, 1):
                put_late(1, span, False)
        pl.when(c == 0)(lambda: attend_back(app, plans[0], between))
        pl.when(c == 1)(lambda: attend_back(app, plans[1], between))
        dq = dqkv[app, :D, :]
        if app == 0:
            put_late_query(0, 1, True)
        d_normed = dot(wq[...], dq)
        after_query()
        if app == 0:
            join_keys(0, (2,))
            put_late_keys(0, 1, True)
        else:
            join_keys(1, range(KV))
        d_normed = d_normed + dot(wkv[...], dqkv[app, D:, :], TN)
        grad[...] += norm_back(d_normed, state[app], root_a[app][0:1], gain_at, gg_a)

    def join_keys(app, groups):
        for g in groups:
            dkv_copy(app, g).wait()
            parts = []
            for n, chunk in enumerate((chunk_a, chunk_b)):
                own = dkv[g, pl.ds(mul(chunk * CH, CH), CH), :]
                other = dkv_in[app, g, n * CH : n * CH + CH, :].astype(F32)
                parts.append((own + other).T)
            both = jnp.concatenate(parts, axis=1)
            a, b = turn(both[:32], both[32:64], -1)
            at = D + g * 2 * HEAD
            dqkv[app, at : at + 2 * HEAD, :] = jnp.concatenate([a, b, both[64:]], axis=0).astype(BF)

    def put_late_query(app, span, add):
        base, start, end = ((B_Q1, 0, 384), (B_Q2, 384, D))[span]
        put(base, D, dot(n_a[app], dqkv[app, start:end, :], NT), add)

    def put_late_keys(app, span, add):
        base, start, end = ((B_K1, D, D + 256), (B_K2, D + 256, D + KV_ROWS))[span]
        put(base, end - start, dot(dqkv[app, start:end, :], n_a[app], NT), add)

    def put_late(app, span, add):
        put_late_query(app, span, add)
        put_late_keys(app, span, add)

    def nothing(*unused):
        return None

    spread_send_wait(x_in, x_land, x_send, x_recv)
    spread_recv_wait(x_in, x_land, x_send, x_recv)
    spread_start(cot_in, c_land, c_send, c_recv)
    for slot in range(4):
        state[0, :, slot * LOC : slot * LOC + LOC] = x_land[slot].astype(F32)
    state[1] = forward(0)
    final = forward(1)
    for slot in range(4):
        x_land[slot] = final[:, slot * LOC : slot * LOC + LOC].astype(BF)
    for slot in range(4):
        home_start(x_land, out, o_send, o_recv, slot)
    spread_send_wait(cot_in, c_land, c_send, c_recv)
    spread_recv_wait(cot_in, c_land, c_send, c_recv)
    for slot in range(4):
        grad[:, slot * LOC : slot * LOC + LOC] = c_land[slot].astype(F32)

    mlp_back(1, nothing)
    attn_back(1, nothing, nothing, nothing, nothing)
    def after_tile(k):
        if k == 1:
            one.pair_start()
        if k == 2:
            one.pair_finish()
            one.scatter_start(0)

    mlp_back(0, after_tile)

    def before_groups():
        two.pair_finish()
        two.scatter_start(0)

    def between(g):
        @pl.when(g == 0)
        def _():
            one.scatter_finish(0)
            one.scatter_start(1)

        @pl.when(g == 1)
        def _():
            one.scatter_finish(1)
            one.swap_start()
            two.scatter_finish(0)
            two.scatter_start(1)
            join_keys(0, (0, 1))
            put_late(0, 0, True)
            third.pair_start()

        @pl.when(g == 2)
        def _():
            one.swap_finish()
            one.gather_start(1)
            third.pair_finish()
            third.scatter_start(0)

    def after_query():
        two.scatter_finish(1)
        two.swap_start()

    attn_back(0, two.pair_start, before_groups, between, after_query)
    lane = lax.broadcasted_iota(jnp.int32, (D, 64), 1)
    sum_a = jnp.sum(gg_a[...], axis=1, keepdims=True)
    sum_m = jnp.sum(gg_m[...], axis=1, keepdims=True)
    columns = jnp.where(lane == 0, sum_a, jnp.where(lane == 1, sum_m, 0.0))
    grads[pl.ds(B_Q2 + D, D), 64:] = columns.astype(BF)
    four.pair_start()
    for slot in range(4):
        c_land[slot] = grad[:, slot * LOC : slot * LOC + LOC].astype(BF)
    for slot in range(4):
        home_start(c_land, in_grad, i_send, i_recv, slot)
    one.gather_finish(1)
    one.gather_piece(1)
    four.pair_finish()
    four.scatter_start(0)
    two.swap_finish()
    two.gather_start(1)
    one.gather_piece(3)
    four.scatter_finish(0)
    four.scatter_start(1)
    third.scatter_finish(0)
    third.scatter_start(1)
    two.gather_finish(1)
    one.gather_piece(2)
    two.gather_piece(1)
    four.scatter_finish(1)
    four.swap_start()
    third.scatter_finish(1)
    third.swap_start()
    two.gather_piece(3)
    four.swap_finish()
    four.gather_start(1)
    third.swap_finish()
    third.gather_start(1)
    two.gather_piece(2)
    one.share()
    four.gather_finish(1)
    four.gather_start(0)
    third.gather_finish(1)
    third.gather_start(0)
    two.share()
    four.share()
    third.share()
    one.share_finish()
    two.share_finish()
    four.share_finish()
    third.share_finish()
    home_wait(x_land, out, o_send, o_recv)
    home_wait(c_land, in_grad, i_send, i_recv)


def train_step(inputs, docs, gain_a, wq, wk, wv, wo, gain_m, wg, wu, wd, cot):
    hbm = pl.BlockSpec(memory_space=pl.ANY)
    vmem = pl.BlockSpec(memory_space=pltpu.VMEM)
    smem = pl.BlockSpec(memory_space=pltpu.SMEM)
    dma = pltpu.SemaphoreType.DMA
    v = pltpu.VMEM
    scratch = [
        v((D, D), BF), v((KV_ROWS, D), BF), v((D, D), BF), v((D, FF), BF), v((D, FF), BF), v((D, FF), BF),
        v((4, D, LOC), BF), v((4, D, LOC), BF), v((D, 128), F32), v((D, 128), F32),
        v((32, TOK), F32), v((32, TOK), F32), v((2, LOC, CH), F32), v((2, CH, CH), F32), v((2, 8, CH), F32),
        v((2, D, TOK), F32), v((2, D, TOK), F32), v((2, D, TOK), BF), v((2, D, TOK), BF), v((2, D, TOK), BF),
        v((2, KV, 128, 6 * CH), BF), v((2, KV, 144, ROW), BF), v((2, KV, ROW, 128), BF), v((2, KV, 8, 6 * CH), F32),
        v((2, 8, TOK), F32), v((2, 8, TOK), F32), v((2, FF, TOK), BF), v((2, FF, TOK), BF),
        v((D, TOK), F32), v((KV, 128, 6 * CH), BF), v((KV, 8, 6 * CH), F32), v((KV, ROW, 128), F32),
        v((2, 960, TOK), BF), v((KV, TOK, 128), BF), v((2, KV, TOK, 128), BF), v((D, 128), F32), v((D, 128), F32),
        v((FF, TOK), BF), v((D, TOK), BF), v((D, TOK), BF),
    ]
    for n, part in ((3, EARLY // 12), (3, EARLY // 12), (2, LATE1 // 4), (2, LATE2 // 4)):
        scratch += [v((n, part, 128), BF), v((n, 3, part // 4, 128), BF), v((n, 3, part // 16, 128), BF)]
        scratch += [v((n, 4, part // 16, 128), BF)]
    scratch += [dma((11,))] + [dma((4,))] * 8 + [dma((2, 2))] * 2 + [dma((2, KV))] * 2
    for n in (3, 3, 2, 2):
        scratch += [dma((5, n)), dma((5, n)), dma((2 * n,)), dma((2 * n,)), pltpu.SemaphoreType.REGULAR]
    out, in_grad, total = pl.pallas_call(
        step_kernel,
        out_shape=(
            jax.ShapeDtypeStruct((4, D, LOC), BF),
            jax.ShapeDtypeStruct((4, D, LOC), BF),
            pltpu.VMEM((TOTAL, 128), BF),
        ),
        in_specs=[hbm, hbm, smem, vmem, vmem] + [hbm] * 7,
        out_specs=(hbm, hbm, vmem),
        scratch_shapes=scratch,
        compiler_params=pltpu.CompilerParams(
            collective_id=0, has_side_effects=True, vmem_limit_bytes=55 * 2**20
        ),
        name="train_step",
    )(inputs, cot, docs, gain_a, gain_m, wq, wk, wv, wo, wg, wu, wd)
    return out, in_grad, total


def unpack_kernel(total, out, in_grad, out_c, in_grad_c, ga, gq, gk, gv, go, gm, gg, gu, gd, state, sq, sk, sv, so, sg, su, sd, in_sem, out_sem):
    loads = [pltpu.make_async_copy(a, state.at[k], in_sem.at[k]) for k, a in enumerate((out, in_grad))]
    for load in loads:
        load.start()
    stores = []

    def store(source, target):
        stores.append(pltpu.make_async_copy(source, target, out_sem.at[len(stores)]))
        stores[-1].start()

    def panels(base, height, width, target):
        for j in range((width + 127) // 128):
            lanes = min(128, width - j * 128)
            target[:, j * 128 : j * 128 + lanes] = total[pl.ds(base + j * height, height), :lanes].astype(F32)

    for k in range(3):
        for base, source, target in ((B_WD, sd, gd), (B_WG, sg, gg), (B_WU, su, gu)):
            span = slice(k * 512, k * 512 + 512)
            panels(k * TILE + base, D, 512, source.at[:, span])
            store(source.at[:, span], target.at[:, span])
    panels(B_WO, D, D, so)
    store(so, go)
    panels(B_Q1, D, 384, sq.at[:, :384])
    panels(B_Q2, D, 192, sq.at[:, 384:])
    store(sq, gq)
    for g, base, height in ((0, B_K1, 256), (1, B_K1 + 128, 256), (2, B_K2, 128)):
        for k, target in enumerate((sk, sv)):
            for j in range(5):
                lanes = min(128, D - j * 128)
                rows = pl.ds(base + j * height + k * HEAD, HEAD)
                target[g * HEAD : g * HEAD + HEAD, j * 128 : j * 128 + lanes] = total[rows, :lanes].astype(F32)
    store(sk, gk)
    store(sv, gv)
    gains = total[pl.ds(B_Q2 + D, D), :].astype(F32).T
    ga[...] = gains[64]
    gm[...] = gains[65]
    for k, target in enumerate((out_c, in_grad_c)):
        loads[k].wait()
        store(state.at[k], target)
    for copy in stores:
        copy.wait()


def unpack(total, out, in_grad):
    hbm = pl.BlockSpec(memory_space=pl.ANY)
    vmem = pl.BlockSpec(memory_space=pltpu.VMEM)
    shape = jax.ShapeDtypeStruct
    v = pltpu.VMEM
    result = pl.pallas_call(
        unpack_kernel,
        out_shape=(
            shape(out.shape, BF), shape(out.shape, BF),
            shape((D,), F32), shape((D, D), F32), shape((192, D), F32), shape((192, D), F32), shape((D, D), F32),
            shape((D,), F32), shape((D, FF), F32), shape((D, FF), F32), shape((D, FF), F32),
        ),
        in_specs=[vmem, hbm, hbm],
        out_specs=(hbm, hbm, vmem, hbm, hbm, hbm, hbm, vmem, hbm, hbm, hbm),
        scratch_shapes=[
            v((2,) + out.shape, BF), v((D, D), F32), v((192, D), F32), v((192, D), F32), v((D, D), F32),
            v((D, FF), F32), v((D, FF), F32), v((D, FF), F32),
            pltpu.SemaphoreType.DMA((2,)), pltpu.SemaphoreType.DMA((15,)),
        ],
        compiler_params=pltpu.CompilerParams(vmem_limit_bytes=56 * 2**20),
        name="unpack",
    )(pltpu.with_memory_space_constraint(total, pltpu.VMEM), out, in_grad)
    return result


def on_device(inputs, docs, gain_a, wq, wk, wv, wo, gain_m, wg, wu, wd, cot):
    out, in_grad, total = train_step(
        inputs.transpose(0, 2, 1), docs, gain_a, wq, wk.T, wv.T, wo, gain_m, wg, wu, wd.T, cot.transpose(0, 2, 1)
    )
    out, in_grad, ga, gq, gk, gv, go, gm, gg, gu, gd = unpack(total, out, in_grad)
    return out.transpose(0, 2, 1), in_grad.transpose(0, 2, 1), ga, gq, gk.T, gv.T, go, gm, gg, gu, gd.T


def solution(mesh):
    token = P("rows", "seq", None)
    in_specs = (token, P("rows", None)) + (P(),) * 9 + (token,)
    out_specs = (token, token) + (P(),) * 9
    return jax.shard_map(on_device, mesh=mesh, in_specs=in_specs, out_specs=out_specs, check_vma=False)
```

```python
import functools

import jax
import jax.numpy as jnp
from jax import lax
from jax.experimental import pallas as pl
from jax.experimental.pallas import tpu as pltpu
from jax.sharding import PartitionSpec as P

D = 576
HEADS = 9
KV = 3
HEAD = 64
FF = 1536
ROW = 1024
LOC = 128
TOK = 512
CH = 256
EPS = 1e-05
THETA = 10000.0
NEG = -1e30
BF = jnp.bfloat16
F32 = jnp.float32
MESH = pl.DeviceIdType.MESH

NN = ((1,), (0,))
NT = ((1,), (1,))
TN = ((0,), (0,))

TILE = 12 * D
B_WD, B_WG, B_WU = 0, 4 * D, 8 * D
B_WO = 3 * TILE
EARLY = 24576
KV_ROWS = 2 * KV * HEAD
LATE1, LATE2 = 3072, 2048
B_Q1 = EARLY
B_K1 = B_Q1 + 3 * D
B_Q2 = EARLY + LATE1
B_K2 = B_Q2 + 2 * D
TOTAL = EARLY + LATE1 + LATE2
ORDERS = (("x", "y", "z"), ("y", "z", "x"), ("z", "x", "y"))
LATE_ORDERS = (("x", "z", "y"), ("z", "x", "y"))


def dot(a, b, dims=NN):
    return lax.dot_general(a, b, (dims, ((), ())), preferred_element_type=F32)


def position():
    s = lax.axis_index("seq")
    r = lax.axis_index("rows")
    return s // 2, s % 2, r // 4, r % 4


def device(y, c, z, x):
    return (y * 2 + c, z * 4 + x)


def mul(offset, size):
    return pl.multiple_of(offset, size)


class Reduction:
    def __init__(self, base, part, orders, grads, landings, sems):
        self.base, self.part, self.grads = base, part, grads
        self.slots = range(len(orders))
        self.landings = landings
        self.send, self.recv, self.pair_s, self.pair_r, self.free = sems
        self.y, self.c, self.z, self.x = position()
        y, z, x = self.y, self.z, self.x
        where = {"x": x, "y": y, "z": z}
        self.orders = orders
        self.index = [[where[a] for a in order] for order in orders]
        self.sizes = (part, part // 4, part // 16)

    def peer(self, axis, index):
        at = {"x": self.x, "y": self.y, "z": self.z}
        at[axis] = index
        return device(at["y"], self.c, at["z"], at["x"])

    def start_of(self, slot, level, core=None):
        core = self.c if core is None else core
        at = self.base + (2 * slot + core) * self.part
        for k in range(level):
            at = at + self.index[slot][k] * self.sizes[k + 1]
        return at

    def within(self, slot, level):
        return self.start_of(slot, level) - self.start_of(slot, 0)

    def rows(self, ref, start, size):
        return ref.at[pl.ds(mul(start, 16), size)]

    def remote(self, source, target, send, recv, slot, axis, index):
        if axis == "core":
            where = device(self.y, 1 - self.c, self.z, self.x)
        else:
            where = self.peer(axis, index)
        return pltpu.make_async_remote_copy(
            src_ref=source, dst_ref=target, send_sem=send, recv_sem=recv, device_id=where, device_id_type=MESH
        )

    def pair_copy(self, slot):
        rows = self.rows(self.grads, self.start_of(slot, 0, 1 - self.c), self.part)
        return self.remote(rows, self.landings[0].at[slot], self.pair_s.at[slot], self.pair_r.at[slot], slot, "core", 0)

    def pair_start(self, slots=None):
        for slot in self.slots if slots is None else slots:
            self.pair_copy(slot).start()

    def pair_finish(self):
        step = min(256, self.part)
        land = self.landings[0]
        for slot in self.slots:
            self.pair_copy(slot).wait()
            at = self.start_of(slot, 0)

            def add(k, carry, slot=slot, at=at):
                here = pl.ds(mul(at + k * step, 16), step)
                there = pl.ds(mul(k * step, 16), step)
                both = self.grads[here, :].astype(F32) + land[slot, there, :].astype(F32)
                land[slot, there, :] = both.astype(BF)
                return carry

            lax.fori_loop(0, self.part // step, add, 0)
        where = device(self.y, 1 - self.c, self.z, self.x)
        pl.semaphore_signal(self.free, inc=1, device_id=where, device_id_type=MESH)

    def counted(self, ref, level, slot):
        axis = self.orders[slot][level % 3]
        index = (self.index[slot][level % 3] + 1) % 4
        return self.remote(ref, ref, self.send.at[level, slot], self.recv.at[level, slot], slot, axis, index)

    def scatter_copy(self, slot, level, d):
        index = (self.index[slot][level] + d) % 4
        size = self.sizes[level + 1]
        return self.remote(
            self.rows(self.landings[0].at[slot], self.within(slot, level) + index * size, size),
            self.landings[level + 1].at[slot, d - 1],
            self.send.at[level, slot],
            self.recv.at[level, slot],
            slot, self.orders[slot][level], index,
        )

    def scatter_start(self, level):
        for d in (2, 1, 3):
            for slot in self.slots:
                self.scatter_copy(slot, level, d).start()

    def scatter_finish(self, level):
        size = self.sizes[level + 1]
        step = next(k for k in (128, 160, size) if size % k == 0)
        land = self.landings[level + 1]
        for slot in self.slots:
            self.counted(land.at[slot], level, slot).wait()
            at = self.within(slot, level + 1)
            work = self.landings[0].at[slot]

            def add(k, carry, slot=slot, at=at, work=work):
                here = pl.ds(mul(at + k * step, 16), step)
                there = pl.ds(mul(k * step, 16), step)
                total = work[here, :].astype(F32)
                for d in range(3):
                    total = total + land[slot, d, there, :].astype(F32)
                work[here, :] = total.astype(BF)
                return carry

            lax.fori_loop(0, size // step, add, 0)

    def swap_copy(self, slot, d):
        mine = self.index[slot][2]
        return self.remote(
            self.rows(self.landings[0].at[slot], self.within(slot, 2), self.sizes[2]),
            self.landings[3].at[slot, mine], self.send.at[2, slot], self.recv.at[2, slot],
            slot, self.orders[slot][2], (mine + d) % 4,
        )

    def swap_start(self):
        for d in (2, 1, 3):
            for slot in self.slots:
                self.swap_copy(slot, d).start()
        for slot in self.slots:
            at = pl.ds(mul(self.within(slot, 2), 16), self.sizes[2])
            self.landings[3][slot, self.index[slot][2]] = self.landings[0][slot, at, :]

    def swap_finish(self):
        land = self.landings[3]
        for slot in self.slots:
            self.counted(land.at[slot, pl.ds(0, 3)], 2, slot).wait()
            total = land[slot, 0].astype(F32)
            for k in range(1, 4):
                total = total + land[slot, k].astype(F32)
            self.grads[pl.ds(mul(self.start_of(slot, 2), 16), self.sizes[2]), :] = total.astype(BF)

    def gather_copy(self, slot, level, d):
        mine = self.index[slot][level]
        rows = self.rows(self.grads, self.start_of(slot, level + 1), self.sizes[level + 1])
        return self.remote(
            rows, rows, self.send.at[3 + level, slot], self.recv.at[3 + level, slot],
            slot, self.orders[slot][level], (mine + d) % 4,
        )

    def gather_piece(self, d):
        for slot in self.slots:
            self.gather_copy(slot, 0, d).start()

    def gather_start(self, level):
        for d in (2, 1, 3):
            for slot in self.slots:
                self.gather_copy(slot, level, d).start()

    def gather_finish(self, level):
        for slot in self.slots:
            self.gather_wait(slot, level)

    def gather_wait(self, slot, level):
        rows = self.rows(self.grads, self.start_of(slot, level), 3 * self.sizes[level + 1])
        self.counted(rows, 3 + level, slot).wait()

    def share_copy(self, slot, core):
        rows = self.rows(self.grads, self.start_of(slot, 0, core), self.part)
        n = len(self.slots)
        return self.remote(rows, rows, self.pair_s.at[n + slot], self.pair_r.at[n + slot], slot, "core", 0)

    def share(self):
        pl.semaphore_wait(self.free, 1)
        for slot in self.slots:
            self.gather_wait(slot, 0)
            self.share_copy(slot, self.c).start()

    def share_finish(self):
        for slot in self.slots:
            self.share_copy(slot, self.c).wait_send()
            self.share_copy(slot, 1 - self.c).wait_recv()


def step_kernel(
    x_in, cot_in, docs, gain_a, gain_m, wq_h, wk_h, wv_h, wo_h, wg_h, wu_h, wd_h,
    out, in_grad, grads,
    wq, wkv, wo, wg, wu, wd,
    x_land, c_land, gain_at, gain_mt, cos_t, sin_t, bias_f, bias_d, big,
    state, after, n_a, n_m, mix, qz, kvt, kvn, lse, root_a, root_m, gate, up,
    grad, d_oz, delta, dkv, dqkv, dkv_out, dkv_in, gg_a, gg_m, hid_keep, g_keep, d_keep,
    a0, a1, a2, a3, b0, b1, b2, b3, l0, l1, l2, l3, m0, m1, m2, m3,
    w_sem, x_send, x_recv, c_send, c_recv, o_send, o_recv, i_send, i_recv, kv_send, kv_recv, dkv_send, dkv_recv,
    a_s, a_r, a_ps, a_pr, a_f, b_s, b_r, b_ps, b_pr, b_f, l_s, l_r, l_ps, l_pr, l_f, m_s, m_r, m_ps, m_pr, m_f,
):
    y, c, z, x = position()
    me = y * 2 + c
    my_slot = (me + 2) % 4
    to_core = ((me + 2) % 8) // 4
    chunk_a = 3 - 2 * c
    chunk_b = 2 * c

    barrier = pltpu.get_barrier_semaphore()
    for k in range(1, 8):
        pl.semaphore_signal(barrier, inc=1, device_id=((me + k) % 8, z * 4 + x), device_id_type=MESH)
    for k in range(1, 4):
        pl.semaphore_signal(barrier, inc=1, device_id=device(y, c, (z + k) % 4, x), device_id_type=MESH)
        pl.semaphore_signal(barrier, inc=1, device_id=device(y, c, z, (x + k) % 4), device_id_type=MESH)
    weight_pairs = [(wq_h, wq), (wo_h, wo), (wg_h, wg), (wu_h, wu), (wd_h, wd)]
    for g in range(KV):
        for k, source in enumerate((wk_h, wv_h)):
            pair = (source.at[pl.ds(g * HEAD, HEAD)], wkv.at[pl.ds((2 * g + k) * HEAD, HEAD)])
            weight_pairs.append(pair)
    loads = [pltpu.make_async_copy(a, b, w_sem.at[k]) for k, (a, b) in enumerate(weight_pairs)]
    pl.semaphore_wait(barrier, 13)

    def spread(source, land, send, recv, k):
        r = (y + k) % 4
        target = r * 2 + to_core
        remote = pltpu.make_async_remote_copy(
            src_ref=source.at[r], dst_ref=land.at[my_slot], send_sem=send.at[k], recv_sem=recv.at[my_slot],
            device_id=(target, z * 4 + x), device_id_type=MESH,
        )
        local = pltpu.make_async_copy(source.at[r], land.at[my_slot], send.at[k])
        return target == me, remote, local

    def spread_start(source, land, send, recv):
        for k in (2, 1, 3, 0):
            own, remote, local = spread(source, land, send, recv, k)
            pl.when(own)(local.start)
            pl.when(jnp.logical_not(own))(remote.start)

    def spread_send_wait(source, land, send, recv):
        for k in range(4):
            own, remote, local = spread(source, land, send, recv, k)
            pl.when(own)(local.wait)
            pl.when(jnp.logical_not(own))(remote.wait_send)

    def spread_recv_wait(source, land, send, recv):
        for slot in range(4):
            home = (slot + 6 + 4 * c) % 8
            landed = pltpu.make_async_remote_copy(
                src_ref=source.at[0], dst_ref=land.at[slot], send_sem=send.at[0], recv_sem=recv.at[slot],
                device_id=(home, z * 4 + x), device_id_type=MESH,
            )
            pl.when(home != me)(landed.wait_recv)

    def home_copy(source, result, send, recv, slot):
        home = (slot + 6 + 4 * c) % 8
        remote = pltpu.make_async_remote_copy(
            src_ref=source.at[slot], dst_ref=result.at[y], send_sem=send.at[slot], recv_sem=recv.at[y],
            device_id=(home, z * 4 + x), device_id_type=MESH,
        )
        local = pltpu.make_async_copy(source.at[slot], result.at[y], send.at[slot])
        return home == me, remote, local

    def home_start(source, result, send, recv, slot):
        own, remote, local = home_copy(source, result, send, recv, slot)
        pl.when(own)(local.start)
        pl.when(jnp.logical_not(own))(remote.start)

    def home_wait(source, result, send, recv):
        for slot in range(4):
            own, remote, local = home_copy(source, result, send, recv, slot)
            pl.when(own)(local.wait)
            pl.when(jnp.logical_not(own))(remote.wait_send)
        for r in range(4):
            origin = r * 2 + to_core
            landed = pltpu.make_async_remote_copy(
                src_ref=source.at[0], dst_ref=result.at[r], send_sem=send.at[0], recv_sem=recv.at[r],
                device_id=(origin, z * 4 + x), device_id_type=MESH,
            )
            pl.when(origin != me)(landed.wait_recv)

    spread_start(x_in, x_land, x_send, x_recv)
    for load in loads:
        load.start()

    end0 = docs[y, 0]
    end1 = end0 + docs[y, 1]
    column = lax.broadcasted_iota(jnp.int32, (1, TOK), 1)
    token = jnp.where(column < CH, column + chunk_a * CH, column - CH + chunk_b * CH)
    first = jnp.where(token < end0, 0, jnp.where(token < end1, end0, end1))
    place = (token - first).astype(F32)
    half = lax.broadcasted_iota(jnp.int32, (HEAD // 2, TOK), 0).astype(F32)
    angles = place * jnp.exp(half * (-2.0 / HEAD * 9.210340371976184))
    cos_t[...] = jnp.cos(angles)
    sin_t[...] = jnp.sin(angles)
    for n, chunk in enumerate((chunk_a, chunk_b)):
        cols = slice(n * CH, n * CH + CH)
        fi, tk = first[:, cols], token[:, cols]
        key = lax.broadcasted_iota(jnp.int32, (LOC, CH), 0)
        bias_f[n] = jnp.where(key >= fi, 0.0, NEG).astype(F32)
        key = lax.broadcasted_iota(jnp.int32, (CH, CH), 0) + chunk * CH
        bias_d[n] = jnp.where((key >= fi) & (key <= tk), 0.0, NEG).astype(F32)
        big[n] = jnp.broadcast_to(jnp.where(fi > LOC, -NEG, 0.0).astype(F32), (8, CH))
    gain_at[...] = jnp.broadcast_to(gain_a[...].reshape(1, D), (128, D)).T
    gain_mt[...] = jnp.broadcast_to(gain_m[...].reshape(1, D), (128, D)).T
    gg_a[...] = jnp.zeros(gg_a.shape, F32)
    gg_m[...] = jnp.zeros(gg_m.shape, F32)
    for app in range(2):
        qz[app, :, HEAD:, :] = jnp.zeros((KV, HEAD, 6 * CH), BF)
        kvt[app, :, 2 * HEAD :, :] = jnp.ones((KV, 16, ROW), BF)
    d_oz[:, :HEAD, :] = jnp.zeros((KV, HEAD, 6 * CH), BF)
    grads[pl.ds(B_WO + 4 * D, D), :] = jnp.zeros((D, 128), BF)
    grads[pl.ds(B_WO + 5 * D, EARLY - B_WO - 5 * D), :] = jnp.zeros((EARLY - B_WO - 5 * D, 128), BF)
    for start, end in ((B_K1 + 4 * 256, EARLY + LATE1), (B_K2 + 4 * 128, TOTAL)):
        grads[pl.ds(start, end - start), :] = jnp.zeros((end - start, 128), BF)

    def wide(gain):
        return jnp.concatenate([gain[...]] * 4, axis=1)

    def norm(values, gain, roots, app):
        root = lax.rsqrt(jnp.mean(values * values, axis=0, keepdims=True) + EPS)
        roots[app] = jnp.broadcast_to(root, (8, TOK))
        return (values * root * wide(gain)).astype(BF)

    def turn(a, b, sign):
        cs, sn = cos_t[...], sin_t[...]
        if sign > 0:
            return a * cs - b * sn, b * cs + a * sn
        return a * cs + b * sn, b * cs - a * sn

    def kv_copy(app, n):
        chunk = chunk_a if n == 0 else chunk_b
        span = kvt.at[app, :, pl.ds(0, 2 * HEAD), pl.ds(mul(chunk * CH, CH), CH)]
        return pltpu.make_async_remote_copy(
            src_ref=span, dst_ref=span, send_sem=kv_send.at[app, n], recv_sem=kv_recv.at[app, n],
            device_id=device(y, 1 - c, z, x), device_id_type=MESH,
        )

    def kv_arrival(app, n):
        chunk = 3 - 2 * (1 - c) if n == 0 else 2 * (1 - c)
        span = kvt.at[app, :, pl.ds(0, 2 * HEAD), pl.ds(mul(chunk * CH, CH), CH)]
        return pltpu.make_async_remote_copy(
            src_ref=span, dst_ref=span, send_sem=kv_send.at[app, n], recv_sem=kv_recv.at[app, n],
            device_id=device(y, 1 - c, z, x), device_id_type=MESH,
        )

    plans = (((0, 3), (1, 0)), ((0, 1), (1, 2)))

    def softmax(s, n, chunk):
        nk = (chunk + 1) * CH
        tail = s[nk - CH :] + bias_d[n]
        top = jnp.max(tail, axis=0, keepdims=True)
        if chunk == 0:
            return top, jnp.exp(tail - top).astype(BF)
        lead = s[:LOC] + bias_f[n]
        shut = big[n][0:1]
        middle = s[LOC : nk - CH]
        top = jnp.maximum(top, jnp.max(lead, axis=0, keepdims=True))
        top = jnp.maximum(top, jnp.max(middle, axis=0, keepdims=True) - shut)
        low = [jnp.exp(lead - top), jnp.exp(middle - (top + shut)), jnp.exp(tail - top)]
        return top, jnp.concatenate([v.astype(BF) for v in low], axis=0)

    def attend(app, plan):
        def group(g, carry):
            scores = []
            for n, chunk in plan:
                nk = (chunk + 1) * CH
                scores.append(dot(kvn[app, g, :nk, :], qz[app, g, :, n * 768 : n * 768 + 768]))
            for (n, chunk), s in zip(plan, scores):
                nk = (chunk + 1) * CH
                for j in range(3):
                    top, low = softmax(s[:, j * CH : j * CH + CH], n, chunk)
                    mixed = dot(kvt[app, g, HEAD:, :nk], low)
                    total_w = mixed[HEAD : HEAD + 1]
                    rows = pl.ds(mul(g * 192 + j * HEAD, HEAD), HEAD)
                    mix[app, rows, n * CH : n * CH + CH] = (mixed[:HEAD] * (1.0 / total_w)).astype(BF)
                    at = n * 768 + j * CH
                    lse[app, g, :, at : at + CH] = jnp.broadcast_to(top + jnp.log(total_w), (8, CH))
            return carry

        lax.fori_loop(0, KV, group, 0)

    def forward(app):
        values = state[app]
        low = norm(values, gain_at, root_a, app)
        n_a[app] = low
        if app == 0:
            for load in loads[5:]:
                load.wait()
        raw = dot(wkv[...], low)
        for g in range(KV):
            a, b = turn(raw[g * 128 : g * 128 + 32], raw[g * 128 + 32 : g * 128 + 64], 1)
            packed = jnp.concatenate([a, b, raw[g * 128 + 64 : g * 128 + 128]], axis=0).astype(BF)
            for n, chunk in enumerate((chunk_a, chunk_b)):
                kvt[app, g, : 2 * HEAD, pl.ds(mul(chunk * CH, CH), CH)] = packed[:, n * CH : n * CH + CH]
        kv_copy(app, 0).start()
        kv_copy(app, 1).start()
        for n, chunk in enumerate((chunk_a, chunk_b)):
            for g in range(KV):
                part = kvt[app, g, : 2 * HEAD, pl.ds(mul(chunk * CH, CH), CH)]
                kvn[app, g, pl.ds(mul(chunk * CH, CH), CH), :] = part.T
        if app == 0:
            loads[0].wait()
        query_raw = dot(wq[...], low, TN)
        for h in range(HEADS):
            g, j = h // 3, h % 3
            a, b = turn(query_raw[h * 64 : h * 64 + 32], query_raw[h * 64 + 32 : h * 64 + 64], 1)
            both = (jnp.concatenate([a, b], axis=0) * 0.125).astype(BF)
            for n in range(2):
                at = n * 768 + j * CH
                qz[app, g, :HEAD, at : at + CH] = both[:, n * CH : n * CH + CH]
        for n in range(2):
            kv_copy(app, n).wait_send()
            kv_arrival(app, n).wait_recv()
            chunk = 3 - 2 * (1 - c) if n == 0 else 2 * (1 - c)
            for g in range(KV):
                part = kvt[app, g, : 2 * HEAD, pl.ds(mul(chunk * CH, CH), CH)]
                kvn[app, g, pl.ds(mul(chunk * CH, CH), CH), :] = part.T
        pl.when(c == 0)(lambda: attend(app, plans[0]))
        pl.when(c == 1)(lambda: attend(app, plans[1]))
        if app == 0:
            loads[1].wait()
        att = state[app] + dot(wo[...], mix[app], TN)
        after[app] = att
        low = norm(att, gain_mt, root_m, app)
        n_m[app] = low
        if app == 0:
            for load in loads[2:5]:
                load.wait()
        result = att
        for k in range(3):
            span = slice(k * 512, k * 512 + 512)
            pre = dot(wg[:, span], low, TN)
            pre_up = dot(wu[:, span], low, TN)
            gate[app, span, :] = pre.astype(BF)
            up[app, span, :] = pre_up.astype(BF)
            hidden = (pre * (1.0 / (1.0 + jnp.exp(-pre))) * pre_up).astype(BF)
            result = result + dot(wd[:, span], hidden)
        return result

    def put(base, height, value, add=False):
        width = value.shape[1]
        for j in range((width + 127) // 128):
            lanes = min(128, width - j * 128)
            here = pl.ds(base + j * height, height)
            part = value[:, j * 128 : j * 128 + lanes]
            if add:
                part = part + grads[here, :lanes].astype(F32)
            grads[here, :lanes] = part.astype(BF)

    def fold(value):
        return value[:, :128] + value[:, 128:256] + value[:, 256:384] + value[:, 384:]

    def norm_back(d_normed, values, root, gain, sums):
        scaled = d_normed * wide(gain)
        sums[...] += fold(d_normed * (values * root))
        mean = jnp.mean(scaled * values, axis=0, keepdims=True)
        return root * scaled - values * (root * root * root * mean)

    one = Reduction(0, EARLY // 12, ORDERS, grads, (a0, a1, a2, a3), (a_s, a_r, a_ps, a_pr, a_f))
    two = Reduction(EARLY // 2, EARLY // 12, ORDERS, grads, (b0, b1, b2, b3), (b_s, b_r, b_ps, b_pr, b_f))
    third = Reduction(EARLY, LATE1 // 4, LATE_ORDERS, grads, (l0, l1, l2, l3), (l_s, l_r, l_ps, l_pr, l_f))
    four = Reduction(EARLY + LATE1, LATE2 // 4, LATE_ORDERS, grads, (m0, m1, m2, m3), (m_s, m_r, m_ps, m_pr, m_f))

    def mlp_back(app, after_tile):
        g_low = grad[...].astype(BF)
        if app == 1:
            g_keep[...] = g_low
        d_normed = None
        for k in range(3):
            span = slice(k * 512, k * 512 + 512)
            d_hidden = dot(wd[:, span], g_low, TN).astype(BF).astype(F32)
            pre = gate[app, span, :].astype(F32)
            pre_up = up[app, span, :].astype(F32)
            s = 1.0 / (1.0 + jnp.exp(-pre))
            act = pre * s
            hidden = (act * pre_up).astype(BF)
            d_gate = (d_hidden * pre_up * (s + act * (1.0 - s))).astype(BF)
            d_up = (d_hidden * act).astype(BF)
            if app == 1:
                hid_keep[span, :] = hidden
                gate[1, span, :] = d_gate
                up[1, span, :] = d_up
            else:
                put(k * TILE + B_WD, D, dot(g_low, hidden, NT) + dot(g_keep[...], hid_keep[span, :], NT))
                put(k * TILE + B_WG, D, dot(n_m[0], d_gate, NT) + dot(n_m[1], gate[1, span, :], NT))
                put(k * TILE + B_WU, D, dot(n_m[0], d_up, NT) + dot(n_m[1], up[1, span, :], NT))
            term = dot(wg[:, span], d_gate) + dot(wu[:, span], d_up)
            d_normed = term if d_normed is None else d_normed + term
            after_tile(k)
        grad[...] += norm_back(d_normed, after[app], root_m[app][0:1], gain_mt, gg_m)

    def attend_back(app, plan, between):
        dkv[...] = jnp.zeros(dkv.shape, F32)

        def products(g, n, k):
            cols = slice(n * 768, n * 768 + 768)
            rows = slice(k * CH, k * CH + CH)
            return dot(kvn[app, g, rows, :], qz[app, g, :, cols]), dot(kvn[app, g, rows, :], d_oz[g, :, cols])

        def three(v):
            return jnp.concatenate([v] * 3, axis=1)

        def group(g, carry):
            tiles = [(n, chunk, k) for n, chunk in plan for k in range(chunk + 1)]
            coming = products(g, tiles[0][0], tiles[0][2])
            d_query = None
            for i, (n, chunk, k) in enumerate(tiles):
                s, d_probs = coming
                if i + 1 < len(tiles):
                    coming = products(g, tiles[i + 1][0], tiles[i + 1][2])
                cols = slice(n * 768, n * 768 + 768)
                rows = slice(k * CH, k * CH + CH)
                log_sum = lse[app, g, 0:1, cols]
                if k == chunk:
                    s = s + three(bias_d[n])
                elif k == 0:
                    s = jnp.concatenate([s[:LOC] + three(bias_f[n]), s[LOC:] - three(big[n][0:1])], axis=0)
                else:
                    log_sum = log_sum + three(big[n][0:1])
                probs = jnp.exp(s - log_sum)
                d_score = (probs * (d_probs - delta[g, 0:1, cols])).astype(BF)
                low = probs.astype(BF)
                term = dot(kvt[app, g, :HEAD, rows], d_score)
                d_query = term if k == 0 else d_query + term
                dkv[g, rows, :] += dot(d_score, qz[app, g, :, cols], NT) + dot(low, d_oz[g, :, cols], NT)
                if k < chunk:
                    continue
                d_query = d_query * 0.125
                at = slice(n * CH, n * CH + CH)
                cs, sn = cos_t[:, at], sin_t[:, at]
                for j in range(3):
                    head = pl.ds(mul(g * 192 + j * HEAD, HEAD), HEAD)
                    a, b = d_query[:32, j * CH : j * CH + CH], d_query[32:, j * CH : j * CH + CH]
                    both = jnp.concatenate([a * cs + b * sn, b * cs - a * sn], axis=0)
                    dqkv[app, head, at] = both.astype(BF)
            for n in range(2):
                chunk = 3 - 2 * (1 - c) if n == 0 else 2 * (1 - c)
                dkv_out[g, n * CH : n * CH + CH, :] = dkv[g, pl.ds(mul(chunk * CH, CH), CH), :].astype(BF)
            dkv_copy(app, g).start()
            between(g)
            return carry

        lax.fori_loop(0, KV, group, 0)

    def dkv_copy(app, g):
        return pltpu.make_async_remote_copy(
            src_ref=dkv_out.at[g], dst_ref=dkv_in.at[app, g], send_sem=dkv_send.at[app, g],
            recv_sem=dkv_recv.at[app, g], device_id=device(y, 1 - c, z, x), device_id_type=MESH,
        )

    def attn_back(app, before, before_groups, between, after_query):
        g_low = grad[...].astype(BF)
        if app == 1:
            d_keep[...] = g_low
        else:
            put(B_WO, D, dot(mix[0], g_low, NT) + dot(mix[1], d_keep[...], NT))
        before()
        d_mixed = dot(wo[...], g_low)
        for h in range(HEADS):
            g, j = h // 3, h % 3
            dm = d_mixed[h * 64 : h * 64 + 64].astype(BF)
            dl = jnp.sum(dm.astype(F32) * mix[app, h * 64 : h * 64 + 64, :].astype(F32), axis=0, keepdims=True)
            for n in range(2):
                at = n * 768 + j * CH
                d_oz[g, HEAD:, at : at + CH] = dm[:, n * CH : n * CH + CH]
                delta[g, :, at : at + CH] = jnp.broadcast_to(dl[:, n * CH : n * CH + CH], (8, CH))
        if app == 0:
            for span in (0, 1):
                put_late(1, span, False)
        before_groups()
        pl.when(c == 0)(lambda: attend_back(app, plans[0], between))
        pl.when(c == 1)(lambda: attend_back(app, plans[1], between))
        dq = dqkv[app, :D, :]
        if app == 0:
            put_late_query(0, 1, True)
        d_normed = dot(wq[...], dq)
        after_query()
        if app == 0:
            join_keys(0, (2,))
            put_late_keys(0, 1, True)
        else:
            join_keys(1, range(KV))
        d_normed = d_normed + dot(wkv[...], dqkv[app, D:, :], TN)
        grad[...] += norm_back(d_normed, state[app], root_a[app][0:1], gain_at, gg_a)

    def join_keys(app, groups):
        for g in groups:
            dkv_copy(app, g).wait()
            parts = []
            for n, chunk in enumerate((chunk_a, chunk_b)):
                own = dkv[g, pl.ds(mul(chunk * CH, CH), CH), :]
                other = dkv_in[app, g, n * CH : n * CH + CH, :].astype(F32)
                parts.append((own + other).T)
            both = jnp.concatenate(parts, axis=1)
            a, b = turn(both[:32], both[32:64], -1)
            at = D + g * 2 * HEAD
            dqkv[app, at : at + 2 * HEAD, :] = jnp.concatenate([a, b, both[64:]], axis=0).astype(BF)

    def put_late_query(app, span, add):
        base, start, end = ((B_Q1, 0, 384), (B_Q2, 384, D))[span]
        put(base, D, dot(n_a[app], dqkv[app, start:end, :], NT), add)

    def put_late_keys(app, span, add):
        base, start, end = ((B_K1, D, D + 256), (B_K2, D + 256, D + KV_ROWS))[span]
        put(base, end - start, dot(dqkv[app, start:end, :], n_a[app], NT), add)

    def put_late(app, span, add):
        put_late_query(app, span, add)
        put_late_keys(app, span, add)

    def nothing(*unused):
        return None

    spread_send_wait(x_in, x_land, x_send, x_recv)
    spread_recv_wait(x_in, x_land, x_send, x_recv)
    spread_start(cot_in, c_land, c_send, c_recv)
    for slot in range(4):
        state[0, :, slot * LOC : slot * LOC + LOC] = x_land[slot].astype(F32)
    state[1] = forward(0)
    final = forward(1)
    for slot in range(4):
        x_land[slot] = final[:, slot * LOC : slot * LOC + LOC].astype(BF)
    for slot in range(4):
        home_start(x_land, out, o_send, o_recv, slot)
    spread_send_wait(cot_in, c_land, c_send, c_recv)
    spread_recv_wait(cot_in, c_land, c_send, c_recv)
    for slot in range(4):
        grad[:, slot * LOC : slot * LOC + LOC] = c_land[slot].astype(F32)

    mlp_back(1, nothing)
    attn_back(1, nothing, nothing, nothing, nothing)
    def after_tile(k):
        if k == 1:
            one.pair_start()
        if k == 2:
            two.pair_start((0, 1))
            one.pair_finish()
            one.scatter_start(0)

    mlp_back(0, after_tile)

    def after_wo():
        two.pair_start((2,))

    def before_groups():
        two.pair_finish()
        two.scatter_start(0)

    def between(g):
        @pl.when(g == 0)
        def _():
            one.scatter_finish(0)
            one.scatter_start(1)

        @pl.when(g == 1)
        def _():
            one.scatter_finish(1)
            one.swap_start()
            two.scatter_finish(0)
            two.scatter_start(1)
            join_keys(0, (0, 1))
            put_late(0, 0, True)
            third.pair_start()

        @pl.when(g == 2)
        def _():
            one.swap_finish()
            one.gather_start(1)
            third.pair_finish()
            third.scatter_start(0)

    def after_query():
        two.scatter_finish(1)
        two.swap_start()

    attn_back(0, after_wo, before_groups, between, after_query)
    lane = lax.broadcasted_iota(jnp.int32, (D, 64), 1)
    sum_a = jnp.sum(gg_a[...], axis=1, keepdims=True)
    sum_m = jnp.sum(gg_m[...], axis=1, keepdims=True)
    columns = jnp.where(lane == 0, sum_a, jnp.where(lane == 1, sum_m, 0.0))
    grads[pl.ds(B_Q2 + D, D), 64:] = columns.astype(BF)
    four.pair_start()
    for slot in range(4):
        c_land[slot] = grad[:, slot * LOC : slot * LOC + LOC].astype(BF)
    for slot in range(4):
        home_start(c_land, in_grad, i_send, i_recv, slot)
    one.gather_finish(1)
    one.gather_piece(1)
    four.pair_finish()
    four.scatter_start(0)
    two.swap_finish()
    two.gather_start(1)
    one.gather_piece(3)
    four.scatter_finish(0)
    four.scatter_start(1)
    third.scatter_finish(0)
    third.scatter_start(1)
    two.gather_finish(1)
    one.gather_piece(2)
    two.gather_piece(1)
    four.scatter_finish(1)
    four.swap_start()
    third.scatter_finish(1)
    third.swap_start()
    two.gather_piece(3)
    four.swap_finish()
    four.gather_start(1)
    third.swap_finish()
    third.gather_start(1)
    two.gather_piece(2)
    one.share()
    four.gather_finish(1)
    four.gather_start(0)
    third.gather_finish(1)
    third.gather_start(0)
    two.share()
    four.share()
    third.share()
    one.share_finish()
    two.share_finish()
    four.share_finish()
    third.share_finish()
    home_wait(x_land, out, o_send, o_recv)
    home_wait(c_land, in_grad, i_send, i_recv)


def train_step(inputs, docs, gain_a, wq, wk, wv, wo, gain_m, wg, wu, wd, cot):
    hbm = pl.BlockSpec(memory_space=pl.ANY)
    vmem = pl.BlockSpec(memory_space=pltpu.VMEM)
    smem = pl.BlockSpec(memory_space=pltpu.SMEM)
    dma = pltpu.SemaphoreType.DMA
    v = pltpu.VMEM
    scratch = [
        v((D, D), BF), v((KV_ROWS, D), BF), v((D, D), BF), v((D, FF), BF), v((D, FF), BF), v((D, FF), BF),
        v((4, D, LOC), BF), v((4, D, LOC), BF), v((D, 128), F32), v((D, 128), F32),
        v((32, TOK), F32), v((32, TOK), F32), v((2, LOC, CH), F32), v((2, CH, CH), F32), v((2, 8, CH), F32),
        v((2, D, TOK), F32), v((2, D, TOK), F32), v((2, D, TOK), BF), v((2, D, TOK), BF), v((2, D, TOK), BF),
        v((2, KV, 128, 6 * CH), BF), v((2, KV, 144, ROW), BF), v((2, KV, ROW, 128), BF), v((2, KV, 8, 6 * CH), F32),
        v((2, 8, TOK), F32), v((2, 8, TOK), F32), v((2, FF, TOK), BF), v((2, FF, TOK), BF),
        v((D, TOK), F32), v((KV, 128, 6 * CH), BF), v((KV, 8, 6 * CH), F32), v((KV, ROW, 128), F32),
        v((2, 960, TOK), BF), v((KV, TOK, 128), BF), v((2, KV, TOK, 128), BF), v((D, 128), F32), v((D, 128), F32),
        v((FF, TOK), BF), v((D, TOK), BF), v((D, TOK), BF),
    ]
    for n, part in ((3, EARLY // 12), (3, EARLY // 12), (2, LATE1 // 4), (2, LATE2 // 4)):
        scratch += [v((n, part, 128), BF), v((n, 3, part // 4, 128), BF), v((n, 3, part // 16, 128), BF)]
        scratch += [v((n, 4, part // 16, 128), BF)]
    scratch += [dma((11,))] + [dma((4,))] * 8 + [dma((2, 2))] * 2 + [dma((2, KV))] * 2
    for n in (3, 3, 2, 2):
        scratch += [dma((5, n)), dma((5, n)), dma((2 * n,)), dma((2 * n,)), pltpu.SemaphoreType.REGULAR]
    out, in_grad, total = pl.pallas_call(
        step_kernel,
        out_shape=(
            jax.ShapeDtypeStruct((4, D, LOC), BF),
            jax.ShapeDtypeStruct((4, D, LOC), BF),
            pltpu.VMEM((TOTAL, 128), BF),
        ),
        in_specs=[hbm, hbm, smem, vmem, vmem] + [hbm] * 7,
        out_specs=(hbm, hbm, vmem),
        scratch_shapes=scratch,
        compiler_params=pltpu.CompilerParams(
            collective_id=0, has_side_effects=True, vmem_limit_bytes=55 * 2**20
        ),
        name="train_step",
    )(inputs, cot, docs, gain_a, gain_m, wq, wk, wv, wo, wg, wu, wd)
    return out, in_grad, total


def unpack_kernel(total, out, in_grad, out_c, in_grad_c, ga, gq, gk, gv, go, gm, gg, gu, gd, state, sq, sk, sv, so, sg, su, sd, in_sem, out_sem):
    loads = [pltpu.make_async_copy(a, state.at[k], in_sem.at[k]) for k, a in enumerate((out, in_grad))]
    for load in loads:
        load.start()
    stores = []

    def store(source, target):
        stores.append(pltpu.make_async_copy(source, target, out_sem.at[len(stores)]))
        stores[-1].start()

    def panels(base, height, width, target):
        for j in range((width + 127) // 128):
            lanes = min(128, width - j * 128)
            target[:, j * 128 : j * 128 + lanes] = total[pl.ds(base + j * height, height), :lanes].astype(F32)

    for k in range(3):
        for base, source, target in ((B_WD, sd, gd), (B_WG, sg, gg), (B_WU, su, gu)):
            span = slice(k * 512, k * 512 + 512)
            panels(k * TILE + base, D, 512, source.at[:, span])
            store(source.at[:, span], target.at[:, span])
    panels(B_WO, D, D, so)
    store(so, go)
    panels(B_Q1, D, 384, sq.at[:, :384])
    panels(B_Q2, D, 192, sq.at[:, 384:])
    store(sq, gq)
    for g, base, height in ((0, B_K1, 256), (1, B_K1 + 128, 256), (2, B_K2, 128)):
        for k, target in enumerate((sk, sv)):
            for j in range(5):
                lanes = min(128, D - j * 128)
                rows = pl.ds(base + j * height + k * HEAD, HEAD)
                target[g * HEAD : g * HEAD + HEAD, j * 128 : j * 128 + lanes] = total[rows, :lanes].astype(F32)
    store(sk, gk)
    store(sv, gv)
    gains = total[pl.ds(B_Q2 + D, D), :].astype(F32).T
    ga[...] = gains[64]
    gm[...] = gains[65]
    for k, target in enumerate((out_c, in_grad_c)):
        loads[k].wait()
        store(state.at[k], target)
    for copy in stores:
        copy.wait()


def unpack(total, out, in_grad):
    hbm = pl.BlockSpec(memory_space=pl.ANY)
    vmem = pl.BlockSpec(memory_space=pltpu.VMEM)
    shape = jax.ShapeDtypeStruct
    v = pltpu.VMEM
    result = pl.pallas_call(
        unpack_kernel,
        out_shape=(
            shape(out.shape, BF), shape(out.shape, BF),
            shape((D,), F32), shape((D, D), F32), shape((192, D), F32), shape((192, D), F32), shape((D, D), F32),
            shape((D,), F32), shape((D, FF), F32), shape((D, FF), F32), shape((D, FF), F32),
        ),
        in_specs=[vmem, hbm, hbm],
        out_specs=(hbm, hbm, vmem, hbm, hbm, hbm, hbm, vmem, hbm, hbm, hbm),
        scratch_shapes=[
            v((2,) + out.shape, BF), v((D, D), F32), v((192, D), F32), v((192, D), F32), v((D, D), F32),
            v((D, FF), F32), v((D, FF), F32), v((D, FF), F32),
            pltpu.SemaphoreType.DMA((2,)), pltpu.SemaphoreType.DMA((15,)),
        ],
        compiler_params=pltpu.CompilerParams(vmem_limit_bytes=56 * 2**20),
        name="unpack",
    )(pltpu.with_memory_space_constraint(total, pltpu.VMEM), out, in_grad)
    return result


def on_device(inputs, docs, gain_a, wq, wk, wv, wo, gain_m, wg, wu, wd, cot):
    out, in_grad, total = train_step(
        inputs.transpose(0, 2, 1), docs, gain_a, wq, wk.T, wv.T, wo, gain_m, wg, wu, wd.T, cot.transpose(0, 2, 1)
    )
    out, in_grad, ga, gq, gk, gv, go, gm, gg, gu, gd = unpack(total, out, in_grad)
    return out.transpose(0, 2, 1), in_grad.transpose(0, 2, 1), ga, gq, gk.T, gv.T, go, gm, gg, gu, gd.T


def solution(mesh):
    token = P("rows", "seq", None)
    in_specs = (token, P("rows", None)) + (P(),) * 9 + (token,)
    out_specs = (token, token) + (P(),) * 9
    return jax.shard_map(on_device, mesh=mesh, in_specs=in_specs, out_specs=out_specs, check_vma=False)
```

```python
import functools

import jax
import jax.numpy as jnp
from jax import lax
from jax.experimental import pallas as pl
from jax.experimental.pallas import tpu as pltpu
from jax.sharding import PartitionSpec as P

D = 576
HEADS = 9
KV = 3
HEAD = 64
FF = 1536
ROW = 1024
LOC = 128
TOK = 512
CH = 256
EPS = 1e-05
THETA = 10000.0
NEG = -1e30
BF = jnp.bfloat16
F32 = jnp.float32
MESH = pl.DeviceIdType.MESH

NN = ((1,), (0,))
NT = ((1,), (1,))
TN = ((0,), (0,))

TILE = 12 * D
B_WD, B_WG, B_WU = 0, 4 * D, 8 * D
B_WO = 3 * TILE
EARLY = 24576
KV_ROWS = 2 * KV * HEAD
LATE1, LATE2 = 3072, 2048
B_Q1 = EARLY
B_K1 = B_Q1 + 3 * D
B_Q2 = EARLY + LATE1
B_K2 = B_Q2 + 2 * D
TOTAL = EARLY + LATE1 + LATE2
ORDERS = (("x", "y", "z"), ("y", "z", "x"), ("z", "x", "y"))
LATE_ORDERS = (("x", "z", "y"), ("z", "x", "y"))


def dot(a, b, dims=NN):
    return lax.dot_general(a, b, (dims, ((), ())), preferred_element_type=F32)


def position():
    s = lax.axis_index("seq")
    r = lax.axis_index("rows")
    return s // 2, s % 2, r // 4, r % 4


def device(y, c, z, x):
    return (y * 2 + c, z * 4 + x)


def mul(offset, size):
    return pl.multiple_of(offset, size)


class Reduction:
    def __init__(self, base, part, orders, grads, landings, sems):
        self.base, self.part, self.grads = base, part, grads
        self.slots = range(len(orders))
        self.landings = landings
        self.send, self.recv, self.pair_s, self.pair_r, self.free = sems
        self.y, self.c, self.z, self.x = position()
        y, z, x = self.y, self.z, self.x
        where = {"x": x, "y": y, "z": z}
        self.orders = orders
        self.index = [[where[a] for a in order] for order in orders]
        self.sizes = (part, part // 4, part // 16)

    def peer(self, axis, index):
        at = {"x": self.x, "y": self.y, "z": self.z}
        at[axis] = index
        return device(at["y"], self.c, at["z"], at["x"])

    def start_of(self, slot, level, core=None):
        core = self.c if core is None else core
        at = self.base + (2 * slot + core) * self.part
        for k in range(level):
            at = at + self.index[slot][k] * self.sizes[k + 1]
        return at

    def within(self, slot, level):
        return self.start_of(slot, level) - self.start_of(slot, 0)

    def rows(self, ref, start, size):
        return ref.at[pl.ds(mul(start, 16), size)]

    def remote(self, source, target, send, recv, slot, axis, index):
        if axis == "core":
            where = device(self.y, 1 - self.c, self.z, self.x)
        else:
            where = self.peer(axis, index)
        return pltpu.make_async_remote_copy(
            src_ref=source, dst_ref=target, send_sem=send, recv_sem=recv, device_id=where, device_id_type=MESH
        )

    def pair_copy(self, slot):
        rows = self.rows(self.grads, self.start_of(slot, 0, 1 - self.c), self.part)
        return self.remote(rows, self.landings[0].at[slot], self.pair_s.at[slot], self.pair_r.at[slot], slot, "core", 0)

    def pair_start(self, slots=None):
        for slot in self.slots if slots is None else slots:
            self.pair_copy(slot).start()

    def pair_finish(self):
        step = min(256, self.part)
        land = self.landings[0]
        for slot in self.slots:
            self.pair_copy(slot).wait()
            at = self.start_of(slot, 0)

            def add(k, carry, slot=slot, at=at):
                here = pl.ds(mul(at + k * step, 16), step)
                there = pl.ds(mul(k * step, 16), step)
                both = self.grads[here, :].astype(F32) + land[slot, there, :].astype(F32)
                land[slot, there, :] = both.astype(BF)
                return carry

            lax.fori_loop(0, self.part // step, add, 0)
        where = device(self.y, 1 - self.c, self.z, self.x)
        pl.semaphore_signal(self.free, inc=1, device_id=where, device_id_type=MESH)

    def counted(self, ref, level, slot):
        axis = self.orders[slot][level % 3]
        index = (self.index[slot][level % 3] + 1) % 4
        return self.remote(ref, ref, self.send.at[level, slot], self.recv.at[level, slot], slot, axis, index)

    def scatter_copy(self, slot, level, d):
        index = (self.index[slot][level] + d) % 4
        size = self.sizes[level + 1]
        return self.remote(
            self.rows(self.landings[0].at[slot], self.within(slot, level) + index * size, size),
            self.landings[level + 1].at[slot, d - 1],
            self.send.at[level, slot],
            self.recv.at[level, slot],
            slot, self.orders[slot][level], index,
        )

    def scatter_start(self, level):
        for d in (2, 1, 3):
            for slot in self.slots:
                self.scatter_copy(slot, level, d).start()

    def scatter_finish(self, level):
        size = self.sizes[level + 1]
        step = next(k for k in (128, 160, size) if size % k == 0)
        land = self.landings[level + 1]
        for slot in self.slots:
            self.counted(land.at[slot], level, slot).wait()
            at = self.within(slot, level + 1)
            work = self.landings[0].at[slot]

            def add(k, carry, slot=slot, at=at, work=work):
                here = pl.ds(mul(at + k * step, 16), step)
                there = pl.ds(mul(k * step, 16), step)
                total = work[here, :].astype(F32)
                for d in range(3):
                    total = total + land[slot, d, there, :].astype(F32)
                work[here, :] = total.astype(BF)
                return carry

            lax.fori_loop(0, size // step, add, 0)

    def swap_copy(self, slot, d):
        mine = self.index[slot][2]
        return self.remote(
            self.rows(self.landings[0].at[slot], self.within(slot, 2), self.sizes[2]),
            self.landings[3].at[slot, mine], self.send.at[2, slot], self.recv.at[2, slot],
            slot, self.orders[slot][2], (mine + d) % 4,
        )

    def swap_start(self):
        for d in (2, 1, 3):
            for slot in self.slots:
                self.swap_copy(slot, d).start()
        for slot in self.slots:
            at = pl.ds(mul(self.within(slot, 2), 16), self.sizes[2])
            self.landings[3][slot, self.index[slot][2]] = self.landings[0][slot, at, :]

    def swap_finish(self):
        land = self.landings[3]
        for slot in self.slots:
            self.counted(land.at[slot, pl.ds(0, 3)], 2, slot).wait()
            total = land[slot, 0].astype(F32)
            for k in range(1, 4):
                total = total + land[slot, k].astype(F32)
            self.grads[pl.ds(mul(self.start_of(slot, 2), 16), self.sizes[2]), :] = total.astype(BF)

    def gather_copy(self, slot, level, d):
        mine = self.index[slot][level]
        rows = self.rows(self.grads, self.start_of(slot, level + 1), self.sizes[level + 1])
        return self.remote(
            rows, rows, self.send.at[3 + level, slot], self.recv.at[3 + level, slot],
            slot, self.orders[slot][level], (mine + d) % 4,
        )

    def gather_piece(self, d):
        for slot in self.slots:
            self.gather_copy(slot, 0, d).start()

    def gather_start(self, level):
        for d in (2, 1, 3):
            for slot in self.slots:
                self.gather_copy(slot, level, d).start()

    def gather_finish(self, level):
        for slot in self.slots:
            self.gather_wait(slot, level)

    def gather_wait(self, slot, level):
        rows = self.rows(self.grads, self.start_of(slot, level), 3 * self.sizes[level + 1])
        self.counted(rows, 3 + level, slot).wait()

    def share_copy(self, slot, core):
        rows = self.rows(self.grads, self.start_of(slot, 0, core), self.part)
        n = len(self.slots)
        return self.remote(rows, rows, self.pair_s.at[n + slot], self.pair_r.at[n + slot], slot, "core", 0)

    def share(self):
        pl.semaphore_wait(self.free, 1)
        for slot in self.slots:
            self.gather_wait(slot, 0)
            self.share_copy(slot, self.c).start()

    def share_finish(self):
        for slot in self.slots:
            self.share_copy(slot, self.c).wait_send()
            self.share_copy(slot, 1 - self.c).wait_recv()


def step_kernel(
    x_in, cot_in, docs, gain_a, gain_m, wq_h, wk_h, wv_h, wo_h, wg_h, wu_h, wd_h,
    out, in_grad, grads,
    wq, wkv, wo, wg, wu, wd,
    x_land, c_land, gain_at, gain_mt, cos_t, sin_t, bias_f, bias_d, big,
    state, after, n_a, n_m, mix, qz, kvt, kvn, lse, root_a, root_m, gate, up,
    grad, d_oz, delta, dkv, dqkv, dkv_out, dkv_in, gg_a, gg_m, hid_keep, g_keep, d_keep,
    a0, a1, a2, a3, b0, b1, b2, b3, l0, l1, l2, l3, m0, m1, m2, m3,
    w_sem, x_send, x_recv, c_send, c_recv, o_send, o_recv, i_send, i_recv, kv_send, kv_recv, dkv_send, dkv_recv,
    a_s, a_r, a_ps, a_pr, a_f, b_s, b_r, b_ps, b_pr, b_f, l_s, l_r, l_ps, l_pr, l_f, m_s, m_r, m_ps, m_pr, m_f,
):
    y, c, z, x = position()
    me = y * 2 + c
    my_slot = (me + 2) % 4
    to_core = ((me + 2) % 8) // 4
    chunk_a = 3 - 2 * c
    chunk_b = 2 * c

    barrier = pltpu.get_barrier_semaphore()
    for k in range(1, 8):
        pl.semaphore_signal(barrier, inc=1, device_id=((me + k) % 8, z * 4 + x), device_id_type=MESH)
    for k in range(1, 4):
        pl.semaphore_signal(barrier, inc=1, device_id=device(y, c, (z + k) % 4, x), device_id_type=MESH)
        pl.semaphore_signal(barrier, inc=1, device_id=device(y, c, z, (x + k) % 4), device_id_type=MESH)
    weight_pairs = [(wq_h, wq), (wo_h, wo), (wg_h, wg), (wu_h, wu), (wd_h, wd)]
    for g in range(KV):
        for k, source in enumerate((wk_h, wv_h)):
            pair = (source.at[pl.ds(g * HEAD, HEAD)], wkv.at[pl.ds((2 * g + k) * HEAD, HEAD)])
            weight_pairs.append(pair)
    loads = [pltpu.make_async_copy(a, b, w_sem.at[k]) for k, (a, b) in enumerate(weight_pairs)]
    pl.semaphore_wait(barrier, 13)

    def spread(source, land, send, recv, k):
        r = (y + k) % 4
        target = r * 2 + to_core
        remote = pltpu.make_async_remote_copy(
            src_ref=source.at[r], dst_ref=land.at[my_slot], send_sem=send.at[k], recv_sem=recv.at[my_slot],
            device_id=(target, z * 4 + x), device_id_type=MESH,
        )
        local = pltpu.make_async_copy(source.at[r], land.at[my_slot], send.at[k])
        return target == me, remote, local

    def spread_start(source, land, send, recv):
        for k in (2, 1, 3, 0):
            own, remote, local = spread(source, land, send, recv, k)
            pl.when(own)(local.start)
            pl.when(jnp.logical_not(own))(remote.start)

    def spread_send_wait(source, land, send, recv):
        for k in range(4):
            own, remote, local = spread(source, land, send, recv, k)
            pl.when(own)(local.wait)
            pl.when(jnp.logical_not(own))(remote.wait_send)

    def spread_recv_wait(source, land, send, recv):
        for slot in range(4):
            home = (slot + 6 + 4 * c) % 8
            landed = pltpu.make_async_remote_copy(
                src_ref=source.at[0], dst_ref=land.at[slot], send_sem=send.at[0], recv_sem=recv.at[slot],
                device_id=(home, z * 4 + x), device_id_type=MESH,
            )
            pl.when(home != me)(landed.wait_recv)

    def home_copy(source, result, send, recv, slot):
        home = (slot + 6 + 4 * c) % 8
        remote = pltpu.make_async_remote_copy(
            src_ref=source.at[slot], dst_ref=result.at[y], send_sem=send.at[slot], recv_sem=recv.at[y],
            device_id=(home, z * 4 + x), device_id_type=MESH,
        )
        local = pltpu.make_async_copy(source.at[slot], result.at[y], send.at[slot])
        return home == me, remote, local

    def home_start(source, result, send, recv, slot):
        own, remote, local = home_copy(source, result, send, recv, slot)
        pl.when(own)(local.start)
        pl.when(jnp.logical_not(own))(remote.start)

    def home_wait(source, result, send, recv):
        for slot in range(4):
            own, remote, local = home_copy(source, result, send, recv, slot)
            pl.when(own)(local.wait)
            pl.when(jnp.logical_not(own))(remote.wait_send)
        for r in range(4):
            origin = r * 2 + to_core
            landed = pltpu.make_async_remote_copy(
                src_ref=source.at[0], dst_ref=result.at[r], send_sem=send.at[0], recv_sem=recv.at[r],
                device_id=(origin, z * 4 + x), device_id_type=MESH,
            )
            pl.when(origin != me)(landed.wait_recv)

    spread_start(x_in, x_land, x_send, x_recv)
    for load in loads:
        load.start()

    end0 = docs[y, 0]
    end1 = end0 + docs[y, 1]
    column = lax.broadcasted_iota(jnp.int32, (1, TOK), 1)
    token = jnp.where(column < CH, column + chunk_a * CH, column - CH + chunk_b * CH)
    first = jnp.where(token < end0, 0, jnp.where(token < end1, end0, end1))
    place = (token - first).astype(F32)
    half = lax.broadcasted_iota(jnp.int32, (HEAD // 2, TOK), 0).astype(F32)
    angles = place * jnp.exp(half * (-2.0 / HEAD * 9.210340371976184))
    cos_t[...] = jnp.cos(angles)
    sin_t[...] = jnp.sin(angles)
    for n, chunk in enumerate((chunk_a, chunk_b)):
        cols = slice(n * CH, n * CH + CH)
        fi, tk = first[:, cols], token[:, cols]
        key = lax.broadcasted_iota(jnp.int32, (LOC, CH), 0)
        bias_f[n] = jnp.where(key >= fi, 0.0, NEG).astype(F32)
        key = lax.broadcasted_iota(jnp.int32, (CH, CH), 0) + chunk * CH
        bias_d[n] = jnp.where((key >= fi) & (key <= tk), 0.0, NEG).astype(F32)
        big[n] = jnp.broadcast_to(jnp.where(fi > LOC, -NEG, 0.0).astype(F32), (8, CH))
    gain_at[...] = jnp.broadcast_to(gain_a[...].reshape(1, D), (128, D)).T
    gain_mt[...] = jnp.broadcast_to(gain_m[...].reshape(1, D), (128, D)).T
    gg_a[...] = jnp.zeros(gg_a.shape, F32)
    gg_m[...] = jnp.zeros(gg_m.shape, F32)
    for app in range(2):
        qz[app, :, HEAD:, :] = jnp.zeros((KV, HEAD, 6 * CH), BF)
        kvt[app, :, 2 * HEAD :, :] = jnp.ones((KV, 16, ROW), BF)
    d_oz[:, :HEAD, :] = jnp.zeros((KV, HEAD, 6 * CH), BF)
    grads[pl.ds(B_WO + 4 * D, D), :] = jnp.zeros((D, 128), BF)
    grads[pl.ds(B_WO + 5 * D, EARLY - B_WO - 5 * D), :] = jnp.zeros((EARLY - B_WO - 5 * D, 128), BF)
    for start, end in ((B_K1 + 4 * 256, EARLY + LATE1), (B_K2 + 4 * 128, TOTAL)):
        grads[pl.ds(start, end - start), :] = jnp.zeros((end - start, 128), BF)

    def wide(gain):
        return jnp.concatenate([gain[...]] * 4, axis=1)

    def norm(values, gain, roots, app):
        root = lax.rsqrt(jnp.mean(values * values, axis=0, keepdims=True) + EPS)
        roots[app] = jnp.broadcast_to(root, (8, TOK))
        return (values * root * wide(gain)).astype(BF)

    def turn(a, b, sign):
        cs, sn = cos_t[...], sin_t[...]
        if sign > 0:
            return a * cs - b * sn, b * cs + a * sn
        return a * cs + b * sn, b * cs - a * sn

    def kv_copy(app, n):
        chunk = chunk_a if n == 0 else chunk_b
        span = kvt.at[app, :, pl.ds(0, 2 * HEAD), pl.ds(mul(chunk * CH, CH), CH)]
        return pltpu.make_async_remote_copy(
            src_ref=span, dst_ref=span, send_sem=kv_send.at[app, n], recv_sem=kv_recv.at[app, n],
            device_id=device(y, 1 - c, z, x), device_id_type=MESH,
        )

    def kv_arrival(app, n):
        chunk = 3 - 2 * (1 - c) if n == 0 else 2 * (1 - c)
        span = kvt.at[app, :, pl.ds(0, 2 * HEAD), pl.ds(mul(chunk * CH, CH), CH)]
        return pltpu.make_async_remote_copy(
            src_ref=span, dst_ref=span, send_sem=kv_send.at[app, n], recv_sem=kv_recv.at[app, n],
            device_id=device(y, 1 - c, z, x), device_id_type=MESH,
        )

    plans = (((0, 3), (1, 0)), ((0, 1), (1, 2)))

    def softmax(s, n, chunk):
        nk = (chunk + 1) * CH
        tail = s[nk - CH :] + bias_d[n]
        top = jnp.max(tail, axis=0, keepdims=True)
        if chunk == 0:
            return top, jnp.exp(tail - top).astype(BF)
        lead = s[:LOC] + bias_f[n]
        shut = big[n][0:1]
        middle = s[LOC : nk - CH]
        top = jnp.maximum(top, jnp.max(lead, axis=0, keepdims=True))
        top = jnp.maximum(top, jnp.max(middle, axis=0, keepdims=True) - shut)
        low = [jnp.exp(lead - top), jnp.exp(middle - (top + shut)), jnp.exp(tail - top)]
        return top, jnp.concatenate([v.astype(BF) for v in low], axis=0)

    def attend(app, plan):
        def group(g, carry):
            scores = []
            for n, chunk in plan:
                nk = (chunk + 1) * CH
                scores.append(dot(kvn[app, g, :nk, :], qz[app, g, :, n * 768 : n * 768 + 768]))
            for (n, chunk), s in zip(plan, scores):
                nk = (chunk + 1) * CH
                for j in range(3):
                    top, low = softmax(s[:, j * CH : j * CH + CH], n, chunk)
                    mixed = dot(kvt[app, g, HEAD:, :nk], low)
                    total_w = mixed[HEAD : HEAD + 1]
                    rows = pl.ds(mul(g * 192 + j * HEAD, HEAD), HEAD)
                    mix[app, rows, n * CH : n * CH + CH] = (mixed[:HEAD] * (1.0 / total_w)).astype(BF)
                    at = n * 768 + j * CH
                    lse[app, g, :, at : at + CH] = jnp.broadcast_to(top + jnp.log(total_w), (8, CH))
            return carry

        lax.fori_loop(0, KV, group, 0)

    def forward(app):
        values = state[app]
        low = norm(values, gain_at, root_a, app)
        n_a[app] = low
        if app == 0:
            for load in loads[5:]:
                load.wait()
        raw = dot(wkv[...], low)
        for g in range(KV):
            a, b = turn(raw[g * 128 : g * 128 + 32], raw[g * 128 + 32 : g * 128 + 64], 1)
            packed = jnp.concatenate([a, b, raw[g * 128 + 64 : g * 128 + 128]], axis=0).astype(BF)
            for n, chunk in enumerate((chunk_a, chunk_b)):
                kvt[app, g, : 2 * HEAD, pl.ds(mul(chunk * CH, CH), CH)] = packed[:, n * CH : n * CH + CH]
        kv_copy(app, 0).start()
        kv_copy(app, 1).start()
        for n, chunk in enumerate((chunk_a, chunk_b)):
            for g in range(KV):
                part = kvt[app, g, : 2 * HEAD, pl.ds(mul(chunk * CH, CH), CH)]
                kvn[app, g, pl.ds(mul(chunk * CH, CH), CH), :] = part.T
        if app == 0:
            loads[0].wait()
        query_raw = dot(wq[...], low, TN)
        for h in range(HEADS):
            g, j = h // 3, h % 3
            a, b = turn(query_raw[h * 64 : h * 64 + 32], query_raw[h * 64 + 32 : h * 64 + 64], 1)
            both = (jnp.concatenate([a, b], axis=0) * 0.125).astype(BF)
            for n in range(2):
                at = n * 768 + j * CH
                qz[app, g, :HEAD, at : at + CH] = both[:, n * CH : n * CH + CH]
        for n in range(2):
            kv_copy(app, n).wait_send()
            kv_arrival(app, n).wait_recv()
            chunk = 3 - 2 * (1 - c) if n == 0 else 2 * (1 - c)
            for g in range(KV):
                part = kvt[app, g, : 2 * HEAD, pl.ds(mul(chunk * CH, CH), CH)]
                kvn[app, g, pl.ds(mul(chunk * CH, CH), CH), :] = part.T
        pl.when(c == 0)(lambda: attend(app, plans[0]))
        pl.when(c == 1)(lambda: attend(app, plans[1]))
        if app == 0:
            loads[1].wait()
        att = state[app] + dot(wo[...], mix[app], TN)
        after[app] = att
        low = norm(att, gain_mt, root_m, app)
        n_m[app] = low
        if app == 0:
            for load in loads[2:5]:
                load.wait()
        result = att
        for k in range(3):
            span = slice(k * 512, k * 512 + 512)
            pre = dot(wg[:, span], low, TN)
            pre_up = dot(wu[:, span], low, TN)
            gate[app, span, :] = pre.astype(BF)
            up[app, span, :] = pre_up.astype(BF)
            hidden = (pre * (1.0 / (1.0 + jnp.exp(-pre))) * pre_up).astype(BF)
            result = result + dot(wd[:, span], hidden)
        return result

    def put(base, height, value, add=False):
        width = value.shape[1]
        for j in range((width + 127) // 128):
            lanes = min(128, width - j * 128)
            here = pl.ds(base + j * height, height)
            part = value[:, j * 128 : j * 128 + lanes]
            if add:
                part = part + grads[here, :lanes].astype(F32)
            grads[here, :lanes] = part.astype(BF)

    def fold(value):
        return value[:, :128] + value[:, 128:256] + value[:, 256:384] + value[:, 384:]

    def norm_back(d_normed, values, root, gain, sums):
        scaled = d_normed * wide(gain)
        sums[...] += fold(d_normed * (values * root))
        mean = jnp.mean(scaled * values, axis=0, keepdims=True)
        return root * scaled - values * (root * root * root * mean)

    one = Reduction(0, EARLY // 12, ORDERS, grads, (a0, a1, a2, a3), (a_s, a_r, a_ps, a_pr, a_f))
    two = Reduction(EARLY // 2, EARLY // 12, ORDERS, grads, (b0, b1, b2, b3), (b_s, b_r, b_ps, b_pr, b_f))
    third = Reduction(EARLY, LATE1 // 4, LATE_ORDERS, grads, (l0, l1, l2, l3), (l_s, l_r, l_ps, l_pr, l_f))
    four = Reduction(EARLY + LATE1, LATE2 // 4, LATE_ORDERS, grads, (m0, m1, m2, m3), (m_s, m_r, m_ps, m_pr, m_f))

    def mlp_back(app, after_tile):
        g_low = grad[...].astype(BF)
        if app == 1:
            g_keep[...] = g_low
        d_normed = None
        for k in range(3):
            span = slice(k * 512, k * 512 + 512)
            d_hidden = dot(wd[:, span], g_low, TN).astype(BF).astype(F32)
            pre = gate[app, span, :].astype(F32)
            pre_up = up[app, span, :].astype(F32)
            s = 1.0 / (1.0 + jnp.exp(-pre))
            act = pre * s
            hidden = (act * pre_up).astype(BF)
            d_gate = (d_hidden * pre_up * (s + act * (1.0 - s))).astype(BF)
            d_up = (d_hidden * act).astype(BF)
            if app == 1:
                hid_keep[span, :] = hidden
                gate[1, span, :] = d_gate
                up[1, span, :] = d_up
            else:
                put(k * TILE + B_WD, D, dot(g_low, hidden, NT) + dot(g_keep[...], hid_keep[span, :], NT))
                put(k * TILE + B_WG, D, dot(n_m[0], d_gate, NT) + dot(n_m[1], gate[1, span, :], NT))
                put(k * TILE + B_WU, D, dot(n_m[0], d_up, NT) + dot(n_m[1], up[1, span, :], NT))
            term = dot(wg[:, span], d_gate) + dot(wu[:, span], d_up)
            d_normed = term if d_normed is None else d_normed + term
            after_tile(k)
        grad[...] += norm_back(d_normed, after[app], root_m[app][0:1], gain_mt, gg_m)

    def attend_back(app, plan, between):
        dkv[...] = jnp.zeros(dkv.shape, F32)

        def products(g, n, k):
            cols = slice(n * 768, n * 768 + 768)
            rows = slice(k * CH, k * CH + CH)
            return dot(kvn[app, g, rows, :], qz[app, g, :, cols]), dot(kvn[app, g, rows, :], d_oz[g, :, cols])

        def three(v):
            return jnp.concatenate([v] * 3, axis=1)

        def group(g, carry):
            tiles = [(n, chunk, k) for n, chunk in plan for k in range(chunk + 1)]
            coming = products(g, tiles[0][0], tiles[0][2])
            d_query = None
            for i, (n, chunk, k) in enumerate(tiles):
                s, d_probs = coming
                if i + 1 < len(tiles):
                    coming = products(g, tiles[i + 1][0], tiles[i + 1][2])
                cols = slice(n * 768, n * 768 + 768)
                rows = slice(k * CH, k * CH + CH)
                log_sum = lse[app, g, 0:1, cols]
                if k == chunk:
                    s = s + three(bias_d[n])
                elif k == 0:
                    s = jnp.concatenate([s[:LOC] + three(bias_f[n]), s[LOC:] - three(big[n][0:1])], axis=0)
                else:
                    log_sum = log_sum + three(big[n][0:1])
                probs = jnp.exp(s - log_sum)
                d_score = (probs * (d_probs - delta[g, 0:1, cols])).astype(BF)
                low = probs.astype(BF)
                term = dot(kvt[app, g, :HEAD, rows], d_score)
                d_query = term if k == 0 else d_query + term
                dkv[g, rows, :] += dot(d_score, qz[app, g, :, cols], NT) + dot(low, d_oz[g, :, cols], NT)
                if k < chunk:
                    continue
                d_query = d_query * 0.125
                at = slice(n * CH, n * CH + CH)
                cs, sn = cos_t[:, at], sin_t[:, at]
                for j in range(3):
                    head = pl.ds(mul(g * 192 + j * HEAD, HEAD), HEAD)
                    a, b = d_query[:32, j * CH : j * CH + CH], d_query[32:, j * CH : j * CH + CH]
                    both = jnp.concatenate([a * cs + b * sn, b * cs - a * sn], axis=0)
                    dqkv[app, head, at] = both.astype(BF)
            for n in range(2):
                chunk = 3 - 2 * (1 - c) if n == 0 else 2 * (1 - c)
                dkv_out[g, n * CH : n * CH + CH, :] = dkv[g, pl.ds(mul(chunk * CH, CH), CH), :].astype(BF)
            dkv_copy(app, g).start()
            between(g)
            return carry

        lax.fori_loop(0, KV, group, 0)

    def dkv_copy(app, g):
        return pltpu.make_async_remote_copy(
            src_ref=dkv_out.at[g], dst_ref=dkv_in.at[app, g], send_sem=dkv_send.at[app, g],
            recv_sem=dkv_recv.at[app, g], device_id=device(y, 1 - c, z, x), device_id_type=MESH,
        )

    def attn_back(app, before, before_groups, between, after_query):
        g_low = grad[...].astype(BF)
        if app == 1:
            d_keep[...] = g_low
        else:
            put(B_WO, D, dot(mix[0], g_low, NT) + dot(mix[1], d_keep[...], NT))
        before()
        d_mixed = dot(wo[...], g_low)
        for h in range(HEADS):
            g, j = h // 3, h % 3
            dm = d_mixed[h * 64 : h * 64 + 64].astype(BF)
            dl = jnp.sum(dm.astype(F32) * mix[app, h * 64 : h * 64 + 64, :].astype(F32), axis=0, keepdims=True)
            for n in range(2):
                at = n * 768 + j * CH
                d_oz[g, HEAD:, at : at + CH] = dm[:, n * CH : n * CH + CH]
                delta[g, :, at : at + CH] = jnp.broadcast_to(dl[:, n * CH : n * CH + CH], (8, CH))
        if app == 0:
            for span in (0, 1):
                put_late(1, span, False)
        before_groups()
        pl.when(c == 0)(lambda: attend_back(app, plans[0], between))
        pl.when(c == 1)(lambda: attend_back(app, plans[1], between))
        dq = dqkv[app, :D, :]
        if app == 0:
            put_late_query(0, 1, True)
        d_normed = dot(wq[...], dq)
        after_query()
        if app == 0:
            join_keys(0, (2,))
            put_late_keys(0, 1, True)
        else:
            join_keys(1, range(KV))
        d_normed = d_normed + dot(wkv[...], dqkv[app, D:, :], TN)
        grad[...] += norm_back(d_normed, state[app], root_a[app][0:1], gain_at, gg_a)

    def join_keys(app, groups):
        for g in groups:
            dkv_copy(app, g).wait()
            parts = []
            for n, chunk in enumerate((chunk_a, chunk_b)):
                own = dkv[g, pl.ds(mul(chunk * CH, CH), CH), :]
                other = dkv_in[app, g, n * CH : n * CH + CH, :].astype(F32)
                parts.append((own + other).T)
            both = jnp.concatenate(parts, axis=1)
            a, b = turn(both[:32], both[32:64], -1)
            at = D + g * 2 * HEAD
            dqkv[app, at : at + 2 * HEAD, :] = jnp.concatenate([a, b, both[64:]], axis=0).astype(BF)

    def put_late_query(app, span, add):
        base, start, end = ((B_Q1, 0, 384), (B_Q2, 384, D))[span]
        put(base, D, dot(n_a[app], dqkv[app, start:end, :], NT), add)

    def put_late_keys(app, span, add):
        base, start, end = ((B_K1, D, D + 256), (B_K2, D + 256, D + KV_ROWS))[span]
        put(base, end - start, dot(dqkv[app, start:end, :], n_a[app], NT), add)

    def put_late(app, span, add):
        put_late_query(app, span, add)
        put_late_keys(app, span, add)

    def nothing(*unused):
        return None

    spread_send_wait(x_in, x_land, x_send, x_recv)
    spread_recv_wait(x_in, x_land, x_send, x_recv)
    spread_start(cot_in, c_land, c_send, c_recv)
    for slot in range(4):
        state[0, :, slot * LOC : slot * LOC + LOC] = x_land[slot].astype(F32)
    state[1] = forward(0)
    final = forward(1)
    for slot in range(4):
        x_land[slot] = final[:, slot * LOC : slot * LOC + LOC].astype(BF)
    for slot in range(4):
        home_start(x_land, out, o_send, o_recv, slot)
    spread_send_wait(cot_in, c_land, c_send, c_recv)
    spread_recv_wait(cot_in, c_land, c_send, c_recv)
    for slot in range(4):
        grad[:, slot * LOC : slot * LOC + LOC] = c_land[slot].astype(F32)

    mlp_back(1, nothing)
    attn_back(1, nothing, nothing, nothing, nothing)
    def after_tile(k):
        if k == 1:
            one.pair_start()
        if k == 2:
            two.pair_start((0, 1))
            one.pair_finish()
            one.scatter_start(0)

    mlp_back(0, after_tile)

    def after_wo():
        two.pair_start((2,))

    def before_groups():
        two.pair_finish()
        two.scatter_start(0)

    def between(g):
        @pl.when(g == 0)
        def _():
            one.scatter_finish(0)
            one.scatter_start(1)

        @pl.when(g == 1)
        def _():
            one.scatter_finish(1)
            one.swap_start()
            two.scatter_finish(0)
            two.scatter_start(1)
            join_keys(0, (0, 1))
            put_late(0, 0, True)
            third.pair_start()

        @pl.when(g == 2)
        def _():
            one.swap_finish()
            one.gather_start(1)
            third.pair_finish()
            third.scatter_start(0)

    attn_back(0, after_wo, before_groups, between, nothing)
    lane = lax.broadcasted_iota(jnp.int32, (D, 64), 1)
    sum_a = jnp.sum(gg_a[...], axis=1, keepdims=True)
    sum_m = jnp.sum(gg_m[...], axis=1, keepdims=True)
    columns = jnp.where(lane == 0, sum_a, jnp.where(lane == 1, sum_m, 0.0))
    grads[pl.ds(B_Q2 + D, D), 64:] = columns.astype(BF)
    four.pair_start()
    for slot in range(4):
        c_land[slot] = grad[:, slot * LOC : slot * LOC + LOC].astype(BF)
    for slot in range(4):
        home_start(c_land, in_grad, i_send, i_recv, slot)
    two.scatter_finish(1)
    two.swap_start()
    one.gather_finish(1)
    one.gather_piece(1)
    four.pair_finish()
    four.scatter_start(0)
    two.swap_finish()
    two.gather_start(1)
    one.gather_piece(3)
    four.scatter_finish(0)
    four.scatter_start(1)
    third.scatter_finish(0)
    third.scatter_start(1)
    two.gather_finish(1)
    one.gather_piece(2)
    two.gather_piece(1)
    four.scatter_finish(1)
    four.swap_start()
    third.scatter_finish(1)
    third.swap_start()
    two.gather_piece(3)
    four.swap_finish()
    four.gather_start(1)
    third.swap_finish()
    third.gather_start(1)
    two.gather_piece(2)
    one.share()
    four.gather_finish(1)
    four.gather_start(0)
    third.gather_finish(1)
    third.gather_start(0)
    two.share()
    four.share()
    third.share()
    one.share_finish()
    two.share_finish()
    four.share_finish()
    third.share_finish()
    home_wait(x_land, out, o_send, o_recv)
    home_wait(c_land, in_grad, i_send, i_recv)


def train_step(inputs, docs, gain_a, wq, wk, wv, wo, gain_m, wg, wu, wd, cot):
    hbm = pl.BlockSpec(memory_space=pl.ANY)
    vmem = pl.BlockSpec(memory_space=pltpu.VMEM)
    smem = pl.BlockSpec(memory_space=pltpu.SMEM)
    dma = pltpu.SemaphoreType.DMA
    v = pltpu.VMEM
    scratch = [
        v((D, D), BF), v((KV_ROWS, D), BF), v((D, D), BF), v((D, FF), BF), v((D, FF), BF), v((D, FF), BF),
        v((4, D, LOC), BF), v((4, D, LOC), BF), v((D, 128), F32), v((D, 128), F32),
        v((32, TOK), F32), v((32, TOK), F32), v((2, LOC, CH), F32), v((2, CH, CH), F32), v((2, 8, CH), F32),
        v((2, D, TOK), F32), v((2, D, TOK), F32), v((2, D, TOK), BF), v((2, D, TOK), BF), v((2, D, TOK), BF),
        v((2, KV, 128, 6 * CH), BF), v((2, KV, 144, ROW), BF), v((2, KV, ROW, 128), BF), v((2, KV, 8, 6 * CH), F32),
        v((2, 8, TOK), F32), v((2, 8, TOK), F32), v((2, FF, TOK), BF), v((2, FF, TOK), BF),
        v((D, TOK), F32), v((KV, 128, 6 * CH), BF), v((KV, 8, 6 * CH), F32), v((KV, ROW, 128), F32),
        v((2, 960, TOK), BF), v((KV, TOK, 128), BF), v((2, KV, TOK, 128), BF), v((D, 128), F32), v((D, 128), F32),
        v((FF, TOK), BF), v((D, TOK), BF), v((D, TOK), BF),
    ]
    for n, part in ((3, EARLY // 12), (3, EARLY // 12), (2, LATE1 // 4), (2, LATE2 // 4)):
        scratch += [v((n, part, 128), BF), v((n, 3, part // 4, 128), BF), v((n, 3, part // 16, 128), BF)]
        scratch += [v((n, 4, part // 16, 128), BF)]
    scratch += [dma((11,))] + [dma((4,))] * 8 + [dma((2, 2))] * 2 + [dma((2, KV))] * 2
    for n in (3, 3, 2, 2):
        scratch += [dma((5, n)), dma((5, n)), dma((2 * n,)), dma((2 * n,)), pltpu.SemaphoreType.REGULAR]
    out, in_grad, total = pl.pallas_call(
        step_kernel,
        out_shape=(
            jax.ShapeDtypeStruct((4, D, LOC), BF),
            jax.ShapeDtypeStruct((4, D, LOC), BF),
            pltpu.VMEM((TOTAL, 128), BF),
        ),
        in_specs=[hbm, hbm, smem, vmem, vmem] + [hbm] * 7,
        out_specs=(hbm, hbm, vmem),
        scratch_shapes=scratch,
        compiler_params=pltpu.CompilerParams(
            collective_id=0, has_side_effects=True, vmem_limit_bytes=55 * 2**20
        ),
        name="train_step",
    )(inputs, cot, docs, gain_a, gain_m, wq, wk, wv, wo, wg, wu, wd)
    return out, in_grad, total


def unpack_kernel(total, out, in_grad, out_c, in_grad_c, ga, gq, gk, gv, go, gm, gg, gu, gd, state, sa, sm, sq, sk, sv, so, sg, su, sd, in_sem, out_sem):
    loads = [pltpu.make_async_copy(a, state.at[k], in_sem.at[k]) for k, a in enumerate((out, in_grad))]
    for load in loads:
        load.start()
    stores = []

    def store(source, target):
        stores.append(pltpu.make_async_copy(source, target, out_sem.at[len(stores)]))
        stores[-1].start()

    def panels(base, height, width, target):
        for j in range((width + 127) // 128):
            lanes = min(128, width - j * 128)
            target[:, j * 128 : j * 128 + lanes] = total[pl.ds(base + j * height, height), :lanes].astype(F32)

    gains = total[pl.ds(B_Q2 + D, D), :].astype(F32).T
    for k, (source, target) in enumerate(((sa, ga), (sm, gm))):
        source[...] = gains[64 + k]
        store(source, target)
    for k in range(3):
        if k == 1:
            for j, target in enumerate((out_c, in_grad_c)):
                loads[j].wait()
                store(state.at[j], target)
        for base, source, target in ((B_WD, sd, gd), (B_WG, sg, gg), (B_WU, su, gu)):
            span = slice(k * 512, k * 512 + 512)
            panels(k * TILE + base, D, 512, source.at[:, span])
            store(source.at[:, span], target.at[:, span])
    panels(B_WO, D, D, so)
    store(so, go)
    panels(B_Q1, D, 384, sq.at[:, :384])
    panels(B_Q2, D, 192, sq.at[:, 384:])
    store(sq, gq)
    for g, base, height in ((0, B_K1, 256), (1, B_K1 + 128, 256), (2, B_K2, 128)):
        for k, target in enumerate((sk, sv)):
            for j in range(5):
                lanes = min(128, D - j * 128)
                rows = pl.ds(base + j * height + k * HEAD, HEAD)
                target[g * HEAD : g * HEAD + HEAD, j * 128 : j * 128 + lanes] = total[rows, :lanes].astype(F32)
    store(sk, gk)
    store(sv, gv)
    for copy in stores:
        copy.wait()


def unpack(total, out, in_grad):
    hbm = pl.BlockSpec(memory_space=pl.ANY)
    vmem = pl.BlockSpec(memory_space=pltpu.VMEM)
    shape = jax.ShapeDtypeStruct
    v = pltpu.VMEM
    result = pl.pallas_call(
        unpack_kernel,
        out_shape=(
            shape(out.shape, BF), shape(out.shape, BF),
            shape((D,), F32), shape((D, D), F32), shape((192, D), F32), shape((192, D), F32), shape((D, D), F32),
            shape((D,), F32), shape((D, FF), F32), shape((D, FF), F32), shape((D, FF), F32),
        ),
        in_specs=[vmem, hbm, hbm],
        out_specs=(hbm,) * 11,
        scratch_shapes=[
            v((2,) + out.shape, BF), v((D,), F32), v((D,), F32), v((D, D), F32), v((192, D), F32), v((192, D), F32), v((D, D), F32),
            v((D, FF), F32), v((D, FF), F32), v((D, FF), F32),
            pltpu.SemaphoreType.DMA((2,)), pltpu.SemaphoreType.DMA((17,)),
        ],
        compiler_params=pltpu.CompilerParams(vmem_limit_bytes=56 * 2**20),
        name="unpack",
    )(pltpu.with_memory_space_constraint(total, pltpu.VMEM), out, in_grad)
    return result


def on_device(inputs, docs, gain_a, wq, wk, wv, wo, gain_m, wg, wu, wd, cot):
    out, in_grad, total = train_step(
        inputs.transpose(0, 2, 1), docs, gain_a, wq, wk.T, wv.T, wo, gain_m, wg, wu, wd.T, cot.transpose(0, 2, 1)
    )
    out, in_grad, ga, gq, gk, gv, go, gm, gg, gu, gd = unpack(total, out, in_grad)
    return out.transpose(0, 2, 1), in_grad.transpose(0, 2, 1), ga, gq, gk.T, gv.T, go, gm, gg, gu, gd.T


def solution(mesh):
    token = P("rows", "seq", None)
    in_specs = (token, P("rows", None)) + (P(),) * 9 + (token,)
    out_specs = (token, token) + (P(),) * 9
    return jax.shard_map(on_device, mesh=mesh, in_specs=in_specs, out_specs=out_specs, check_vma=False)
```
